256 devices in a mesh: ctx: 128 (over y, x, z_lo, core), chan: 2 (over z_hi).
Axes of the slice: x: 4, y: 4, z: 8 (z_hi: 2, z_lo: 4; z = z_hi * 4 + z_lo), core: 2. Of those that a mesh axis runs over, the one named last changes fastest.
Arguments:
- streams: bfloat16 [32768, 3, 2048], P('ctx', None, 'chan'), may hold values from -6 to 6
- short_filter: float32 [3, 3, 2048], P(None, None, 'chan'), may hold values from -3 to 3
- residue: float32 [2048, 16], P('chan'), may hold values from -1.5 to 1.5
- decay_rate: float32 [2048, 16], P('chan'), may hold values from 1.5258789e-05 to 0.03, as said below
- skip_gain: float32 [2048], P('chan'), may hold values from 0.5 to 1.5
Outputs:
- hyena_out: bfloat16 [32768, 2048], P(('ctx', 'chan'))
The draws below stay inside these ranges and needn't reach their ends.
Inputs may be any that keep to these rules, and one draw needn't show every extreme that they name: `decay_rate`: each rate is drawn for its channel and mode independently; nothing beyond these bounds is promised.
All inputs are finite; a program needn't handle non-finite values.
Results may differ from the reference program's by a relative error of at most 0.0095.
Values may be sent and summed in bfloat16 or wider, within the bound.
No kernel may reach another device: no remote copies, remote signals or barrier semaphores. Data moves between devices by JAX's collectives and lax.ppermute only.
A program may use at most 128 MiB of HBM per device.

```python
import math
import jax
import jax.numpy as jnp
from jax import lax

CH = 2048
MODES = 16
TAPS = 3
TOKENS = 32768


def draw_decay_rate(key, part):
    key = jax.random.fold_in(key, 7)
    lowest = 0.5 / TOKENS
    highest = 0.03
    spread_key = jax.random.fold_in(key, 3)
    choose_key = jax.random.fold_in(key, 5)
    spread_val = jax.random.uniform(spread_key, (CH, MODES), jnp.float32)
    choose_val = jax.random.uniform(choose_key, (CH, MODES), jnp.float32)
    slow_rates = lowest * jnp.exp(spread_val * jnp.log(4.0))
    wide_rates = lowest * jnp.exp(spread_val * jnp.log(highest / lowest))
    rate_values = jnp.where(choose_val < 0.5, slow_rates, wide_rates)
    return jnp.clip(rate_values, lowest, highest)


def shard_levels(stream_key, extent, shards, least, top_value):
    def one(dim, parts):
        heights = jax.random.uniform(jax.random.fold_in(jax.random.fold_in(stream_key, 6), dim), (parts,), jnp.float32, least / len(shards), top_value / len(shards))
        return jnp.repeat(jnp.exp(heights), extent[dim] // parts).reshape((-1,) + (1,) * (len(extent) - dim - 1))

    loudness = one(*shards[0])
    for cut in shards[1:]:
        loudness = loudness * one(*cut)
    return loudness


def scatter_about(own_key, extent, deviation, reach, pieces=(), kind=jnp.bfloat16):
    level = shard_levels(own_key, extent, pieces, -0.22, 0.18) if pieces else 1.0
    values = jax.random.normal(own_key, extent, jnp.float32) * deviation * level
    return jnp.minimum(jnp.maximum(values, -reach), reach).astype(kind)


def setup_inputs(seed: int = 0) -> dict:
    arg_keys = jax.random.split(jax.random.key(seed), 6)
    return {
        "streams": scatter_about(arg_keys[0], (TOKENS, 3, CH), 1.0, 6.0, ((0, 128), (2, 2))),
        "short_filter": scatter_about(arg_keys[1], (TAPS, 3, CH), 0.6, 3.0, ((2, 2),), jnp.float32),
        "residue": scatter_about(arg_keys[2], (CH, MODES), MODES ** -0.5, 1.5, ((0, 2),), jnp.float32),
        "decay_rate": draw_decay_rate(jax.random.fold_in(arg_keys[5], 71), 0),
        "skip_gain": jnp.clip(0.5 + 1.0 * jax.random.uniform(arg_keys[4], (CH,), jnp.float32) ** shard_levels(arg_keys[4], (CH,), ((0, 2),), -0.2, 0.2), 0.5, 1.5),
    }


TWO_PI = 2.0 * math.pi

def spectrum(angles, parity, residue, decay_rate, seq_len):
    half_sine = jnp.sin(0.5 * angles)
    sine_angle = jnp.sin(angles)
    double_sq = 2.0 * half_sine * half_sine
    zero_field = jnp.zeros(angles.shape[:-1] + (residue.shape[0],), jnp.float32)

    def add_mode(mode_index, totals):
        rate_now = lax.dynamic_index_in_dim(decay_rate, mode_index, 1, keepdims=False)
        mode_weight = lax.dynamic_index_in_dim(residue, mode_index, 1, keepdims=False) * jnp.sqrt(2.0 * rate_now)
        keep_factor = jnp.exp(-rate_now)
        numerator = 1.0 - jnp.exp(-rate_now * seq_len) * parity
        den_real = -jnp.expm1(-rate_now) + keep_factor * double_sq
        den_imag = keep_factor * sine_angle
        common_factor = mode_weight * numerator / (den_real * den_real + den_imag * den_imag)
        return (totals[0] + common_factor * den_real, totals[1] - common_factor * den_imag)
    return lax.fori_loop(0, residue.shape[1], add_mode, (zero_field, zero_field))

def reference(streams, short_filter, residue, decay_rate, skip_gain):
    seq_len = streams.shape[0]
    total_len = 2 * seq_len
    widened = streams.astype(jnp.float32)
    padded = jnp.pad(widened, ((TAPS - 1, 0), (0, 0), (0, 0)))
    summed = jnp.zeros(streams.shape, jnp.float32)
    for tap_index in range(TAPS):
        offset = TAPS - 1 - tap_index
        summed = summed + short_filter[tap_index][None] * padded[offset:offset + seq_len]
    features = summed.astype(jnp.bfloat16)
    query_in = features[:, 0].astype(jnp.float32)
    gated_in = (features[:, 1].astype(jnp.float32) * features[:, 2].astype(jnp.float32)).astype(jnp.bfloat16)
    gated_wide = gated_in.astype(jnp.float32)
    block_width = math.gcd(CH, 64)
    block_count = CH // block_width
    gated_blocks = jnp.transpose(gated_wide.reshape(seq_len, block_count, block_width), (1, 0, 2))
    residue_blocks = residue.reshape(block_count, block_width, MODES)
    decay_blocks = decay_rate.reshape(block_count, block_width, MODES)
    frequency = jnp.arange(total_len, dtype=jnp.int32)
    angles = (frequency.astype(jnp.float32) * (TWO_PI / total_len))[:, None]
    parity = (1 - 2 * (frequency % 2)).astype(jnp.float32)[:, None]

    def one_block(inputs):
        signal, res_block, dec_block = inputs
        spec_real, spec_imag = spectrum(angles, parity, res_block, dec_block, seq_len)
        padded_signal = jnp.concatenate([signal, jnp.zeros_like(signal)], axis=0)
        transform = jnp.fft.fft(padded_signal, axis=0)
        product = transform * lax.complex(spec_real, spec_imag)
        return jnp.real(jnp.fft.ifft(product, axis=0))[:seq_len]
    filtered_blocks = lax.map(one_block, (gated_blocks, residue_blocks, decay_blocks))
    filtered = jnp.transpose(filtered_blocks, (1, 0, 2)).reshape(seq_len, CH)
    result = query_in * (filtered + skip_gain[None, :] * gated_wide)
    return result.astype(jnp.bfloat16)
```

```python
import functools

import jax
import jax.numpy as jnp
from jax import lax
from jax.experimental import pallas as pl
from jax.experimental.pallas import tpu as pltpu
from jax.sharding import PartitionSpec as P

LANES = 128
SUB = 8
F32 = jnp.float32
BF16 = jnp.bfloat16


def sub_index():
    return lax.broadcasted_iota(jnp.int32, (SUB, LANES), 0)


def rows_of(ref, cols):
    return [
        jnp.broadcast_to(ref[m : m + 1, cols], (SUB, LANES)) for m in range(ref.shape[0])
    ]


def features_kernel(
    chan_ref, x_ref, halo_ref, taps_ref, rate_ref,
    q_own, g_own, q_send, g_send, state_ref, half_ref, wide, gated,
):
    side = chan_ref[0]
    _, toks, width = x_ref.shape
    half = toks // 2
    tap_count = taps_ref.shape[0]
    rim = tap_count - 1
    step = 32
    for s in range(3):
        wide[s, SUB - rim : SUB, :] = halo_ref[s].astype(F32)
        for r in range(0, toks, step):
            wide[s, SUB + r : SUB + r + step, :] = x_ref[s, r : r + step, :].astype(F32)
    for c in range(0, width, LANES):
        cols = slice(c, c + LANES)
        taps = [
            [
                jnp.broadcast_to(taps_ref[j, s : s + 1, cols], (step, LANES))
                for j in range(tap_count)
            ]
            for s in range(3)
        ]
        for r in range(0, toks, step):
            feats = []
            for s in range(3):
                total = taps[s][0] * wide[s, SUB + r : SUB + r + step, cols]
                for j in range(1, tap_count):
                    total = total + taps[s][j] * wide[s, SUB + r - j : SUB + r - j + step, cols]
                feats.append(total.astype(BF16))
            gate = (feats[1].astype(F32) * feats[2].astype(F32)).astype(BF16)
            gated[r : r + step, :] = gate.astype(F32)
            at = r % half

            @pl.when(side == r // half)
            def _():
                q_own[at : at + step, cols] = feats[0]
                g_own[at : at + step, cols] = gate

            @pl.when(side != r // half)
            def _():
                q_send[at : at + step, cols] = feats[0]
                g_send[at : at + step, cols] = gate

        run = toks // SUB
        rates = rows_of(rate_ref, cols)
        keep = [jnp.exp(-rate) for rate in rates]

        def advance(j, states):
            now = gated[pl.ds(j, SUB, stride=run), :]
            return tuple(k * state + now for k, state in zip(keep, states))

        ends = lax.fori_loop(
            0, run, advance, tuple(jnp.zeros((SUB, LANES), F32) for _ in keep), unroll=4
        )
        index = sub_index()
        left = (SUB - 1 - index).astype(F32) * run
        in_half = index < SUB // 2
        left_half = jnp.maximum(SUB // 2 - 1 - index, 0).astype(F32) * run
        for m, (rate, end) in enumerate(zip(rates, ends)):
            state_ref[m : m + 1, cols] = jnp.sum(
                jnp.exp(-rate * left) * end, axis=0, keepdims=True
            )
            half_ref[m : m + 1, cols] = jnp.sum(
                jnp.where(in_half, jnp.exp(-rate * left_half) * end, 0.0), axis=0, keepdims=True
            )


def local_kernel(g_ref, res_ref, rate_ref, skip_ref, out_ref, gated):
    toks, width = g_ref.shape
    run = toks // SUB
    step = 32
    index = sub_index()
    for c in range(0, width, LANES):
        cols = slice(c, c + LANES)
        for r in range(0, toks, step):
            gated[r : r + step, :] = g_ref[r : r + step, cols].astype(F32)
        rates = rows_of(rate_ref, cols)
        keep = [jnp.exp(-rate) for rate in rates]

        def advance(j, states):
            now = gated[pl.ds(j, SUB, stride=run), :]
            return tuple(k * state + now for k, state in zip(keep, states))

        ends = lax.fori_loop(
            0, run, advance, tuple(jnp.zeros((SUB, LANES), F32) for _ in keep), unroll=4
        )
        begins = []
        for rate, total in zip(rates, ends):
            for shift in (1, 2, 4):
                total = total + jnp.where(
                    index >= shift,
                    jnp.exp(-rate * (shift * run)) * pltpu.roll(total, shift, 0),
                    0.0,
                )
            begins.append(jnp.where(index >= 1, pltpu.roll(total, 1, 0), 0.0))
        gains = [
            res * jnp.sqrt(2.0 * rate) for res, rate in zip(rows_of(res_ref, cols), rates)
        ]
        skip = jnp.broadcast_to(skip_ref[0:1, cols], (SUB, LANES))

        def emit(j, states):
            now = gated[pl.ds(j, SUB, stride=run), :]
            states = tuple(k * state + now for k, state in zip(keep, states))
            terms = [skip * now] + [gain * state for gain, state in zip(gains, states)]
            while len(terms) > 1:
                terms = [
                    terms[i] + terms[i + 1] if i + 1 < len(terms) else terms[i]
                    for i in range(0, len(terms), 2)
                ]
            out_ref[pl.ds(j + c * toks // LANES, SUB, stride=run), :] = terms[0]
            return states

        lax.fori_loop(0, run, emit, tuple(begins), unroll=4)


def finish_kernel(
    chan_ref, q_own, p_own, x_own, res_own, rate_own,
    q_far, p_far, x_far, res_far, rate_far, out_ref, carry,
):
    side = chan_ref[0]
    toks, width = q_own.shape
    run = toks // SUB
    index = sub_index()
    passed = (index * run + 1).astype(F32)
    step = 32
    for part, (q_ref, p_ref, x_ref, res_ref, rate_ref) in enumerate(
        ((q_own, p_own, x_own, res_own, rate_own), (q_far, p_far, x_far, res_far, rate_far))
    ):
        base = width * (side if part == 0 else 1 - side)
        for c in range(0, width, LANES):
            cols = slice(c, c + LANES)
            rates = rows_of(rate_ref, cols)
            keep = [jnp.exp(-rate) for rate in rates]
            begins = tuple(
                res * jnp.sqrt(2.0 * rate) * jnp.exp(-rate * passed) * x
                for res, rate, x in zip(rows_of(res_ref, cols), rates, rows_of(x_ref, cols))
            )

            def fade(j, states):
                terms = list(states)
                while len(terms) > 1:
                    terms = [terms[i] + terms[i + 1] for i in range(0, len(terms), 2)]
                carry[pl.ds(j, SUB, stride=run), :] = terms[0]
                return tuple(k * state for k, state in zip(keep, states))

            lax.fori_loop(0, run, fade, begins, unroll=4)
            where = pl.ds(pl.multiple_of(base + c, LANES), LANES)
            for r in range(0, toks, step):
                rows = slice(r, r + step)
                out_ref[rows, where] = (
                    q_ref[rows, cols].astype(F32) * (p_ref[c * toks // LANES + r : c * toks // LANES + r + step, :] + carry[rows, :])
                ).astype(BF16)


def stage(state_total, prefix, rate_span, index, stride, count, behind):
    ctx_count = lax.axis_size("ctx")
    place = index // stride % count
    sent = state_total.astype(BF16)
    arrived = []
    for k in range(1, count):
        route = []
        for i in range(ctx_count):
            j = i // stride % count
            route.append((i, i + ((j + k) % count - j) * stride))
        arrived.append(lax.ppermute(sent, "ctx", route))
    total = jnp.exp(-rate_span * ((count - 1 - place) * stride).astype(F32)) * state_total
    for k, got in enumerate(arrived, 1):
        got = got.astype(F32)
        origin = (place - k) % count
        total = total + jnp.exp(-rate_span * ((count - 1 - origin) * stride).astype(F32)) * got
        between = ((k - 1) * stride + behind).astype(F32)
        prefix = prefix + jnp.where(place >= k, jnp.exp(-rate_span * between), 0.0) * got
    return total, prefix


def shards(streams, short_filter, residue, decay_rate, skip_gain):
    ctx_count = lax.axis_size("ctx")
    index = lax.axis_index("ctx")
    side = lax.axis_index("chan")
    toks, _, width = streams.shape
    half = toks // 2
    modes = residue.shape[1]
    rim = short_filter.shape[0] - 1
    swap = [(0, 1), (1, 0)]

    x = jnp.transpose(streams, (1, 0, 2))
    rates = decay_rate.T
    weights = residue.T
    skip = skip_gain[None, :]
    halo = lax.ppermute(
        x[:, toks - rim :, :], "ctx", [(i, i + 1) for i in range(ctx_count - 1)]
    )
    params = lax.ppermute(jnp.concatenate([rates, weights, skip], axis=0), "chan", swap)
    rates_far, weights_far, skip_far = (
        params[:modes],
        params[modes : 2 * modes],
        params[2 * modes :],
    )
    chan_id = side.astype(jnp.int32).reshape(1)

    tile = 256 if width % 256 == 0 else LANES
    vmem = pltpu.CompilerParams(vmem_limit_bytes=48 * 1024 * 1024)
    rows = lambda n: pl.BlockSpec((n, tile), lambda i, *_: (0, i))
    q_own, g_own, q_send, g_send, state, state_half = pl.pallas_call(
        features_kernel,
        grid_spec=pltpu.PrefetchScalarGridSpec(
            num_scalar_prefetch=1,
            grid=(width // tile,),
            in_specs=[
                pl.BlockSpec((3, toks, tile), lambda i, *_: (0, 0, i)),
                pl.BlockSpec((3, rim, tile), lambda i, *_: (0, 0, i)),
                pl.BlockSpec((rim + 1, 3, tile), lambda i, *_: (0, 0, i)),
                rows(modes),
            ],
            out_specs=[rows(half)] * 4 + [rows(modes)] * 2,
            scratch_shapes=[
                pltpu.VMEM((3, toks + SUB, tile), F32),
                pltpu.VMEM((toks, LANES), F32),
            ],
        ),
        out_shape=[jax.ShapeDtypeStruct((half, width), BF16)] * 4
        + [jax.ShapeDtypeStruct((modes, width), F32)] * 2,
        compiler_params=vmem,
        name="features",
    )(chan_id, x, halo, short_filter, rates)

    g_far = lax.ppermute(g_send, "chan", swap)
    q_far = lax.ppermute(q_send, "chan", swap)

    def local(g, res, rate, skip_row, name):
        return pl.pallas_call(
            local_kernel,
            grid=(width // tile,),
            in_specs=[
                pl.BlockSpec((half, tile), lambda i: (0, i)),
                pl.BlockSpec((modes, tile), lambda i: (0, i)),
                pl.BlockSpec((modes, tile), lambda i: (0, i)),
                pl.BlockSpec((1, tile), lambda i: (0, i)),
            ],
            out_specs=pl.BlockSpec((half * tile // LANES, LANES), lambda i: (i, 0)),
            out_shape=jax.ShapeDtypeStruct((half * width // LANES, LANES), F32),
            scratch_shapes=[pltpu.VMEM((half, LANES), F32)],
            compiler_params=vmem,
            name=name,
        )(g, res, rate, skip_row)

    p_own = local(g_own, weights, rates, skip, "local_own")
    p_far = local(g_far, weights_far, rates_far, skip_far, "local_far")

    span = rates * float(toks)
    prefix = jnp.zeros_like(state)
    total = state
    stride = 1
    for count in scan_radices(ctx_count):
        total, prefix = stage(total, prefix, span, index, stride, count, index % stride)
        stride *= count

    later = jnp.exp(-rates * float(half)) * prefix + state_half
    mine = jnp.where(side == 0, prefix, later)
    theirs = jnp.where(side == 0, later, prefix)
    x_far = lax.ppermute(theirs.astype(BF16), "chan", swap).astype(F32)

    full = lambda a: pl.BlockSpec(a.shape, lambda *_: (0,) * a.ndim)
    operands = (
        q_own, p_own, mine, weights, rates, q_far, p_far, x_far, weights_far, rates_far,
    )
    return pl.pallas_call(
        finish_kernel,
        grid_spec=pltpu.PrefetchScalarGridSpec(
            num_scalar_prefetch=1,
            grid=(1,),
            in_specs=[full(a) for a in operands],
            out_specs=pl.BlockSpec((half, 2 * width), lambda *_: (0, 0)),
            scratch_shapes=[pltpu.VMEM((half, LANES), F32)],
        ),
        out_shape=jax.ShapeDtypeStruct((half, 2 * width), BF16),
        compiler_params=vmem,
        name="finish",
    )(chan_id, *operands)


def scan_radices(count):
    radices = [2] if count % 2 == 0 else []
    left = count // 2 if radices else count
    while left % 4 == 0:
        radices.append(4)
        left //= 4
    if left > 1:
        radices.append(left)
    return radices


def solution(mesh):
    return jax.shard_map(
        shards,
        mesh=mesh,
        in_specs=(
            P("ctx", None, "chan"),
            P(None, None, "chan"),
            P("chan", None),
            P("chan", None),
            P("chan"),
        ),
        out_specs=P(("ctx", "chan"), None),
        check_vma=False,
    )
```

```python
import jax
import jax.numpy as jnp
from jax import lax
from jax.experimental import pallas as pl
from jax.experimental.pallas import tpu as pltpu
from jax.sharding import PartitionSpec as P

LANES = 128
SUB = 8
STEP = 32
F32 = jnp.float32
BF16 = jnp.bfloat16
VMEM_LIMIT = 16 * 1024 * 1024


def spread(ref, m, cols):
    return jnp.broadcast_to(ref[m : m + 1, cols], (SUB, LANES))


def tree_sum(terms):
    terms = list(terms)
    while len(terms) > 1:
        terms = [
            terms[i] + terms[i + 1] if i + 1 < len(terms) else terms[i]
            for i in range(0, len(terms), 2)
        ]
    return terms[0]


def short_conv(wide, taps, row, count, cols):
    total = taps[0] * wide[SUB + row : SUB + row + count, cols]
    for j in range(1, len(taps)):
        total = total + taps[j] * wide[SUB + row - j : SUB + row - j + count, cols]
    return total.astype(BF16)


def tap_rows(taps_ref, s, cols, count):
    return [
        jnp.broadcast_to(taps_ref[j, s : s + 1, cols], (count, LANES))
        for j in range(taps_ref.shape[0])
    ]


def state_kernel(
    x_hbm, halo_ref, taps_ref, rate_ref,
    gate_ref, ends_ref, state_ref, half_ref,
    raw, wide, gated, keep_ref, run_ref, sems,
):
    step_id = pl.program_id(0)
    steps = pl.num_programs(0)
    _, toks, width = wide.shape[0], wide.shape[1] - SUB, wide.shape[2]
    half = toks // 2
    rim = taps_ref.shape[0] - 1
    modes = rate_ref.shape[0]
    run = half // SUB

    def fetch(i):
        return pltpu.make_async_copy(
            x_hbm.at[pl.ds(1, 2), :, pl.ds(pl.multiple_of(i * width, LANES), width)],
            raw.at[i],
            sems.at[i],
        )

    @pl.when(step_id == 0)
    def _():
        for i in range(raw.shape[0]):
            fetch(i).start()

    keep_ref[...] = jnp.exp(-rate_ref[...])
    run_ref[...] = jnp.exp(-rate_ref[...] * run)
    fetch(step_id).wait()
    for s in range(2):
        wide[s, SUB - rim : SUB, :] = halo_ref[s + 1].astype(F32)
        for r in range(0, toks, STEP):
            wide[s, SUB + r : SUB + r + STEP, :] = raw[step_id, s, r : r + STEP, :].astype(F32)
    index = lax.broadcasted_iota(jnp.int32, (SUB, LANES), 0)
    for t, c in enumerate(range(0, width, LANES)):
        cols = slice(c, c + LANES)
        key_taps = tap_rows(taps_ref, 1, cols, STEP)
        value_taps = tap_rows(taps_ref, 2, cols, STEP)
        for r in range(0, toks, STEP):
            key = short_conv(wide.at[0], key_taps, r, STEP, cols)
            value = short_conv(wide.at[1], value_taps, r, STEP, cols)
            gate = (key.astype(F32) * value.astype(F32)).astype(BF16)
            gate_ref[r // half, r % half : r % half + STEP, cols] = gate
            gated[r : r + STEP, :] = gate.astype(F32)
        keep = [spread(keep_ref, m, cols) for m in range(modes)]
        run_keep = run_ref[:, cols]
        run_keep2 = run_keep * run_keep
        run_keep4 = run_keep2 * run_keep2
        half_rows = []
        for part in range(2):

            def advance(j, states, part=part):
                now = gated[pl.ds(j + part * half, SUB, stride=run), :]
                return tuple(k * state + now for k, state in zip(keep, states))

            ends = lax.fori_loop(
                1,
                run,
                advance,
                tuple(gated[pl.ds(part * half, SUB, stride=run), :] for _ in keep),
                unroll=5,
            )
            rows = []
            for m, end in enumerate(ends):
                ends_ref[part, t, m] = end
                for shift, factor in ((1, run_keep), (2, run_keep2), (4, run_keep4)):
                    end = end + jnp.broadcast_to(
                        factor[m : m + 1], (SUB, LANES)
                    ) * pltpu.roll(end, shift, 0)
                rows.append(end[SUB - 1 : SUB])
            half_rows.append(rows)
        run_keep8 = run_keep4 * run_keep4
        for m in range(modes):
            first, second = half_rows[0][m], half_rows[1][m]
            half_ref[m : m + 1, cols] = first
            state_ref[m : m + 1, cols] = run_keep8[m : m + 1] * first + second


def local_kernel(
    half_id, x_hbm, halo_ref, taps_ref, gate_ref, ends_ref, res_ref, rate_ref, skip_ref,
    out_ref, raw, wide, gated, shown, keep_ref, gain_ref, run_ref, sems,
):
    step_id = pl.program_id(0)
    part = half_id[0]
    half, width = gate_ref.shape
    rim = taps_ref.shape[0] - 1
    modes = rate_ref.shape[0]
    run = half // SUB

    def fetch(i):
        return pltpu.make_async_copy(
            x_hbm.at[0, :, pl.ds(pl.multiple_of(i * width, LANES), width)],
            raw.at[i],
            sems.at[i],
        )

    @pl.when(step_id == 0)
    def _():
        for i in range(raw.shape[0]):
            fetch(i).start()

    rates = rate_ref[...]
    keep_ref[...] = jnp.exp(-rates)
    run_ref[...] = jnp.exp(-rates * run)
    gain_ref[...] = res_ref[...] * jnp.sqrt(2.0 * rates)
    high = rates.astype(BF16)
    out_ref[2 * half : 2 * half + modes, :] = high
    out_ref[2 * half + modes : 2 * half + 2 * modes, :] = (rates - high.astype(F32)).astype(BF16)

    index = lax.broadcasted_iota(jnp.int32, (SUB, LANES), 0)
    for t, c in enumerate(range(0, width, LANES)):
        cols = slice(c, c + LANES)
        for r in range(0, half, STEP):
            gated[r : r + STEP, :] = gate_ref[r : r + STEP, cols].astype(F32)
        keep = [spread(keep_ref, m, cols) for m in range(modes)]
        gains = [spread(gain_ref, m, cols) for m in range(modes)]
        skip = spread(skip_ref, 0, cols)
        run_keep = run_ref[:, cols]
        run_keep2 = run_keep * run_keep
        run_keep4 = run_keep2 * run_keep2
        begins = []
        for m in range(modes):
            total = ends_ref[t, m]
            for shift, factor in ((1, run_keep), (2, run_keep2), (4, run_keep4)):
                total = total + jnp.where(
                    index >= shift,
                    jnp.broadcast_to(factor[m : m + 1], (SUB, LANES))
                    * pltpu.roll(total, shift, 0),
                    0.0,
                )
            begins.append(jnp.where(index >= 1, pltpu.roll(total, 1, 0), 0.0))

        def emit(j, states):
            now = gated[pl.ds(j, SUB, stride=run), :]
            states = tuple(k * state + now for k, state in zip(keep, states))
            shown[pl.ds(j, SUB, stride=run), :] = tree_sum(
                [skip * now] + [gain * state for gain, state in zip(gains, states)]
            )
            return states

        lax.fori_loop(0, run, emit, tuple(begins), unroll=4)
        for r in range(0, half, STEP):
            out_ref[half + r : half + r + STEP, cols] = shown[r : r + STEP, :].astype(BF16)

    fetch(step_id).wait()
    start = pl.multiple_of(part * half, half)
    for r in range(0, half, STEP):
        wide[SUB + r : SUB + r + STEP, :] = raw[
            step_id, pl.ds(pl.multiple_of(start + r, STEP), STEP), :
        ].astype(F32)
    before = raw[step_id, half - 16 : half, :].astype(F32)[16 - rim :]
    wide[SUB - rim : SUB, :] = jnp.where(part == 0, halo_ref[0].astype(F32), before)
    for c in range(0, width, LANES):
        cols = slice(c, c + LANES)
        taps = tap_rows(taps_ref, 0, cols, STEP)
        for r in range(0, half, STEP):
            out_ref[r : r + STEP, cols] = short_conv(wide, taps, r, STEP, cols)


def finish_kernel(
    chan_ref, own_ref, begin_own, far_ref, begin_far, out_ref, carry, keep_ref, run_ref
):
    side = chan_ref[0]
    modes, width = begin_own.shape
    half = out_ref.shape[0]
    run = half // SUB
    index = lax.broadcasted_iota(jnp.int32, (SUB, LANES), 0)
    for part, (pq_ref, begin_ref) in enumerate(((own_ref, begin_own), (far_ref, begin_far))):
        base = width * (side if part == 0 else 1 - side)
        rates = pq_ref[2 * half : 2 * half + modes, :].astype(F32) + pq_ref[
            2 * half + modes : 2 * half + 2 * modes, :
        ].astype(F32)
        keep_ref[...] = jnp.exp(-rates)
        run_ref[...] = jnp.exp(-rates * run)

        def tile(t, _, base=base, pq_ref=pq_ref, begin_ref=begin_ref):
            c = pl.multiple_of(t * LANES, LANES)
            cols = pl.ds(c, LANES)
            keep = [spread(keep_ref, m, cols) for m in range(modes)]
            run_keep = run_ref[:, cols]
            begin = begin_ref[:, cols].astype(F32) * keep_ref[:, cols]
            states = []
            powers = []
            for shift in (1, 2, 4):
                powers.append((index & shift, run_keep))
                run_keep = run_keep * run_keep
            for m in range(modes):
                state = jnp.broadcast_to(begin[m : m + 1], (SUB, LANES))
                for bit, factor in powers:
                    state = state * jnp.where(
                        bit != 0, jnp.broadcast_to(factor[m : m + 1], (SUB, LANES)), 1.0
                    )
                states.append(state)

            def fade(j, states):
                carry[pl.ds(j, SUB, stride=run), :] = tree_sum(states)
                return tuple(k * state for k, state in zip(keep, states))

            lax.fori_loop(0, run, fade, tuple(states), unroll=4)
            where = pl.ds(pl.multiple_of(base + c, LANES), LANES)
            for r in range(0, half, STEP):
                rows = slice(r, r + STEP)
                late = slice(half + r, half + r + STEP)
                out_ref[rows, where] = (
                    pq_ref[rows, cols].astype(F32)
                    * (pq_ref[late, cols].astype(F32) + carry[rows, :])
                ).astype(BF16)
            return 0

        lax.fori_loop(0, width // LANES, tile, 0)


def stage(run_state, prefix, span, index, stride, count, behind, last):
    ctx_count = lax.axis_size("ctx")
    place = index // stride % count
    sent = run_state.astype(BF16)
    arrived = []
    for k in range(1, count):
        route = []
        for i in range(ctx_count):
            j = i // stride % count
            if not last or j + k < count:
                route.append((i, i + ((j + k) % count - j) * stride))
        arrived.append(lax.ppermute(sent, "ctx", route))
    total = jnp.exp(-span * ((count - 1 - place) * stride).astype(F32)) * run_state
    for k, got in enumerate(arrived, 1):
        got = got.astype(F32)
        origin = (place - k) % count
        total = total + jnp.exp(-span * ((count - 1 - origin) * stride).astype(F32)) * got
        between = ((k - 1) * stride + behind).astype(F32)
        prefix = prefix + jnp.where(place >= k, jnp.exp(-span * between), 0.0) * got
    return total, prefix


def scan_counts(blocks):
    counts = [2] if blocks % 2 == 0 else []
    left = blocks // 2 if counts else blocks
    while left % 4 == 0:
        counts.append(4)
        left //= 4
    if left > 1:
        counts.append(left)
    return counts


def cheap(nbytes):
    return pl.CostEstimate(flops=1000, bytes_accessed=nbytes, transcendentals=0)


def shards(streams, short_filter, residue, decay_rate, skip_gain):
    ctx_count = lax.axis_size("ctx")
    index = lax.axis_index("ctx")
    side = lax.axis_index("chan")
    toks, _, width = streams.shape
    half = toks // 2
    modes = residue.shape[1]
    rim = short_filter.shape[0] - 1
    swap = [(0, 1), (1, 0)]
    tile = 256 if width % 256 == 0 else LANES
    steps = width // tile
    tiles = tile // LANES

    x = jnp.transpose(streams, (1, 0, 2))
    rates = decay_rate.T
    weights = residue.T
    skip = skip_gain[None, :]
    halo = lax.ppermute(
        x[:, toks - rim :, :], "ctx", [(i, i + 1) for i in range(ctx_count - 1)]
    )
    chan_id = side.astype(jnp.int32).reshape(1)

    x_kept, taps_kept, rates_kept = (
        pltpu.with_memory_space_constraint(a, pltpu.HBM) for a in (x, short_filter, rates)
    )
    params = pltpu.CompilerParams(vmem_limit_bytes=VMEM_LIMIT)
    in_hbm = pl.BlockSpec(memory_space=pltpu.HBM)
    strip = lambda *lead: pl.BlockSpec(lead + (tile,), lambda i, *_: (0,) * len(lead) + (i,))
    gate, ends, state, state_half = pl.pallas_call(
        state_kernel,
        grid=(steps,),
        in_specs=[in_hbm, strip(3, rim), strip(rim + 1, 3), strip(modes)],
        out_specs=[
            strip(2, half),
            pl.BlockSpec((2, tiles, modes, SUB, LANES), lambda i: (0, i, 0, 0, 0)),
            strip(modes),
            strip(modes),
        ],
        out_shape=[
            jax.ShapeDtypeStruct((2, half, width), BF16),
            jax.ShapeDtypeStruct((2, width // LANES, modes, SUB, LANES), F32),
            jax.ShapeDtypeStruct((modes, width), F32),
            jax.ShapeDtypeStruct((modes, width), F32),
        ],
        scratch_shapes=[
            pltpu.VMEM((steps, 2, toks, tile), BF16),
            pltpu.VMEM((2, toks + SUB, tile), F32),
            pltpu.VMEM((toks, LANES), F32),
            pltpu.VMEM((modes, tile), F32),
            pltpu.VMEM((modes, tile), F32),
            pltpu.SemaphoreType.DMA((steps,)),
        ],
        compiler_params=params,
        cost_estimate=cheap(1000),
        name="states",
    )(x_kept, halo, taps_kept, rates_kept)

    def local(which, name):
        return pl.pallas_call(
            local_kernel,
            grid_spec=pltpu.PrefetchScalarGridSpec(
                num_scalar_prefetch=1,
                grid=(steps,),
                in_specs=[
                    in_hbm,
                    strip(3, rim),
                    strip(rim + 1, 3),
                    pl.BlockSpec((None, half, tile), lambda i, w: (w[0], 0, i)),
                    pl.BlockSpec(
                        (None, tiles, modes, SUB, LANES), lambda i, w: (w[0], i, 0, 0, 0)
                    ),
                    strip(modes),
                    strip(modes),
                    strip(1),
                ],
                out_specs=strip(2 * half + 2 * modes),
                scratch_shapes=[
                    pltpu.VMEM((steps, toks, tile), BF16),
                    pltpu.VMEM((half + SUB, tile), F32),
                    pltpu.VMEM((half, LANES), F32),
                    pltpu.VMEM((half, LANES), F32),
                    pltpu.VMEM((modes, tile), F32),
                    pltpu.VMEM((modes, tile), F32),
                    pltpu.VMEM((modes, tile), F32),
                    pltpu.SemaphoreType.DMA((steps,)),
                ],
            ),
            out_shape=jax.ShapeDtypeStruct((2 * half + 2 * modes, width), BF16),
            compiler_params=params,
            cost_estimate=cheap(1000),
            name=name,
        )(which, x_kept, halo, short_filter, gate, ends, weights, rates, skip)

    sent = local(1 - chan_id, "local_sent")
    own = local(chan_id, "local_own")

    span = rates * float(toks)
    prefix = jnp.zeros_like(state)
    run_state = state
    stride = 1
    counts = scan_counts(ctx_count)
    for level, count in enumerate(counts):
        if level == 1:
            run_state, sent = lax.optimization_barrier((run_state, sent))
        last = level == len(counts) - 1
        run_state, prefix = stage(
            run_state, prefix, span, index, stride, count, index % stride, last
        )
        stride *= count

    far = lax.ppermute(sent, "chan", swap)
    gains = weights * jnp.sqrt(2.0 * rates)
    first = gains * prefix
    second = gains * (jnp.exp(-rates * float(half)) * prefix + state_half)
    mine = jnp.where(side == 0, first, second)
    theirs = jnp.where(side == 0, second, first).astype(BF16)
    begin_far = lax.ppermute(theirs, "chan", swap)

    full = lambda a: pl.BlockSpec(a.shape, lambda *_: (0,) * a.ndim)
    operands = (own, mine, far, begin_far)
    return pl.pallas_call(
        finish_kernel,
        grid_spec=pltpu.PrefetchScalarGridSpec(
            num_scalar_prefetch=1,
            grid=(1,),
            in_specs=[full(a) for a in operands],
            out_specs=pl.BlockSpec((half, 2 * width), lambda *_: (0, 0)),
            scratch_shapes=[
                pltpu.VMEM((half, LANES), F32),
                pltpu.VMEM((modes, width), F32),
                pltpu.VMEM((modes, width), F32),
            ],
        ),
        out_shape=jax.ShapeDtypeStruct((half, 2 * width), BF16),
        compiler_params=params,
        cost_estimate=cheap(1000),
        name="finish",
    )(chan_id, *operands)


def solution(mesh):
    return jax.shard_map(
        shards,
        mesh=mesh,
        in_specs=(
            P("ctx", None, "chan"),
            P(None, None, "chan"),
            P("chan", None),
            P("chan", None),
            P("chan"),
        ),
        out_specs=P(("ctx", "chan"), None),
        check_vma=False,
    )
```

```python
import jax
import jax.numpy as jnp
from jax import lax
from jax.experimental import pallas as pl
from jax.experimental.pallas import tpu as pltpu
from jax.sharding import PartitionSpec as P

LANES = 128
SUB = 8
STEP = 32
PAIR = 16
F32 = jnp.float32
BF16 = jnp.bfloat16
VMEM_LIMIT = 16 * 1024 * 1024


def spread(ref, m, cols):
    return jnp.broadcast_to(ref[m : m + 1, cols], (SUB, LANES))


def tree_sum(terms):
    terms = list(terms)
    while len(terms) > 1:
        terms = [
            terms[i] + terms[i + 1] if i + 1 < len(terms) else terms[i]
            for i in range(0, len(terms), 2)
        ]
    return terms[0]


def short_conv(load, taps, j):
    total = taps[0] * load(j)
    for k in range(1, len(taps)):
        total = total + taps[k] * load(j - k)
    return total


def tap_rows(taps_ref, s, cols):
    return [
        jnp.broadcast_to(taps_ref[j, s : s + 1, cols], (SUB, LANES))
        for j in range(taps_ref.shape[0])
    ]


def modes_at(ref, i, modes):
    return jnp.concatenate(
        [ref[pl.ds(i + SUB * m, SUB, stride=SUB), :] for m in range(0, modes, SUB)], axis=0
    )


def put_modes_at(ref, i, value):
    for m in range(0, value.shape[0], SUB):
        ref[pl.ds(i + SUB * m, SUB, stride=SUB), :] = value[m : m + SUB]


def state_kernel(
    x_hbm, taps_ref, rate_ref,
    gate_ref, ends_ref, state_ref, sum_ref,
    raw, raw_query, wide, keep_ref, run_ref, sems,
):
    step_id = pl.program_id(0)
    _, _, toks, width = raw.shape
    half = toks // 2
    rim = taps_ref.shape[0] - 1
    modes = rate_ref.shape[0]
    run = half // SUB

    def fetches(i):
        cols = pl.ds(pl.multiple_of(i * width, LANES), width)
        return (
            pltpu.make_async_copy(x_hbm.at[pl.ds(1, 2), :, cols], raw.at[i], sems.at[0, i]),
            pltpu.make_async_copy(
                x_hbm.at[0, pl.ds(0, PAIR), cols], raw_query.at[i, 0], sems.at[1, i]
            ),
            pltpu.make_async_copy(
                x_hbm.at[0, pl.ds(toks - PAIR, PAIR), cols], raw_query.at[i, 1], sems.at[2, i]
            ),
        )

    @pl.when(step_id == 0)
    def _():
        for i in range(raw.shape[0]):
            for copy in fetches(i):
                copy.start()

    keep_ref[...] = jnp.exp(-rate_ref[...])
    run_ref[...] = jnp.exp(-rate_ref[...] * run)
    for copy in fetches(step_id):
        copy.wait()
    index = lax.broadcasted_iota(jnp.int32, (SUB, LANES), 0)
    for t, c in enumerate(range(0, width, LANES)):
        cols = slice(c, c + LANES)
        for s in range(2):
            wide[s, :SUB, :] = jnp.zeros((SUB, LANES), F32)
            for r in range(0, toks, STEP):
                wide[s, SUB + r : SUB + r + STEP, :] = raw[
                    step_id, s, r : r + STEP, cols
                ].astype(F32)
        key_taps = tap_rows(taps_ref, 1, cols)
        value_taps = tap_rows(taps_ref, 2, cols)
        keep = [spread(keep_ref, m, cols) for m in range(modes)]
        total = None
        for part in range(2):
            base = part * half
            states = None
            for j in range(run):
                load = lambda s, at: wide[s, pl.ds(SUB + base + at, SUB, stride=run), :]
                key = short_conv(lambda at: load(0, at), key_taps, j)
                value = short_conv(lambda at: load(1, at), value_taps, j)
                gate = key * value
                if part == 0 and j < rim:
                    gate = jnp.where(index == 0, 0.0, gate)
                gate_ref[pl.ds(t * toks + base + j, SUB, stride=run), :] = gate
                if states is None:
                    states = [gate] * modes
                else:
                    states = [k * state + gate for k, state in zip(keep, states)]
            for m, end in enumerate(states):
                ends_ref[t, part, m * SUB : (m + 1) * SUB, :] = end
            run_keep = run_ref[:, cols]
            for i in range(SUB):
                end = modes_at(ends_ref.at[t, part], i, modes)
                total = end if total is None else run_keep * total + end
        state_ref[:, cols] = total
        sum_ref[:modes, cols] = total.astype(BF16)
        query = raw_query[step_id, :, :, cols].astype(F32)
        sum_ref[modes:, cols] = jnp.concatenate(
            [
                wide[0, SUB : SUB + rim, :],
                wide[1, SUB : SUB + rim, :],
                query[1, PAIR - rim :],
                wide[0, SUB + toks - rim : SUB + toks, :],
                wide[1, SUB + toks - rim : SUB + toks, :],
                query[0, :rim],
                jnp.zeros((PAIR - 6 * rim, LANES), F32),
            ],
            axis=0,
        ).astype(BF16)


def first_gates(past, first, taps):
    rows = []
    for s in range(2):
        before, here = past[s], first[s]
        line = [before[0:1], before[1:2], here[0:1], here[1:2]]
        rows.append(
            [
                taps[s][0] * line[at] + taps[s][1] * line[at - 1] + taps[s][2] * line[at - 2]
                for at in (2, 3)
            ]
        )
    return [key * value for key, value in zip(*rows)]


def join_kernel(ids, stride, count, toks, last, *refs):
    taps_ref, rate_ref, state_ref, prefix_ref, past_ref, own_ref = refs[:6]
    near = (own_ref,) + refs[6 : 5 + count]
    outs = refs[5 + count :]
    prefix_out, past_out = outs[:2]
    modes, width = rate_ref.shape
    index = ids[0]
    place = lax.rem(lax.div(index, stride), count)
    behind = lax.rem(index, stride)
    origins = [lax.rem(place - k + count, count) for k in range(count)]
    as_float = lambda n: n.astype(F32)

    def tile(t, _):
        cols = pl.ds(pl.multiple_of(t * LANES, LANES), LANES)
        rates = rate_ref[:, cols]
        span = rates * float(toks)
        taps = [[taps_ref[j, s : s + 1, cols] for j in range(3)] for s in (1, 2)]
        extra = [ref[modes:, cols].astype(F32) for ref in near]
        firsts = [(e[0:2], e[2:4]) for e in extra]
        states = [state_ref[:, cols]] + [ref[:modes, cols].astype(F32) for ref in near[1:]]
        first_keep = jnp.exp(-rates * float(toks - 1))
        second_keep = jnp.exp(-rates * float(toks - 2))
        rest = jnp.exp(-span * float(stride - 1))
        joins = []
        for k in range(count):
            linked = origins[k] >= 1
            past = extra[(k + 1) % count][4:10]
            past = jnp.where(linked, past, 0.0)
            one, two = first_gates((past[2:4], past[4:6]), firsts[k], taps)
            join = first_keep * one + second_keep * two
            if not last:
                join = jnp.where(linked, join, 0.0)
            joins.append(join)
            states[k] = states[k] + rest * join
        prefix = prefix_ref[:, cols] + jnp.where(
            behind >= 1,
            jnp.exp(-span * as_float(jnp.maximum(behind - 1, 0))) * joins[0],
            0.0,
        )
        for k in range(1, count):
            gap = as_float((k - 1) * stride + behind)
            prefix = prefix + jnp.where(place >= k, jnp.exp(-span * gap) * states[k], 0.0)
        prefix_out[:, cols] = prefix
        past = jnp.where((place >= 1) & (behind == 0), extra[1][4:10], past_ref[0:6, cols])
        past_out[:, cols] = jnp.concatenate([past, jnp.zeros((SUB - 6, LANES), F32)], axis=0)
        if not last:
            state_out, sum_out = outs[2:]
            total = None
            for k in range(count):
                gap = as_float((count - 1 - origins[k]) * stride)
                term = jnp.exp(-span * gap) * states[k]
                total = term if total is None else total + term
            state_out[:, cols] = total
            first = extra[0]
            end = extra[0]
            for k in range(1, count):
                first = jnp.where(origins[k] == 0, extra[k], first)
                end = jnp.where(origins[k] == count - 1, extra[k], end)
            sum_out[:modes, cols] = total.astype(BF16)
            sum_out[modes:, cols] = jnp.concatenate([first[0:4], end[4:]], axis=0).astype(BF16)
        return 0

    lax.fori_loop(0, width // LANES, tile, 0)


def local_kernel(
    part_id, x_hbm, taps_ref, gate_ref, ends_ref, res_ref, rate_ref, skip_ref,
    query_ref, local_ref, raw, wide, begins, keep_ref, gain_ref, run_ref, sems,
):
    step_id = pl.program_id(0)
    part = part_id[0]
    _, toks, width = raw.shape
    half = toks // 2
    rim = taps_ref.shape[0] - 1
    modes = rate_ref.shape[0]
    run = half // SUB

    def fetch(i):
        return pltpu.make_async_copy(
            x_hbm.at[0, :, pl.ds(pl.multiple_of(i * width, LANES), width)],
            raw.at[i],
            sems.at[i],
        )

    @pl.when(step_id == 0)
    def _():
        for i in range(raw.shape[0]):
            fetch(i).start()

    rates = rate_ref[...]
    keep_ref[...] = jnp.exp(-rates)
    run_ref[...] = jnp.exp(-rates * run)
    gain_ref[...] = res_ref[...] * jnp.sqrt(2.0 * rates)
    for t, c in enumerate(range(0, width, LANES)):
        cols = slice(c, c + LANES)
        run_keep = run_ref[:, cols]
        state = jnp.zeros((modes, LANES), F32)
        for i in range(SUB):
            state = run_keep * state + modes_at(ends_ref.at[t, 0], i, modes)
        state = jnp.where(part == 0, 0.0, state)
        for i in range(SUB):
            put_modes_at(begins, i, state)
            if i + 1 < SUB:
                state = run_keep * state + modes_at(ends_ref.at[t, part], i, modes)
        keep = [spread(keep_ref, m, cols) for m in range(modes)]
        gains = [spread(gain_ref, m, cols) for m in range(modes)]
        skip = spread(skip_ref, 0, cols)
        states = [begins[m * SUB : (m + 1) * SUB, :] for m in range(modes)]
        for j in range(run):
            now = gate_ref[pl.ds(t * toks + part * half + j, SUB, stride=run), :]
            states = [k * state + now for k, state in zip(keep, states)]
            local_ref[pl.ds(t * half + j, SUB, stride=run), :] = tree_sum(
                [skip * now] + [gain * state for gain, state in zip(gains, states)]
            )

    fetch(step_id).wait()
    start = pl.multiple_of(part * half, half)
    for t, c in enumerate(range(0, width, LANES)):
        cols = slice(c, c + LANES)
        for r in range(0, half, STEP):
            wide[SUB + r : SUB + r + STEP, :] = raw[
                step_id, pl.ds(pl.multiple_of(start + r, STEP), STEP), cols
            ].astype(F32)
        before = raw[step_id, half - 16 : half, cols].astype(F32)[16 - rim :]
        wide[SUB - rim : SUB, :] = before
        taps = tap_rows(taps_ref, 0, cols)
        for j in range(run):
            query_ref[pl.ds(t * half + j, SUB, stride=run), :] = short_conv(
                lambda at: wide[pl.ds(SUB + at, SUB, stride=run), :], taps, j
            )


def finish_kernel(
    ids, query_ref, local_ref, prefix_ref, past_ref, sum_ref, taps_ref, res_ref, rate_ref, skip_ref,
    out_ref, begins, carry,
):
    part = ids[0]
    modes, width = prefix_ref.shape
    half = out_ref.shape[0]
    run = half // SUB
    row = lax.broadcasted_iota(jnp.int32, (STEP, LANES), 0)
    for t, c in enumerate(range(0, width, LANES)):
        cols = slice(c, c + LANES)
        rates = rate_ref[:, cols]
        gains = res_ref[:, cols] * jnp.sqrt(2.0 * rates)
        keep_all = jnp.exp(-rates)
        run_keep = jnp.exp(-rates * run)
        past = past_ref[:, cols]
        here = sum_ref[modes:, cols].astype(F32)
        taps = [[taps_ref[j, s : s + 1, cols] for j in range(3)] for s in range(3)]
        one, two = first_gates((past[2:4], past[4:6]), (here[0:2], here[2:4]), taps[1:])
        line = [past[0:1], past[1:2], here[10:11], here[11:12]]
        queries = [
            taps[0][0] * line[at] + taps[0][1] * line[at - 1] + taps[0][2] * line[at - 2]
            for at in (2, 3)
        ]
        grow = jnp.exp(rates)
        state = gains * (prefix_ref[:, cols] + grow * (one + grow * two))
        state = state * jnp.where(part == 0, keep_all, jnp.exp(-rates * (half + 1)))
        for i in range(SUB):
            put_modes_at(begins, i, state)
            state = run_keep * state
        keep = [jnp.broadcast_to(keep_all[m : m + 1], (SUB, LANES)) for m in range(modes)]
        states = [begins[m * SUB : (m + 1) * SUB, :] for m in range(modes)]
        for j in range(run):
            carry[pl.ds(j, SUB, stride=run), :] = tree_sum(states)
            states = [k * state for k, state in zip(keep, states)]
        skip = skip_ref[:, cols]
        over = jnp.sum(gains * grow, axis=0, keepdims=True)
        for r in range(0, half, STEP):
            rows = slice(t * half + r, t * half + r + STEP)
            value = query_ref[rows, :] * (local_ref[rows, :] + carry[r : r + STEP, :])
            if r == 0:
                begin = carry[0:SUB, :]
                head = queries[0] * (begin[0:1] - over * two + skip * one)
                second = queries[1] * (begin[1:2] + skip * two)
                value = jnp.where((row == 0) & (part == 0), head, value)
                value = jnp.where((row == 1) & (part == 0), second, value)
            out_ref[r : r + STEP, cols] = value.astype(BF16)


def place_kernel(ids, far_ref, held_ref, out_ref, sem):
    del held_ref
    width = far_ref.shape[1]
    copy = pltpu.make_async_copy(
        far_ref,
        out_ref.at[:, pl.ds(pl.multiple_of(ids[0] * width, LANES), width)],
        sem,
    )
    copy.start()
    copy.wait()


def scan_counts(blocks):
    counts = [2] if blocks % 2 == 0 else []
    left = blocks // 2 if counts else blocks
    while left % 4 == 0:
        counts.append(4)
        left //= 4
    if left > 1:
        counts.append(left)
    return counts


def shards(streams, short_filter, residue, decay_rate, skip_gain):
    ctx_count = lax.axis_size("ctx")
    index = lax.axis_index("ctx")
    side = lax.axis_index("chan").astype(jnp.int32).reshape(1)
    toks, _, width = streams.shape
    half = toks // 2
    modes = residue.shape[1]
    rim = short_filter.shape[0] - 1
    tile = 256 if width % 256 == 0 else LANES
    steps = width // tile
    tiles = tile // LANES
    all_tiles = width // LANES

    x = jnp.transpose(streams, (1, 0, 2))
    rates = decay_rate.T
    weights = residue.T
    skip = skip_gain[None, :]
    x_kept, taps_kept, rates_kept = (
        pltpu.with_memory_space_constraint(a, pltpu.HBM) for a in (x, short_filter, rates)
    )
    params = pltpu.CompilerParams(vmem_limit_bytes=VMEM_LIMIT)
    in_hbm = pl.BlockSpec(memory_space=pltpu.HBM)
    strip = lambda *lead: pl.BlockSpec(lead + (tile,), lambda i, *_: (0,) * len(lead) + (i,))
    tall = lambda rows: pl.BlockSpec((tiles * rows, LANES), lambda i, *_: (i, 0))
    ends_spec = pl.BlockSpec((tiles, 2, modes * SUB, LANES), lambda i, *_: (i, 0, 0, 0))
    gate, ends, state, summary = pl.pallas_call(
        state_kernel,
        grid=(steps,),
        in_specs=[in_hbm, strip(rim + 1, 3), strip(modes)],
        out_specs=[tall(toks), ends_spec, strip(modes), strip(modes + PAIR)],
        out_shape=[
            jax.ShapeDtypeStruct((all_tiles * toks, LANES), F32),
            jax.ShapeDtypeStruct((all_tiles, 2, modes * SUB, LANES), F32),
            jax.ShapeDtypeStruct((modes, width), F32),
            jax.ShapeDtypeStruct((modes + PAIR, width), BF16),
        ],
        scratch_shapes=[
            pltpu.VMEM((steps, 2, toks, tile), BF16),
            pltpu.VMEM((steps, 2, PAIR, tile), BF16),
            pltpu.VMEM((2, toks + SUB, LANES), F32),
            pltpu.VMEM((modes, tile), F32),
            pltpu.VMEM((modes, tile), F32),
            pltpu.SemaphoreType.DMA((3, steps)),
        ],
        compiler_params=params,
        name="states",
    )(x_kept, taps_kept, rates_kept)

    def local(which, name):
        return pl.pallas_call(
            local_kernel,
            grid_spec=pltpu.PrefetchScalarGridSpec(
                num_scalar_prefetch=1,
                grid=(steps,),
                in_specs=[
                    in_hbm,
                    strip(rim + 1, 3),
                    tall(toks),
                    ends_spec,
                    strip(modes),
                    strip(modes),
                    strip(1),
                ],
                out_specs=[tall(half), tall(half)],
                scratch_shapes=[
                    pltpu.VMEM((steps, toks, tile), BF16),
                    pltpu.VMEM((half + SUB, LANES), F32),
                    pltpu.VMEM((modes * SUB, LANES), F32),
                    pltpu.VMEM((modes, tile), F32),
                    pltpu.VMEM((modes, tile), F32),
                    pltpu.VMEM((modes, tile), F32),
                    pltpu.SemaphoreType.DMA((steps,)),
                ],
            ),
            out_shape=[jax.ShapeDtypeStruct((all_tiles * half, LANES), F32)] * 2,
            compiler_params=params,
            name=name,
        )(which, x_kept, short_filter, gate, ends, weights, rates, skip)

    locals_sent = local(1 - side, "local_sent")
    locals_own = local(side, "local_own")

    ids = index.astype(jnp.int32).reshape(1)
    in_vmem = pl.BlockSpec(memory_space=pltpu.VMEM)
    prefix = jnp.zeros((modes, width), F32)
    past = jnp.zeros((SUB, width), F32)
    own = summary
    stride = 1
    counts = scan_counts(ctx_count)
    for level, count in enumerate(counts):
        last = level == len(counts) - 1
        if level == 2:
            summary, locals_sent = lax.optimization_barrier((summary, locals_sent))
        if level == 3:
            summary, locals_own = lax.optimization_barrier((summary, locals_own))
        arrived = []
        for k in range(1, count):
            route = []
            for i in range(ctx_count):
                j = i // stride % count
                route.append((i, i + ((j + k) % count - j) * stride))
            arrived.append(lax.ppermute(summary, "ctx", route))
        shapes = [
            jax.ShapeDtypeStruct((modes, width), F32),
            jax.ShapeDtypeStruct((SUB, width), F32),
        ]
        if not last:
            shapes += [
                jax.ShapeDtypeStruct((modes, width), F32),
                jax.ShapeDtypeStruct((modes + PAIR, width), BF16),
            ]

        def body(ids, *refs, stride=stride, count=count, last=last):
            join_kernel(ids, stride, count, toks, last, *refs)

        results = pl.pallas_call(
            body,
            in_specs=[pl.BlockSpec(memory_space=pltpu.SMEM)] + [in_vmem] * (5 + count),
            out_specs=[in_vmem] * len(shapes),
            out_shape=shapes,
            compiler_params=params,
            name=f"join_{level}",
        )(ids, short_filter, rates, state, prefix, past, summary, *arrived)
        prefix, past = results[:2]
        if not last:
            state, summary = results[2:]
        stride *= count

    def finish(which, column, columns, locals_, prefix, name):
        return pl.pallas_call(
            finish_kernel,
            grid_spec=pltpu.PrefetchScalarGridSpec(
                num_scalar_prefetch=1,
                grid=(steps,),
                in_specs=[
                    tall(half),
                    tall(half),
                    strip(modes),
                    strip(SUB),
                    strip(modes + PAIR),
                    strip(rim + 1, 3),
                    strip(modes),
                    strip(modes),
                    strip(1),
                ],
                out_specs=pl.BlockSpec((half, tile), lambda i, ids: (0, ids[1] * steps + i)),
                scratch_shapes=[
                    pltpu.VMEM((modes * SUB, LANES), F32),
                    pltpu.VMEM((half, LANES), F32),
                ],
            ),
            out_shape=jax.ShapeDtypeStruct((half, columns), BF16),
            compiler_params=params,
            name=name,
        )(
            jnp.concatenate([which, column]),
            *locals_,
            prefix,
            past,
            own,
            short_filter,
            weights,
            rates,
            skip,
        )

    sent = finish(1 - side, jnp.zeros_like(side), width, locals_sent, prefix, "finish_sent")
    far = lax.ppermute(sent, "chan", [(0, 1), (1, 0)])
    prefix, sent = lax.optimization_barrier((prefix, sent))
    held = finish(side, side, 2 * width, locals_own, prefix, "finish_own")
    return pl.pallas_call(
        place_kernel,
        grid_spec=pltpu.PrefetchScalarGridSpec(
            num_scalar_prefetch=1,
            grid=(1,),
            in_specs=[pl.BlockSpec(memory_space=pl.ANY)] * 2,
            out_specs=pl.BlockSpec(memory_space=pl.ANY),
            scratch_shapes=[pltpu.SemaphoreType.DMA(())],
        ),
        out_shape=jax.ShapeDtypeStruct((half, 2 * width), BF16),
        input_output_aliases={2: 0},
        compiler_params=params,
        name="place",
    )(1 - side, far, held)


def solution(mesh):
    return jax.shard_map(
        shards,
        mesh=mesh,
        in_specs=(
            P("ctx", None, "chan"),
            P(None, None, "chan"),
            P("chan", None),
            P("chan", None),
            P("chan"),
        ),
        out_specs=P(("ctx", "chan"), None),
        check_vma=False,
    )
```

```python
import jax
import jax.numpy as jnp
from jax import lax
from jax.experimental import pallas as pl
from jax.experimental.pallas import tpu as pltpu
from jax.sharding import PartitionSpec as P

LANES = 128
SUB = 8
STEP = 32
PAIR = 16
F32 = jnp.float32
BF16 = jnp.bfloat16
VMEM_LIMIT = 16 * 1024 * 1024


def spread(ref, m, cols):
    return jnp.broadcast_to(ref[m : m + 1, cols], (SUB, LANES))


def tree_sum(terms):
    terms = list(terms)
    while len(terms) > 1:
        terms = [
            terms[i] + terms[i + 1] if i + 1 < len(terms) else terms[i]
            for i in range(0, len(terms), 2)
        ]
    return terms[0]


def short_conv(load, taps, j):
    total = taps[0] * load(j)
    for k in range(1, len(taps)):
        total = total + taps[k] * load(j - k)
    return total


def tap_rows(taps_ref, s, cols):
    return [
        jnp.broadcast_to(taps_ref[j, s : s + 1, cols], (SUB, LANES))
        for j in range(taps_ref.shape[0])
    ]


def modes_at(ref, i, modes):
    return jnp.concatenate(
        [ref[pl.ds(i + SUB * m, SUB, stride=SUB), :] for m in range(0, modes, SUB)], axis=0
    )


def put_modes_at(ref, i, value):
    for m in range(0, value.shape[0], SUB):
        ref[pl.ds(i + SUB * m, SUB, stride=SUB), :] = value[m : m + SUB]


def state_kernel(
    x_hbm, taps_ref, rate_ref,
    gate_ref, ends_ref, state_ref, sum_ref,
    raw, raw_query, wide, keep_ref, run_ref, sems,
):
    step_id = pl.program_id(0)
    _, _, toks, width = raw.shape
    half = toks // 2
    rim = taps_ref.shape[0] - 1
    modes = rate_ref.shape[0]
    run = half // SUB

    def fetches(i):
        cols = pl.ds(pl.multiple_of(i * width, LANES), width)
        return (
            pltpu.make_async_copy(x_hbm.at[pl.ds(1, 2), :, cols], raw.at[i], sems.at[0, i]),
            pltpu.make_async_copy(
                x_hbm.at[0, pl.ds(0, PAIR), cols], raw_query.at[i, 0], sems.at[1, i]
            ),
            pltpu.make_async_copy(
                x_hbm.at[0, pl.ds(toks - PAIR, PAIR), cols], raw_query.at[i, 1], sems.at[2, i]
            ),
        )

    @pl.when(step_id == 0)
    def _():
        for i in range(raw.shape[0]):
            for copy in fetches(i):
                copy.start()

    keep_ref[...] = jnp.exp(-rate_ref[...])
    run_ref[...] = jnp.exp(-rate_ref[...] * run)
    for copy in fetches(step_id):
        copy.wait()
    index = lax.broadcasted_iota(jnp.int32, (SUB, LANES), 0)
    for t, c in enumerate(range(0, width, LANES)):
        cols = slice(c, c + LANES)
        for s in range(2):
            wide[s, :SUB, :] = jnp.zeros((SUB, LANES), F32)
            for r in range(0, toks, STEP):
                wide[s, SUB + r : SUB + r + STEP, :] = raw[
                    step_id, s, r : r + STEP, cols
                ].astype(F32)
        key_taps = tap_rows(taps_ref, 1, cols)
        value_taps = tap_rows(taps_ref, 2, cols)
        keep = [spread(keep_ref, m, cols) for m in range(modes)]
        total = None
        for part in range(2):
            base = part * half
            states = None
            for j in range(run):
                load = lambda s, at: wide[s, pl.ds(SUB + base + at, SUB, stride=run), :]
                key = short_conv(lambda at: load(0, at), key_taps, j)
                value = short_conv(lambda at: load(1, at), value_taps, j)
                gate = key * value
                if part == 0 and j < rim:
                    gate = jnp.where(index == 0, 0.0, gate)
                gate_ref[pl.ds(t * toks + base + j, SUB, stride=run), :] = gate
                if states is None:
                    states = [gate] * modes
                else:
                    states = [k * state + gate for k, state in zip(keep, states)]
            for m, end in enumerate(states):
                ends_ref[t, part, m * SUB : (m + 1) * SUB, :] = end
            run_keep = run_ref[:, cols]
            for i in range(SUB):
                end = modes_at(ends_ref.at[t, part], i, modes)
                total = end if total is None else run_keep * total + end
        state_ref[:, cols] = total
        sum_ref[:modes, cols] = total.astype(BF16)
        query = raw_query[step_id, :, :, cols].astype(F32)
        sum_ref[modes:, cols] = jnp.concatenate(
            [
                wide[0, SUB : SUB + rim, :],
                wide[1, SUB : SUB + rim, :],
                query[1, PAIR - rim :],
                wide[0, SUB + toks - rim : SUB + toks, :],
                wide[1, SUB + toks - rim : SUB + toks, :],
                query[0, :rim],
                jnp.zeros((PAIR - 6 * rim, LANES), F32),
            ],
            axis=0,
        ).astype(BF16)


def first_gates(past, first, taps):
    rows = []
    for s in range(2):
        before, here = past[s], first[s]
        line = [before[0:1], before[1:2], here[0:1], here[1:2]]
        rows.append(
            [
                taps[s][0] * line[at] + taps[s][1] * line[at - 1] + taps[s][2] * line[at - 2]
                for at in (2, 3)
            ]
        )
    return [key * value for key, value in zip(*rows)]


def join_kernel(ids, stride, count, toks, last, *refs):
    taps_ref, rate_ref, state_ref, prefix_ref, past_ref, own_ref = refs[:6]
    near = (own_ref,) + refs[6 : 5 + count]
    shared = count == 4 and stride % 2 == 0
    outs = refs[5 + count :]
    prefix_out, past_out = outs[:2]
    modes, width = rate_ref.shape
    index = ids[0]
    place = lax.rem(lax.div(index, stride), count)
    behind = lax.rem(index, stride)
    origins = [lax.rem(place - k + count, count) for k in range(count)]
    as_float = lambda n: n.astype(F32)

    def tile(t, _):
        cols = pl.ds(pl.multiple_of(t * LANES, LANES), LANES)
        rates = rate_ref[:, cols]
        span = rates * float(toks)
        taps = [[taps_ref[j, s : s + 1, cols] for j in range(3)] for s in (1, 2)]
        full = [ref[:, cols].astype(F32) for ref in near]
        if shared:
            odd = lax.rem(index, 2) == 1
            full[1], full[3] = jnp.where(odd, full[3], full[1]), jnp.where(odd, full[1], full[3])
        extra = [value[modes:] for value in full]
        firsts = [(e[0:2], e[2:4]) for e in extra]
        states = [state_ref[:, cols]] + [value[:modes] for value in full[1:]]
        first_keep = jnp.exp(-rates * float(toks - 1))
        second_keep = jnp.exp(-rates * float(toks - 2))
        rest = jnp.exp(-span * float(stride - 1))
        joins = []
        for k in range(count):
            linked = origins[k] >= 1
            past = extra[(k + 1) % count][4:10]
            past = jnp.where(linked, past, 0.0)
            one, two = first_gates((past[2:4], past[4:6]), firsts[k], taps)
            join = first_keep * one + second_keep * two
            if not last:
                join = jnp.where(linked, join, 0.0)
            joins.append(join)
            states[k] = states[k] + rest * join
        prefix = prefix_ref[:, cols] + jnp.where(
            behind >= 1,
            jnp.exp(-span * as_float(jnp.maximum(behind - 1, 0))) * joins[0],
            0.0,
        )
        for k in range(1, count):
            gap = as_float((k - 1) * stride + behind)
            prefix = prefix + jnp.where(place >= k, jnp.exp(-span * gap) * states[k], 0.0)
        prefix_out[:, cols] = prefix
        past = jnp.where((place >= 1) & (behind == 0), extra[1][4:10], past_ref[0:6, cols])
        past_out[:, cols] = jnp.concatenate([past, jnp.zeros((SUB - 6, LANES), F32)], axis=0)
        if not last:
            state_out, sum_out = outs[2:]
            total = None
            for k in range(count):
                gap = as_float((count - 1 - origins[k]) * stride)
                term = jnp.exp(-span * gap) * states[k]
                total = term if total is None else total + term
            state_out[:, cols] = total
            first = extra[0]
            end = extra[0]
            for k in range(1, count):
                first = jnp.where(origins[k] == 0, extra[k], first)
                end = jnp.where(origins[k] == count - 1, extra[k], end)
            sum_out[:modes, cols] = total.astype(BF16)
            sum_out[modes:, cols] = jnp.concatenate([first[0:4], end[4:]], axis=0).astype(BF16)
        return 0

    lax.fori_loop(0, width // LANES, tile, 0)


def local_kernel(
    part_id, x_hbm, taps_ref, gate_ref, ends_ref, res_ref, rate_ref, skip_ref,
    query_ref, local_ref, raw, wide, begins, keep_ref, gain_ref, run_ref, sems,
):
    step_id = pl.program_id(0)
    part = part_id[0]
    _, toks, width = raw.shape
    half = toks // 2
    rim = taps_ref.shape[0] - 1
    modes = rate_ref.shape[0]
    run = half // SUB

    def fetch(i):
        return pltpu.make_async_copy(
            x_hbm.at[0, :, pl.ds(pl.multiple_of(i * width, LANES), width)],
            raw.at[i],
            sems.at[i],
        )

    @pl.when(step_id == 0)
    def _():
        for i in range(raw.shape[0]):
            fetch(i).start()

    rates = rate_ref[...]
    keep_ref[...] = jnp.exp(-rates)
    run_ref[...] = jnp.exp(-rates * run)
    gain_ref[...] = res_ref[...] * jnp.sqrt(2.0 * rates)
    for t, c in enumerate(range(0, width, LANES)):
        cols = slice(c, c + LANES)
        run_keep = run_ref[:, cols]
        state = jnp.zeros((modes, LANES), F32)
        for i in range(SUB):
            state = run_keep * state + modes_at(ends_ref.at[t, 0], i, modes)
        state = jnp.where(part == 0, 0.0, state)
        for i in range(SUB):
            put_modes_at(begins, i, state)
            if i + 1 < SUB:
                state = run_keep * state + modes_at(ends_ref.at[t, part], i, modes)
        keep = [spread(keep_ref, m, cols) for m in range(modes)]
        gains = [spread(gain_ref, m, cols) for m in range(modes)]
        skip = spread(skip_ref, 0, cols)
        states = [begins[m * SUB : (m + 1) * SUB, :] for m in range(modes)]
        for j in range(run):
            now = gate_ref[pl.ds(t * toks + part * half + j, SUB, stride=run), :]
            states = [k * state + now for k, state in zip(keep, states)]
            local_ref[pl.ds(t * half + j, SUB, stride=run), :] = tree_sum(
                [skip * now] + [gain * state for gain, state in zip(gains, states)]
            )

    fetch(step_id).wait()
    start = pl.multiple_of(part * half, half)
    for t, c in enumerate(range(0, width, LANES)):
        cols = slice(c, c + LANES)
        for r in range(0, half, STEP):
            wide[SUB + r : SUB + r + STEP, :] = raw[
                step_id, pl.ds(pl.multiple_of(start + r, STEP), STEP), cols
            ].astype(F32)
        before = raw[step_id, half - 16 : half, cols].astype(F32)[16 - rim :]
        wide[SUB - rim : SUB, :] = before
        taps = tap_rows(taps_ref, 0, cols)
        for j in range(run):
            query_ref[pl.ds(t * half + j, SUB, stride=run), :] = short_conv(
                lambda at: wide[pl.ds(SUB + at, SUB, stride=run), :], taps, j
            )


def finish_kernel(
    ids, query_ref, local_ref, prefix_ref, past_ref, sum_ref, taps_ref, res_ref, rate_ref, skip_ref,
    out_ref, begins, carry,
):
    part = ids[0]
    modes, width = prefix_ref.shape
    half = out_ref.shape[0]
    run = half // SUB
    row = lax.broadcasted_iota(jnp.int32, (STEP, LANES), 0)
    for t, c in enumerate(range(0, width, LANES)):
        cols = slice(c, c + LANES)
        rates = rate_ref[:, cols]
        gains = res_ref[:, cols] * jnp.sqrt(2.0 * rates)
        keep_all = jnp.exp(-rates)
        run_keep = jnp.exp(-rates * run)
        past = past_ref[:, cols]
        here = sum_ref[modes:, cols].astype(F32)
        taps = [[taps_ref[j, s : s + 1, cols] for j in range(3)] for s in range(3)]
        one, two = first_gates((past[2:4], past[4:6]), (here[0:2], here[2:4]), taps[1:])
        line = [past[0:1], past[1:2], here[10:11], here[11:12]]
        queries = [
            taps[0][0] * line[at] + taps[0][1] * line[at - 1] + taps[0][2] * line[at - 2]
            for at in (2, 3)
        ]
        grow = jnp.exp(rates)
        state = gains * (prefix_ref[:, cols] + grow * (one + grow * two))
        state = state * jnp.where(part == 0, keep_all, jnp.exp(-rates * (half + 1)))
        for i in range(SUB):
            put_modes_at(begins, i, state)
            state = run_keep * state
        keep = [jnp.broadcast_to(keep_all[m : m + 1], (SUB, LANES)) for m in range(modes)]
        states = [begins[m * SUB : (m + 1) * SUB, :] for m in range(modes)]
        for j in range(run):
            carry[pl.ds(j, SUB, stride=run), :] = tree_sum(states)
            states = [k * state for k, state in zip(keep, states)]
        skip = skip_ref[:, cols]
        over = jnp.sum(gains * grow, axis=0, keepdims=True)
        for r in range(0, half, STEP):
            rows = slice(t * half + r, t * half + r + STEP)
            value = query_ref[rows, :] * (local_ref[rows, :] + carry[r : r + STEP, :])
            if r == 0:
                begin = carry[0:SUB, :]
                head = queries[0] * (begin[0:1] - over * two + skip * one)
                second = queries[1] * (begin[1:2] + skip * two)
                value = jnp.where((row == 0) & (part == 0), head, value)
                value = jnp.where((row == 1) & (part == 0), second, value)
            out_ref[r : r + STEP, cols] = value.astype(BF16)


def place_kernel(ids, far_ref, held_ref, out_ref, sem):
    del held_ref
    width = far_ref.shape[1]
    copy = pltpu.make_async_copy(
        far_ref,
        out_ref.at[:, pl.ds(pl.multiple_of(ids[0] * width, LANES), width)],
        sem,
    )
    copy.start()
    copy.wait()


def exchange(summary, blocks, index, stride, count):
    def route(hop):
        pairs = []
        for i in range(blocks):
            j = i // stride % count
            pairs.append((i, i + ((j + hop(i)) % count - j) * stride))
        return pairs

    def send(value, hop):
        return lax.ppermute(value, "ctx", route(hop))

    if count != 4 or stride % 2:
        return [send(summary, lambda i, k=k: k) for k in range(1, count)]
    beside = send(summary, lambda i: 3 if i % 2 else 1)
    across = send(summary, lambda i: 2)
    other = lax.ppermute(beside, "ctx", [(i, i ^ 1) for i in range(blocks)])
    return [beside, across, other]


def scan_counts(blocks):
    counts = [2] if blocks % 2 == 0 else []
    left = blocks // 2 if counts else blocks
    while left % 4 == 0:
        counts.append(4)
        left //= 4
    if left > 1:
        counts.append(left)
    return counts


def shards(streams, short_filter, residue, decay_rate, skip_gain):
    ctx_count = lax.axis_size("ctx")
    index = lax.axis_index("ctx")
    side = lax.axis_index("chan").astype(jnp.int32).reshape(1)
    toks, _, width = streams.shape
    half = toks // 2
    modes = residue.shape[1]
    rim = short_filter.shape[0] - 1
    tile = 256 if width % 256 == 0 else LANES
    steps = width // tile
    tiles = tile // LANES
    all_tiles = width // LANES

    x = jnp.transpose(streams, (1, 0, 2))
    rates = decay_rate.T
    weights = residue.T
    skip = skip_gain[None, :]
    x_kept, taps_kept, rates_kept = (
        pltpu.with_memory_space_constraint(a, pltpu.HBM) for a in (x, short_filter, rates)
    )
    params = pltpu.CompilerParams(vmem_limit_bytes=VMEM_LIMIT)
    in_hbm = pl.BlockSpec(memory_space=pltpu.HBM)
    strip = lambda *lead: pl.BlockSpec(lead + (tile,), lambda i, *_: (0,) * len(lead) + (i,))
    tall = lambda rows: pl.BlockSpec((tiles * rows, LANES), lambda i, *_: (i, 0))
    ends_spec = pl.BlockSpec((tiles, 2, modes * SUB, LANES), lambda i, *_: (i, 0, 0, 0))
    gate, ends, state, summary = pl.pallas_call(
        state_kernel,
        grid=(steps,),
        in_specs=[in_hbm, strip(rim + 1, 3), strip(modes)],
        out_specs=[tall(toks), ends_spec, strip(modes), strip(modes + PAIR)],
        out_shape=[
            jax.ShapeDtypeStruct((all_tiles * toks, LANES), F32),
            jax.ShapeDtypeStruct((all_tiles, 2, modes * SUB, LANES), F32),
            jax.ShapeDtypeStruct((modes, width), F32),
            jax.ShapeDtypeStruct((modes + PAIR, width), BF16),
        ],
        scratch_shapes=[
            pltpu.VMEM((steps, 2, toks, tile), BF16),
            pltpu.VMEM((steps, 2, PAIR, tile), BF16),
            pltpu.VMEM((2, toks + SUB, LANES), F32),
            pltpu.VMEM((modes, tile), F32),
            pltpu.VMEM((modes, tile), F32),
            pltpu.SemaphoreType.DMA((3, steps)),
        ],
        compiler_params=params,
        name="states",
    )(x_kept, taps_kept, rates_kept)

    def local(which, gate, name):
        return pl.pallas_call(
            local_kernel,
            grid_spec=pltpu.PrefetchScalarGridSpec(
                num_scalar_prefetch=1,
                grid=(steps,),
                in_specs=[
                    in_hbm,
                    strip(rim + 1, 3),
                    tall(toks),
                    ends_spec,
                    strip(modes),
                    strip(modes),
                    strip(1),
                ],
                out_specs=[tall(half), tall(half)],
                scratch_shapes=[
                    pltpu.VMEM((steps, toks, tile), BF16),
                    pltpu.VMEM((half + SUB, LANES), F32),
                    pltpu.VMEM((modes * SUB, LANES), F32),
                    pltpu.VMEM((modes, tile), F32),
                    pltpu.VMEM((modes, tile), F32),
                    pltpu.VMEM((modes, tile), F32),
                    pltpu.SemaphoreType.DMA((steps,)),
                ],
            ),
            out_shape=[jax.ShapeDtypeStruct((all_tiles * half, LANES), F32)] * 2,
            compiler_params=params,
            name=name,
        )(which, x_kept, short_filter, gate, ends, weights, rates, skip)

    locals_sent = local(1 - side, gate, "local_sent")

    ids = index.astype(jnp.int32).reshape(1)
    in_vmem = pl.BlockSpec(memory_space=pltpu.VMEM)
    prefix = jnp.zeros((modes, width), F32)
    past = jnp.zeros((SUB, width), F32)
    own = summary
    stride = 1
    counts = scan_counts(ctx_count)
    for level, count in enumerate(counts):
        last = level == len(counts) - 1
        if level == 2:
            summary, locals_sent = lax.optimization_barrier((summary, locals_sent))
        arrived = exchange(summary, ctx_count, index, stride, count)
        shapes = [
            jax.ShapeDtypeStruct((modes, width), F32),
            jax.ShapeDtypeStruct((SUB, width), F32),
        ]
        if not last:
            shapes += [
                jax.ShapeDtypeStruct((modes, width), F32),
                jax.ShapeDtypeStruct((modes + PAIR, width), BF16),
            ]

        def body(ids, *refs, stride=stride, count=count, last=last):
            join_kernel(ids, stride, count, toks, last, *refs)

        results = pl.pallas_call(
            body,
            in_specs=[pl.BlockSpec(memory_space=pltpu.SMEM)] + [in_vmem] * (5 + count),
            out_specs=[in_vmem] * len(shapes),
            out_shape=shapes,
            compiler_params=params,
            name=f"join_{level}",
        )(ids, short_filter, rates, state, prefix, past, summary, *arrived)
        prefix, past = results[:2]
        if not last:
            state, summary = results[2:]
        stride *= count

    def finish(which, column, columns, locals_, prefix, name):
        return pl.pallas_call(
            finish_kernel,
            grid_spec=pltpu.PrefetchScalarGridSpec(
                num_scalar_prefetch=1,
                grid=(steps,),
                in_specs=[
                    tall(half),
                    tall(half),
                    strip(modes),
                    strip(SUB),
                    strip(modes + PAIR),
                    strip(rim + 1, 3),
                    strip(modes),
                    strip(modes),
                    strip(1),
                ],
                out_specs=pl.BlockSpec((half, tile), lambda i, ids: (0, ids[1] * steps + i)),
                scratch_shapes=[
                    pltpu.VMEM((modes * SUB, LANES), F32),
                    pltpu.VMEM((half, LANES), F32),
                ],
            ),
            out_shape=jax.ShapeDtypeStruct((half, columns), BF16),
            compiler_params=params,
            name=name,
        )(
            jnp.concatenate([which, column]),
            *locals_,
            prefix,
            past,
            own,
            short_filter,
            weights,
            rates,
            skip,
        )

    sent = finish(1 - side, jnp.zeros_like(side), width, locals_sent, prefix, "finish_sent")
    far = lax.ppermute(sent, "chan", [(0, 1), (1, 0)])
    prefix, gate, sent = lax.optimization_barrier((prefix, gate, sent))
    locals_own = local(side, gate, "local_own")
    held = finish(side, side, 2 * width, locals_own, prefix, "finish_own")
    return pl.pallas_call(
        place_kernel,
        grid_spec=pltpu.PrefetchScalarGridSpec(
            num_scalar_prefetch=1,
            grid=(1,),
            in_specs=[pl.BlockSpec(memory_space=pl.ANY)] * 2,
            out_specs=pl.BlockSpec(memory_space=pl.ANY),
            scratch_shapes=[pltpu.SemaphoreType.DMA(())],
        ),
        out_shape=jax.ShapeDtypeStruct((half, 2 * width), BF16),
        input_output_aliases={2: 0},
        compiler_params=params,
        name="place",
    )(1 - side, far, held)


def solution(mesh):
    return jax.shard_map(
        shards,
        mesh=mesh,
        in_specs=(
            P("ctx", None, "chan"),
            P(None, None, "chan"),
            P("chan", None),
            P("chan", None),
            P("chan"),
        ),
        out_specs=P(("ctx", "chan"), None),
        check_vma=False,
    )
```

```python
import functools

import jax
import jax.numpy as jnp
from jax import lax
from jax.experimental import pallas as pl
from jax.experimental.pallas import tpu as pltpu
from jax.sharding import PartitionSpec as P

LANES = 128
SUB = 8
STEP = 32
PAIR = 16
F32 = jnp.float32
BF16 = jnp.bfloat16
VMEM_LIMIT = 16 * 1024 * 1024


def spread(ref, m, cols):
    return jnp.broadcast_to(ref[m : m + 1, cols], (SUB, LANES))


def tree_sum(terms):
    terms = list(terms)
    while len(terms) > 1:
        terms = [
            terms[i] + terms[i + 1] if i + 1 < len(terms) else terms[i]
            for i in range(0, len(terms), 2)
        ]
    return terms[0]


def short_conv(line, taps):
    total = taps[0] * line[-1]
    for k in range(1, len(taps)):
        total = total + taps[k] * line[-1 - k]
    return total


def tap_rows(taps_ref, s, cols):
    return [
        jnp.broadcast_to(taps_ref[j, s : s + 1, cols], (SUB, LANES))
        for j in range(taps_ref.shape[0])
    ]


def modes_at(ref, i, modes):
    return jnp.concatenate(
        [ref[pl.ds(i + SUB * m, SUB, stride=SUB), :] for m in range(0, modes, SUB)], axis=0
    )


def put_modes_at(ref, i, value):
    for m in range(0, value.shape[0], SUB):
        ref[pl.ds(i + SUB * m, SUB, stride=SUB), :] = value[m : m + SUB]


def state_kernel(
    x_hbm, taps_hbm, rate_hbm,
    gate_ref, ends_ref, state_ref, sum_ref,
    raw, raw_query, wide, keep_ref, run_ref, taps_all, rate_all, sems, small_sems,
):
    step_id = pl.program_id(0)
    _, _, toks, width = raw.shape
    half = toks // 2
    rim = taps_all.shape[0] - 1
    modes = rate_all.shape[0]
    run = half // SUB

    def fetches(i):
        cols = pl.ds(pl.multiple_of(i * width, LANES), width)
        return (
            pltpu.make_async_copy(x_hbm.at[pl.ds(1, 2), :, cols], raw.at[i], sems.at[0, i]),
            pltpu.make_async_copy(
                x_hbm.at[0, pl.ds(0, PAIR), cols], raw_query.at[i, 0], sems.at[1, i]
            ),
            pltpu.make_async_copy(
                x_hbm.at[0, pl.ds(toks - PAIR, PAIR), cols], raw_query.at[i, 1], sems.at[2, i]
            ),
        )

    small = (
        pltpu.make_async_copy(taps_hbm, taps_all, small_sems.at[0]),
        pltpu.make_async_copy(rate_hbm, rate_all, small_sems.at[1]),
    )

    @pl.when(step_id == 0)
    def _():
        for copy in small:
            copy.start()
        for i in range(raw.shape[0]):
            for copy in fetches(i):
                copy.start()
        for copy in small:
            copy.wait()

    strip = pl.ds(pl.multiple_of(step_id * width, LANES), width)
    taps_ref = taps_all.at[:, :, strip]
    rates = rate_all[:, strip]
    keep_ref[...] = jnp.exp(-rates)
    run_ref[...] = jnp.exp(-rates * run)
    for copy in fetches(step_id):
        copy.wait()
    index = lax.broadcasted_iota(jnp.int32, (SUB, LANES), 0)
    for t, c in enumerate(range(0, width, LANES)):
        cols = slice(c, c + LANES)
        for s in range(2):
            wide[s, :SUB, :] = jnp.zeros((SUB, LANES), F32)
            for r in range(0, toks, STEP):
                wide[s, SUB + r : SUB + r + STEP, :] = raw[
                    step_id, s, r : r + STEP, cols
                ].astype(F32)
        key_taps = tap_rows(taps_ref, 1, cols)
        value_taps = tap_rows(taps_ref, 2, cols)
        keep = [spread(keep_ref, m, cols) for m in range(modes)]
        total = None
        for part in range(2):
            base = part * half
            states = None
            load = lambda s, at: wide[s, pl.ds(SUB + base + at, SUB, stride=run), :]
            lines = [[load(s, at) for at in range(-rim, 0)] for s in range(2)]
            for j in range(run):
                lines = [line[-rim:] + [load(s, j)] for s, line in enumerate(lines)]
                gate = short_conv(lines[0], key_taps) * short_conv(lines[1], value_taps)
                if part == 0 and j < rim:
                    gate = jnp.where(index == 0, 0.0, gate)
                gate_ref[pl.ds(t * toks + base + j, SUB, stride=run), :] = gate
                if states is None:
                    states = [gate] * modes
                else:
                    states = [k * state + gate for k, state in zip(keep, states)]
            for m, end in enumerate(states):
                ends_ref[t, part, m * SUB : (m + 1) * SUB, :] = end
            run_keep = run_ref[:, cols]
            for i in range(SUB):
                end = modes_at(ends_ref.at[t, part], i, modes)
                total = end if total is None else run_keep * total + end
        state_ref[:, cols] = total
        sum_ref[:modes, cols] = total.astype(BF16)
        query = raw_query[step_id, :, :, cols].astype(F32)
        sum_ref[modes:, cols] = jnp.concatenate(
            [
                wide[0, SUB : SUB + rim, :],
                wide[1, SUB : SUB + rim, :],
                query[1, PAIR - rim :],
                wide[0, SUB + toks - rim : SUB + toks, :],
                wide[1, SUB + toks - rim : SUB + toks, :],
                query[0, :rim],
                jnp.zeros((PAIR - 6 * rim, LANES), F32),
            ],
            axis=0,
        ).astype(BF16)


def first_gates(past, first, taps):
    rows = []
    for s in range(2):
        before, here = past[s], first[s]
        line = [before[0:1], before[1:2], here[0:1], here[1:2]]
        rows.append(
            [
                taps[s][0] * line[at] + taps[s][1] * line[at - 1] + taps[s][2] * line[at - 2]
                for at in (2, 3)
            ]
        )
    return [key * value for key, value in zip(*rows)]


def join_kernel(ids, stride, count, toks, last, *refs):
    taps_ref, rate_ref, state_ref, prefix_ref, past_ref, own_ref = refs[:6]
    near = (own_ref,) + refs[6 : 5 + count]
    shared = count == 4 and stride % 2 == 0
    outs = refs[5 + count :]
    prefix_out, past_out = outs[:2]
    modes, width = rate_ref.shape
    index = ids[0]
    place = lax.rem(lax.div(index, stride), count)
    behind = lax.rem(index, stride)
    origins = [lax.rem(place - k + count, count) for k in range(count)]
    as_float = lambda n: n.astype(F32)

    def tile(t, _):
        cols = pl.ds(pl.multiple_of(t * LANES, LANES), LANES)
        rates = rate_ref[:, cols]
        span = rates * float(toks)
        taps = [[taps_ref[j, s : s + 1, cols] for j in range(3)] for s in (1, 2)]
        full = [ref[:, cols].astype(F32) for ref in near]
        if shared:
            odd = lax.rem(index, 2) == 1
            full[1], full[3] = jnp.where(odd, full[3], full[1]), jnp.where(odd, full[1], full[3])
        extra = [value[modes:] for value in full]
        firsts = [(e[0:2], e[2:4]) for e in extra]
        states = [state_ref[:, cols]] + [value[:modes] for value in full[1:]]
        first_keep = jnp.exp(-rates * float(toks - 1))
        second_keep = jnp.exp(-rates * float(toks - 2))
        rest = jnp.exp(-span * float(stride - 1))
        joins = []
        for k in range(count):
            linked = origins[k] >= 1
            past = extra[(k + 1) % count][4:10]
            past = jnp.where(linked, past, 0.0)
            one, two = first_gates((past[2:4], past[4:6]), firsts[k], taps)
            join = first_keep * one + second_keep * two
            if not last:
                join = jnp.where(linked, join, 0.0)
            joins.append(join)
            states[k] = states[k] + rest * join
        prefix = prefix_ref[:, cols] + jnp.where(
            behind >= 1,
            jnp.exp(-span * as_float(jnp.maximum(behind - 1, 0))) * joins[0],
            0.0,
        )
        for k in range(1, count):
            gap = as_float((k - 1) * stride + behind)
            prefix = prefix + jnp.where(place >= k, jnp.exp(-span * gap) * states[k], 0.0)
        prefix_out[:, cols] = prefix
        past = jnp.where((place >= 1) & (behind == 0), extra[1][4:10], past_ref[0:6, cols])
        past_out[:, cols] = jnp.concatenate([past, jnp.zeros((SUB - 6, LANES), F32)], axis=0)
        if not last:
            state_out, sum_out = outs[2:]
            total = None
            for k in range(count):
                gap = as_float((count - 1 - origins[k]) * stride)
                term = jnp.exp(-span * gap) * states[k]
                total = term if total is None else total + term
            state_out[:, cols] = total
            first = extra[0]
            end = extra[0]
            for k in range(1, count):
                first = jnp.where(origins[k] == 0, extra[k], first)
                end = jnp.where(origins[k] == count - 1, extra[k], end)
            sum_out[:modes, cols] = total.astype(BF16)
            sum_out[modes:, cols] = jnp.concatenate([first[0:4], end[4:]], axis=0).astype(BF16)
        return 0

    lax.fori_loop(0, width // LANES, tile, 0)


def local_kernel(
    first_strip, part_id, x_hbm, taps_ref, gate_ref, ends_ref, res_ref, rate_ref, skip_ref, *refs
):
    query_ref, local_ref, raw, wide, begins, keep_ref, gain_ref, run_ref, sems = refs[-9:]
    step_id = pl.program_id(0)
    part = part_id[0]
    _, toks, width = raw.shape
    half = toks // 2
    rim = taps_ref.shape[0] - 1
    modes = rate_ref.shape[0]
    run = half // SUB

    def fetch(i):
        return pltpu.make_async_copy(
            x_hbm.at[0, :, pl.ds(pl.multiple_of((first_strip + i) * width, LANES), width)],
            raw.at[i],
            sems.at[i],
        )

    @pl.when(step_id == 0)
    def _():
        for i in range(raw.shape[0]):
            fetch(i).start()

    rates = rate_ref[...]
    keep_ref[...] = jnp.exp(-rates)
    run_ref[...] = jnp.exp(-rates * run)
    gain_ref[...] = res_ref[...] * jnp.sqrt(2.0 * rates)
    for t, c in enumerate(range(0, width, LANES)):
        cols = slice(c, c + LANES)
        run_keep = run_ref[:, cols]
        state = jnp.zeros((modes, LANES), F32)
        for i in range(SUB):
            state = run_keep * state + modes_at(ends_ref.at[t, 0], i, modes)
        state = jnp.where(part == 0, 0.0, state)
        for i in range(SUB):
            put_modes_at(begins, i, state)
            if i + 1 < SUB:
                state = run_keep * state + modes_at(ends_ref.at[t, part], i, modes)
        keep = [spread(keep_ref, m, cols) for m in range(modes)]
        gains = [spread(gain_ref, m, cols) for m in range(modes)]
        skip = spread(skip_ref, 0, cols)
        states = [begins[m * SUB : (m + 1) * SUB, :] for m in range(modes)]
        for j in range(run):
            now = gate_ref[pl.ds(t * toks + part * half + j, SUB, stride=run), :]
            states = [k * state + now for k, state in zip(keep, states)]
            local_ref[pl.ds(t * half + j, SUB, stride=run), :] = tree_sum(
                [skip * now] + [gain * state for gain, state in zip(gains, states)]
            )

    fetch(step_id).wait()
    start = pl.multiple_of(part * half, half)
    for t, c in enumerate(range(0, width, LANES)):
        cols = slice(c, c + LANES)
        for r in range(0, half, STEP):
            wide[SUB + r : SUB + r + STEP, :] = raw[
                step_id, pl.ds(pl.multiple_of(start + r, STEP), STEP), cols
            ].astype(F32)
        before = raw[step_id, half - 16 : half, cols].astype(F32)[16 - rim :]
        wide[SUB - rim : SUB, :] = before
        taps = tap_rows(taps_ref, 0, cols)
        load = lambda at: wide[pl.ds(SUB + at, SUB, stride=run), :]
        line = [load(at) for at in range(-rim, 0)]
        for j in range(run):
            line = line[-rim:] + [load(j)]
            query_ref[pl.ds(t * half + j, SUB, stride=run), :] = short_conv(line, taps)


def finish_kernel(
    ids, query_ref, local_ref, prefix_ref, past_ref, sum_ref, taps_ref, res_ref, rate_ref, skip_ref,
    out_ref, begins, carry,
):
    part = ids[0]
    modes, width = prefix_ref.shape
    half = out_ref.shape[0]
    run = half // SUB
    row = lax.broadcasted_iota(jnp.int32, (STEP, LANES), 0)

    def tile(t, _):
        cols = pl.ds(pl.multiple_of(t * LANES, LANES), LANES)
        rates = rate_ref[:, cols]
        gains = res_ref[:, cols] * jnp.sqrt(2.0 * rates)
        keep_all = jnp.exp(-rates)
        run_keep = jnp.exp(-rates * run)
        past = past_ref[:, cols]
        here = sum_ref[modes:, cols].astype(F32)
        taps = [[taps_ref[j, s : s + 1, cols] for j in range(3)] for s in range(3)]
        one, two = first_gates((past[2:4], past[4:6]), (here[0:2], here[2:4]), taps[1:])
        line = [past[0:1], past[1:2], here[10:11], here[11:12]]
        queries = [
            taps[0][0] * line[at] + taps[0][1] * line[at - 1] + taps[0][2] * line[at - 2]
            for at in (2, 3)
        ]
        grow = jnp.exp(rates)
        state = gains * (prefix_ref[:, cols] + grow * (one + grow * two))
        state = state * jnp.where(part == 0, keep_all, jnp.exp(-rates * (half + 1)))
        for i in range(SUB):
            put_modes_at(begins, i, state)
            state = run_keep * state
        keep = [jnp.broadcast_to(keep_all[m : m + 1], (SUB, LANES)) for m in range(modes)]
        states = [begins[m * SUB : (m + 1) * SUB, :] for m in range(modes)]
        for j in range(run):
            carry[pl.ds(j, SUB, stride=run), :] = tree_sum(states)
            states = [k * state for k, state in zip(keep, states)]
        skip = skip_ref[:, cols]
        over = jnp.sum(gains * grow, axis=0, keepdims=True)
        for r in range(0, half, STEP):
            rows = pl.ds(pl.multiple_of(t * half + r, STEP), STEP)
            value = query_ref[rows, :] * (local_ref[rows, :] + carry[r : r + STEP, :])
            if r == 0:
                begin = carry[0:SUB, :]
                head = queries[0] * (begin[0:1] - over * two + skip * one)
                second = queries[1] * (begin[1:2] + skip * two)
                value = jnp.where((row == 0) & (part == 0), head, value)
                value = jnp.where((row == 1) & (part == 0), second, value)
            out_ref[r : r + STEP, cols] = value.astype(BF16)
        return 0

    lax.fori_loop(0, width // LANES, tile, 0)


def place_kernel(ids, far_ref, held_ref, out_ref, sem):
    del held_ref
    width = far_ref.shape[1]
    copy = pltpu.make_async_copy(
        far_ref,
        out_ref.at[:, pl.ds(pl.multiple_of(ids[0] * width, LANES), width)],
        sem,
    )
    copy.start()
    copy.wait()


def exchange(summary, blocks, index, stride, count):
    def route(hop):
        pairs = []
        for i in range(blocks):
            j = i // stride % count
            pairs.append((i, i + ((j + hop(i)) % count - j) * stride))
        return pairs

    def send(value, hop):
        return lax.ppermute(value, "ctx", route(hop))

    if count != 4 or stride % 2:
        return [send(summary, lambda i, k=k: k) for k in range(1, count)]
    beside = send(summary, lambda i: 3 if i % 2 else 1)
    across = send(summary, lambda i: 2)
    other = lax.ppermute(beside, "ctx", [(i, i ^ 1) for i in range(blocks)])
    return [beside, across, other]


def scan_counts(blocks):
    counts = [2] if blocks % 2 == 0 else []
    left = blocks // 2 if counts else blocks
    while left % 4 == 0:
        counts.append(4)
        left //= 4
    if left > 1:
        counts.append(left)
    return counts


def shards(streams, short_filter, residue, decay_rate, skip_gain):
    ctx_count = lax.axis_size("ctx")
    index = lax.axis_index("ctx")
    side = lax.axis_index("chan").astype(jnp.int32).reshape(1)
    toks, _, width = streams.shape
    half = toks // 2
    modes = residue.shape[1]
    rim = short_filter.shape[0] - 1
    tile = 256 if width % 256 == 0 else LANES
    steps = width // tile
    tiles = tile // LANES
    all_tiles = width // LANES

    x = jnp.transpose(streams, (1, 0, 2))
    rates = decay_rate.T
    weights = residue.T
    skip = skip_gain[None, :]
    x_kept, taps_kept, rates_kept = (
        pltpu.with_memory_space_constraint(a, pltpu.HBM) for a in (x, short_filter, rates)
    )
    params = pltpu.CompilerParams(vmem_limit_bytes=VMEM_LIMIT)
    in_hbm = pl.BlockSpec(memory_space=pltpu.HBM)
    strip = lambda *lead: pl.BlockSpec(lead + (tile,), lambda i, *_: (0,) * len(lead) + (i,))
    tall = lambda rows: pl.BlockSpec((tiles * rows, LANES), lambda i, *_: (i, 0))
    ends_spec = pl.BlockSpec((tiles, 2, modes * SUB, LANES), lambda i, *_: (i, 0, 0, 0))
    gate, ends, state, summary = pl.pallas_call(
        state_kernel,
        grid=(steps,),
        in_specs=[in_hbm] * 3,
        out_specs=[tall(toks), ends_spec, strip(modes), strip(modes + PAIR)],
        out_shape=[
            jax.ShapeDtypeStruct((all_tiles * toks, LANES), F32),
            jax.ShapeDtypeStruct((all_tiles, 2, modes * SUB, LANES), F32),
            jax.ShapeDtypeStruct((modes, width), F32),
            jax.ShapeDtypeStruct((modes + PAIR, width), BF16),
        ],
        scratch_shapes=[
            pltpu.VMEM((steps, 2, toks, tile), BF16),
            pltpu.VMEM((steps, 2, PAIR, tile), BF16),
            pltpu.VMEM((2, toks + SUB, LANES), F32),
            pltpu.VMEM((modes, tile), F32),
            pltpu.VMEM((modes, tile), F32),
            pltpu.VMEM((rim + 1, 3, width), F32),
            pltpu.VMEM((modes, width), F32),
            pltpu.SemaphoreType.DMA((3, steps)),
            pltpu.SemaphoreType.DMA((2,)),
        ],
        compiler_params=params,
        name="states",
    )(x_kept, taps_kept, rates_kept)

    def shifted(first, *lead):
        return pl.BlockSpec(lead + (tile,), lambda i, *_: (0,) * len(lead) + (first + i,))

    def local(which, gate, first, count, held, name):
        return pl.pallas_call(
            functools.partial(local_kernel, first),
            grid_spec=pltpu.PrefetchScalarGridSpec(
                num_scalar_prefetch=1,
                grid=(count,),
                in_specs=[
                    in_hbm,
                    shifted(first, rim + 1, 3),
                    pl.BlockSpec((tiles * toks, LANES), lambda i, *_: (first + i, 0)),
                    pl.BlockSpec(
                        (tiles, 2, modes * SUB, LANES), lambda i, *_: (first + i, 0, 0, 0)
                    ),
                    shifted(first, modes),
                    shifted(first, modes),
                    shifted(first, 1),
                ]
                + [pl.BlockSpec(memory_space=pl.ANY)] * len(held),
                out_specs=[pl.BlockSpec((tiles * half, LANES), lambda i, *_: (first + i, 0))] * 2,
                scratch_shapes=[
                    pltpu.VMEM((count, toks, tile), BF16),
                    pltpu.VMEM((half + SUB, LANES), F32),
                    pltpu.VMEM((modes * SUB, LANES), F32),
                    pltpu.VMEM((modes, tile), F32),
                    pltpu.VMEM((modes, tile), F32),
                    pltpu.VMEM((modes, tile), F32),
                    pltpu.SemaphoreType.DMA((count,)),
                ],
            ),
            out_shape=[jax.ShapeDtypeStruct((all_tiles * half, LANES), F32)] * 2,
            input_output_aliases={8: 0, 9: 1} if held else {},
            compiler_params=params,
            name=name,
        )(which, x_kept, short_filter, gate, ends, weights, rates, skip, *held)

    few = steps // 2
    locals_sent = local(1 - side, gate, 0, few, (), "local_sent_0")

    ids = index.astype(jnp.int32).reshape(1)
    in_vmem = pl.BlockSpec(memory_space=pltpu.VMEM)
    prefix = jnp.zeros((modes, width), F32)
    past = jnp.zeros((SUB, width), F32)
    own = summary
    stride = 1
    counts = scan_counts(ctx_count)
    for level, count in enumerate(counts):
        last = level == len(counts) - 1
        if level == 2:
            summary, locals_sent = lax.optimization_barrier((summary, locals_sent))
            locals_sent = local(1 - side, gate, few, steps - few, locals_sent, "local_sent_1")
        if level == 3:
            summary, locals_sent = lax.optimization_barrier((summary, locals_sent))
        arrived = exchange(summary, ctx_count, index, stride, count)
        shapes = [
            jax.ShapeDtypeStruct((modes, width), F32),
            jax.ShapeDtypeStruct((SUB, width), F32),
        ]
        if not last:
            shapes += [
                jax.ShapeDtypeStruct((modes, width), F32),
                jax.ShapeDtypeStruct((modes + PAIR, width), BF16),
            ]

        def body(ids, *refs, stride=stride, count=count, last=last):
            join_kernel(ids, stride, count, toks, last, *refs)

        results = pl.pallas_call(
            body,
            in_specs=[pl.BlockSpec(memory_space=pltpu.SMEM)] + [in_vmem] * (5 + count),
            out_specs=[in_vmem] * len(shapes),
            out_shape=shapes,
            compiler_params=params,
            name=f"join_{level}",
        )(ids, short_filter, rates, state, prefix, past, summary, *arrived)
        prefix, past = results[:2]
        if not last:
            state, summary = results[2:]
        stride *= count

    def finish(which, column, columns, locals_, prefix, name):
        return pl.pallas_call(
            finish_kernel,
            grid_spec=pltpu.PrefetchScalarGridSpec(
                num_scalar_prefetch=1,
                grid=(steps,),
                in_specs=[
                    tall(half),
                    tall(half),
                    strip(modes),
                    strip(SUB),
                    strip(modes + PAIR),
                    strip(rim + 1, 3),
                    strip(modes),
                    strip(modes),
                    strip(1),
                ],
                out_specs=pl.BlockSpec((half, tile), lambda i, ids: (0, ids[1] * steps + i)),
                scratch_shapes=[
                    pltpu.VMEM((modes * SUB, LANES), F32),
                    pltpu.VMEM((half, LANES), F32),
                ],
            ),
            out_shape=jax.ShapeDtypeStruct((half, columns), BF16),
            compiler_params=params,
            name=name,
        )(
            jnp.concatenate([which, column]),
            *locals_,
            prefix,
            past,
            own,
            short_filter,
            weights,
            rates,
            skip,
        )

    sent = pl.pallas_call(
        finish_kernel,
        in_specs=[pl.BlockSpec(memory_space=pltpu.SMEM)] + [in_vmem] * 9,
        out_specs=in_vmem,
        out_shape=jax.ShapeDtypeStruct((half, width), BF16),
        scratch_shapes=[pltpu.VMEM((modes * SUB, LANES), F32), pltpu.VMEM((half, LANES), F32)],
        compiler_params=params,
        name="finish_sent",
    )(1 - side, *locals_sent, prefix, past, own, short_filter, weights, rates, skip)
    far = lax.ppermute(sent, "chan", [(0, 1), (1, 0)])
    prefix, gate, sent = lax.optimization_barrier((prefix, gate, sent))
    locals_own = local(side, gate, 0, steps, (), "local_own")
    held = finish(side, side, 2 * width, locals_own, prefix, "finish_own")
    return pl.pallas_call(
        place_kernel,
        grid_spec=pltpu.PrefetchScalarGridSpec(
            num_scalar_prefetch=1,
            grid=(1,),
            in_specs=[pl.BlockSpec(memory_space=pl.ANY)] * 2,
            out_specs=pl.BlockSpec(memory_space=pl.ANY),
            scratch_shapes=[pltpu.SemaphoreType.DMA(())],
        ),
        out_shape=jax.ShapeDtypeStruct((half, 2 * width), BF16),
        input_output_aliases={2: 0},
        compiler_params=params,
        name="place",
    )(1 - side, far, held)


def solution(mesh):
    return jax.shard_map(
        shards,
        mesh=mesh,
        in_specs=(
            P("ctx", None, "chan"),
            P(None, None, "chan"),
            P("chan", None),
            P("chan", None),
            P("chan"),
        ),
        out_specs=P(("ctx", "chan"), None),
        check_vma=False,
    )
```

```python
import functools

import jax
import jax.numpy as jnp
from jax import lax
from jax.experimental import pallas as pl
from jax.experimental.pallas import tpu as pltpu
from jax.sharding import PartitionSpec as P

LANES = 128
SUB = 8
UNROLL = 8
STEP = 32
PAIR = 16
F32 = jnp.float32
BF16 = jnp.bfloat16
VMEM_LIMIT = 16 * 1024 * 1024


def spread(ref, m, cols):
    return jnp.broadcast_to(ref[m : m + 1, cols], (SUB, LANES))


def tree_sum(terms):
    terms = list(terms)
    while len(terms) > 1:
        terms = [
            terms[i] + terms[i + 1] if i + 1 < len(terms) else terms[i]
            for i in range(0, len(terms), 2)
        ]
    return terms[0]


def short_conv(line, taps):
    total = taps[0] * line[-1]
    for k in range(1, len(taps)):
        total = total + taps[k] * line[-1 - k]
    return total


def tap_rows(taps_ref, s, cols):
    return [
        jnp.broadcast_to(taps_ref[j, s : s + 1, cols], (SUB, LANES))
        for j in range(taps_ref.shape[0])
    ]


def modes_at(ref, i, modes):
    return jnp.concatenate(
        [ref[pl.ds(i + SUB * m, SUB, stride=SUB), :] for m in range(0, modes, SUB)], axis=0
    )


def put_modes_at(ref, i, value):
    for m in range(0, value.shape[0], SUB):
        ref[pl.ds(i + SUB * m, SUB, stride=SUB), :] = value[m : m + SUB]


def state_kernel(
    x_hbm, taps_hbm, rate_hbm,
    gate_ref, ends_ref, state_ref, sum_ref,
    raw, raw_query, wide, keep_ref, run_ref, taps_all, rate_all, sems, small_sems,
):
    step_id = pl.program_id(0)
    _, _, toks, width = raw.shape
    half = toks // 2
    rim = taps_all.shape[0] - 1
    modes = rate_all.shape[0]
    run = half // SUB

    def fetches(i):
        cols = pl.ds(pl.multiple_of(i * width, LANES), width)
        return (
            pltpu.make_async_copy(x_hbm.at[pl.ds(1, 2), :, cols], raw.at[i], sems.at[0, i]),
            pltpu.make_async_copy(
                x_hbm.at[0, pl.ds(0, PAIR), cols], raw_query.at[i, 0], sems.at[1, i]
            ),
            pltpu.make_async_copy(
                x_hbm.at[0, pl.ds(toks - PAIR, PAIR), cols], raw_query.at[i, 1], sems.at[2, i]
            ),
        )

    small = (
        pltpu.make_async_copy(taps_hbm, taps_all, small_sems.at[0]),
        pltpu.make_async_copy(rate_hbm, rate_all, small_sems.at[1]),
    )

    @pl.when(step_id == 0)
    def _():
        for copy in small:
            copy.start()
        for i in range(raw.shape[0]):
            for copy in fetches(i):
                copy.start()
        for copy in small:
            copy.wait()

    strip = pl.ds(pl.multiple_of(step_id * width, LANES), width)
    taps_ref = taps_all.at[:, :, strip]
    rates = rate_all[:, strip]
    keep_ref[...] = jnp.exp(-rates)
    run_ref[...] = jnp.exp(-rates * run)
    for copy in fetches(step_id):
        copy.wait()
    index = lax.broadcasted_iota(jnp.int32, (SUB, LANES), 0)
    for t, c in enumerate(range(0, width, LANES)):
        cols = slice(c, c + LANES)
        for s in range(2):
            wide[s, :SUB, :] = jnp.zeros((SUB, LANES), F32)
            for r in range(0, toks, STEP):
                wide[s, SUB + r : SUB + r + STEP, :] = raw[
                    step_id, s, r : r + STEP, cols
                ].astype(F32)
        key_taps = tap_rows(taps_ref, 1, cols)
        value_taps = tap_rows(taps_ref, 2, cols)
        keep = [spread(keep_ref, m, cols) for m in range(modes)]
        total = None
        for part in range(2):
            base = part * half
            states = None
            load = lambda s, at: wide[s, pl.ds(SUB + base + at, SUB, stride=run), :]
            lines = [[load(s, at) for at in range(-rim, 0)] for s in range(2)]
            for j in range(run):
                lines = [line[-rim:] + [load(s, j)] for s, line in enumerate(lines)]
                gate = short_conv(lines[0], key_taps) * short_conv(lines[1], value_taps)
                if part == 0 and j < rim:
                    gate = jnp.where(index == 0, 0.0, gate)
                gate_ref[pl.ds(t * toks + base + j, SUB, stride=run), :] = gate
                if states is None:
                    states = [gate] * modes
                else:
                    states = [k * state + gate for k, state in zip(keep, states)]
            for m, end in enumerate(states):
                ends_ref[t, part, m * SUB : (m + 1) * SUB, :] = end
            run_keep = run_ref[:, cols]
            for i in range(SUB):
                end = modes_at(ends_ref.at[t, part], i, modes)
                total = end if total is None else run_keep * total + end
        state_ref[:, cols] = total
        sum_ref[:modes, cols] = total.astype(BF16)
        query = raw_query[step_id, :, :, cols].astype(F32)
        sum_ref[modes:, cols] = jnp.concatenate(
            [
                wide[0, SUB : SUB + rim, :],
                wide[1, SUB : SUB + rim, :],
                query[1, PAIR - rim :],
                wide[0, SUB + toks - rim : SUB + toks, :],
                wide[1, SUB + toks - rim : SUB + toks, :],
                query[0, :rim],
                jnp.zeros((PAIR - 6 * rim, LANES), F32),
            ],
            axis=0,
        ).astype(BF16)


def first_gates(past, first, taps):
    rows = []
    for s in range(2):
        before, here = past[s], first[s]
        line = [before[0:1], before[1:2], here[0:1], here[1:2]]
        rows.append(
            [
                taps[s][0] * line[at] + taps[s][1] * line[at - 1] + taps[s][2] * line[at - 2]
                for at in (2, 3)
            ]
        )
    return [key * value for key, value in zip(*rows)]


def join_kernel(ids, stride, count, toks, last, *refs):
    taps_ref, rate_ref, state_ref, prefix_ref, past_ref, own_ref = refs[:6]
    near = (own_ref,) + refs[6 : 5 + count]
    shared = count == 4 and stride % 2 == 0
    outs = refs[5 + count :]
    prefix_out, past_out = outs[:2]
    modes, width = rate_ref.shape
    index = ids[0]
    place = lax.rem(lax.div(index, stride), count)
    behind = lax.rem(index, stride)
    origins = [lax.rem(place - k + count, count) for k in range(count)]
    as_float = lambda n: n.astype(F32)

    def tile(t, _):
        cols = pl.ds(pl.multiple_of(t * LANES, LANES), LANES)
        rates = rate_ref[:, cols]
        span = rates * float(toks)
        taps = [[taps_ref[j, s : s + 1, cols] for j in range(3)] for s in (1, 2)]
        full = [ref[:, cols].astype(F32) for ref in near]
        if shared:
            odd = lax.rem(index, 2) == 1
            full[1], full[3] = jnp.where(odd, full[3], full[1]), jnp.where(odd, full[1], full[3])
        extra = [value[modes:] for value in full]
        firsts = [(e[0:2], e[2:4]) for e in extra]
        states = [state_ref[:, cols]] + [value[:modes] for value in full[1:]]
        keep = jnp.exp(-rates)
        second_keep = jnp.exp(-rates * float(toks - 2))
        first_keep = second_keep * keep
        block_keep = first_keep * keep
        rest = jnp.exp(-span * float(stride - 1)) if stride > 1 else 1.0
        run_keep = rest * block_keep
        powers = [1.0, run_keep]
        while len(powers) < count:
            powers.append(powers[-1] * run_keep)
        before = jnp.exp(-span * as_float(jnp.maximum(behind - 1, 0)))
        joins = []
        for k in range(count):
            linked = origins[k] >= 1
            past = extra[(k + 1) % count][4:10]
            past = jnp.where(linked, past, 0.0)
            one, two = first_gates((past[2:4], past[4:6]), firsts[k], taps)
            join = first_keep * one + second_keep * two
            if not last:
                join = jnp.where(linked, join, 0.0)
            joins.append(join)
            states[k] = states[k] + rest * join
        passed = jnp.where(behind >= 1, before * block_keep, 1.0)
        prefix = prefix_ref[:, cols] + jnp.where(behind >= 1, before * joins[0], 0.0)
        for k in range(1, count):
            prefix = prefix + jnp.where(place >= k, passed * powers[k - 1] * states[k], 0.0)
        prefix_out[:, cols] = prefix
        past = jnp.where((place >= 1) & (behind == 0), extra[1][4:10], past_ref[0:6, cols])
        past_out[:, cols] = jnp.concatenate([past, jnp.zeros((SUB - 6, LANES), F32)], axis=0)
        if not last:
            state_out, sum_out = outs[2:]
            total = None
            for k in range(count):
                factor = jnp.ones_like(run_keep)
                for gap in range(1, count):
                    factor = jnp.where(origins[k] == count - 1 - gap, powers[gap], factor)
                term = factor * states[k]
                total = term if total is None else total + term
            state_out[:, cols] = total
            first = extra[0]
            end = extra[0]
            for k in range(1, count):
                first = jnp.where(origins[k] == 0, extra[k], first)
                end = jnp.where(origins[k] == count - 1, extra[k], end)
            sum_out[:modes, cols] = total.astype(BF16)
            sum_out[modes:, cols] = jnp.concatenate([first[0:4], end[4:]], axis=0).astype(BF16)
        return 0

    lax.fori_loop(0, width // LANES, tile, 0, unroll=UNROLL)


def local_kernel(
    first_strip, part_id, x_hbm, taps_ref, gate_ref, ends_ref, res_ref, rate_ref, skip_ref, *refs
):
    query_ref, local_ref, raw, wide, begins, keep_ref, gain_ref, run_ref, sems = refs[-9:]
    step_id = pl.program_id(0)
    part = part_id[0]
    _, toks, width = raw.shape
    half = toks // 2
    rim = taps_ref.shape[0] - 1
    modes = rate_ref.shape[0]
    run = half // SUB

    def fetch(i):
        return pltpu.make_async_copy(
            x_hbm.at[0, :, pl.ds(pl.multiple_of((first_strip + i) * width, LANES), width)],
            raw.at[i],
            sems.at[i],
        )

    @pl.when(step_id == 0)
    def _():
        for i in range(raw.shape[0]):
            fetch(i).start()

    rates = rate_ref[...]
    keep_ref[...] = jnp.exp(-rates)
    run_ref[...] = jnp.exp(-rates * run)
    gain_ref[...] = res_ref[...] * jnp.sqrt(2.0 * rates)
    for t, c in enumerate(range(0, width, LANES)):
        cols = slice(c, c + LANES)
        run_keep = run_ref[:, cols]
        state = jnp.zeros((modes, LANES), F32)
        for i in range(SUB):
            state = run_keep * state + modes_at(ends_ref.at[t, 0], i, modes)
        state = jnp.where(part == 0, 0.0, state)
        for i in range(SUB):
            put_modes_at(begins, i, state)
            if i + 1 < SUB:
                state = run_keep * state + modes_at(ends_ref.at[t, part], i, modes)
        keep = [spread(keep_ref, m, cols) for m in range(modes)]
        gains = [spread(gain_ref, m, cols) for m in range(modes)]
        skip = spread(skip_ref, 0, cols)
        states = [begins[m * SUB : (m + 1) * SUB, :] for m in range(modes)]
        for j in range(run):
            now = gate_ref[pl.ds(t * toks + part * half + j, SUB, stride=run), :]
            states = [k * state + now for k, state in zip(keep, states)]
            local_ref[pl.ds(t * half + j, SUB, stride=run), :] = tree_sum(
                [skip * now] + [gain * state for gain, state in zip(gains, states)]
            )

    fetch(step_id).wait()
    start = pl.multiple_of(part * half, half)
    for t, c in enumerate(range(0, width, LANES)):
        cols = slice(c, c + LANES)
        for r in range(0, half, STEP):
            wide[SUB + r : SUB + r + STEP, :] = raw[
                step_id, pl.ds(pl.multiple_of(start + r, STEP), STEP), cols
            ].astype(F32)
        before = raw[step_id, half - 16 : half, cols].astype(F32)[16 - rim :]
        wide[SUB - rim : SUB, :] = before
        taps = tap_rows(taps_ref, 0, cols)
        load = lambda at: wide[pl.ds(SUB + at, SUB, stride=run), :]
        line = [load(at) for at in range(-rim, 0)]
        for j in range(run):
            line = line[-rim:] + [load(j)]
            query_ref[pl.ds(t * half + j, SUB, stride=run), :] = short_conv(line, taps)


def finish_kernel(
    ids, query_ref, local_ref, prefix_ref, past_ref, sum_ref, taps_ref, res_ref, rate_ref, skip_ref,
    out_ref, begins, carry,
):
    part = ids[0]
    modes, width = prefix_ref.shape
    half = out_ref.shape[0]
    run = half // SUB
    row = lax.broadcasted_iota(jnp.int32, (STEP, LANES), 0)

    def tile(t, _):
        cols = pl.ds(pl.multiple_of(t * LANES, LANES), LANES)
        rates = rate_ref[:, cols]
        gains = res_ref[:, cols] * jnp.sqrt(2.0 * rates)
        keep_all = jnp.exp(-rates)
        run_keep = jnp.exp(-rates * run)
        past = past_ref[:, cols]
        here = sum_ref[modes:, cols].astype(F32)
        taps = [[taps_ref[j, s : s + 1, cols] for j in range(3)] for s in range(3)]
        one, two = first_gates((past[2:4], past[4:6]), (here[0:2], here[2:4]), taps[1:])
        line = [past[0:1], past[1:2], here[10:11], here[11:12]]
        queries = [
            taps[0][0] * line[at] + taps[0][1] * line[at - 1] + taps[0][2] * line[at - 2]
            for at in (2, 3)
        ]
        grow = jnp.exp(rates)
        state = gains * (prefix_ref[:, cols] + grow * (one + grow * two))
        state = state * jnp.where(part == 0, keep_all, jnp.exp(-rates * (half + 1)))
        for i in range(SUB):
            put_modes_at(begins, i, state)
            state = run_keep * state
        keep = [jnp.broadcast_to(keep_all[m : m + 1], (SUB, LANES)) for m in range(modes)]
        states = [begins[m * SUB : (m + 1) * SUB, :] for m in range(modes)]
        for j in range(run):
            carry[pl.ds(j, SUB, stride=run), :] = tree_sum(states)
            states = [k * state for k, state in zip(keep, states)]
        skip = skip_ref[:, cols]
        over = jnp.sum(gains * grow, axis=0, keepdims=True)
        for r in range(0, half, STEP):
            rows = pl.ds(pl.multiple_of(t * half + r, STEP), STEP)
            value = query_ref[rows, :] * (local_ref[rows, :] + carry[r : r + STEP, :])
            if r == 0:
                begin = carry[0:SUB, :]
                head = queries[0] * (begin[0:1] - over * two + skip * one)
                second = queries[1] * (begin[1:2] + skip * two)
                value = jnp.where((row == 0) & (part == 0), head, value)
                value = jnp.where((row == 1) & (part == 0), second, value)
            out_ref[r : r + STEP, cols] = value.astype(BF16)
        return 0

    lax.fori_loop(0, width // LANES, tile, 0, unroll=UNROLL)


def place_kernel(ids, far_ref, held_ref, out_ref, sem):
    del held_ref
    width = far_ref.shape[1]
    copy = pltpu.make_async_copy(
        far_ref,
        out_ref.at[:, pl.ds(pl.multiple_of(ids[0] * width, LANES), width)],
        sem,
    )
    copy.start()
    copy.wait()


def exchange(summary, blocks, index, stride, count):
    def route(hop):
        pairs = []
        for i in range(blocks):
            j = i // stride % count
            pairs.append((i, i + ((j + hop(i)) % count - j) * stride))
        return pairs

    def send(value, hop):
        return lax.ppermute(value, "ctx", route(hop))

    if count != 4 or stride % 2:
        return [send(summary, lambda i, k=k: k) for k in range(1, count)]
    beside = send(summary, lambda i: 3 if i % 2 else 1)
    across = send(summary, lambda i: 2)
    other = lax.ppermute(beside, "ctx", [(i, i ^ 1) for i in range(blocks)])
    return [beside, across, other]


def scan_counts(blocks):
    counts = [2] if blocks % 2 == 0 else []
    left = blocks // 2 if counts else blocks
    while left % 4 == 0:
        counts.append(4)
        left //= 4
    if left > 1:
        counts.append(left)
    return counts


def shards(streams, short_filter, residue, decay_rate, skip_gain):
    ctx_count = lax.axis_size("ctx")
    index = lax.axis_index("ctx")
    side = lax.axis_index("chan").astype(jnp.int32).reshape(1)
    toks, _, width = streams.shape
    half = toks // 2
    modes = residue.shape[1]
    rim = short_filter.shape[0] - 1
    tile = 256 if width % 256 == 0 else LANES
    steps = width // tile
    tiles = tile // LANES
    all_tiles = width // LANES

    x = jnp.transpose(streams, (1, 0, 2))
    rates = decay_rate.T
    weights = residue.T
    skip = skip_gain[None, :]
    x_kept, taps_kept, rates_kept = (
        pltpu.with_memory_space_constraint(a, pltpu.HBM) for a in (x, short_filter, rates)
    )
    params = pltpu.CompilerParams(vmem_limit_bytes=VMEM_LIMIT)
    in_hbm = pl.BlockSpec(memory_space=pltpu.HBM)
    strip = lambda *lead: pl.BlockSpec(lead + (tile,), lambda i, *_: (0,) * len(lead) + (i,))
    tall = lambda rows: pl.BlockSpec((tiles * rows, LANES), lambda i, *_: (i, 0))
    ends_spec = pl.BlockSpec((tiles, 2, modes * SUB, LANES), lambda i, *_: (i, 0, 0, 0))
    gate, ends, state, summary = pl.pallas_call(
        state_kernel,
        grid=(steps,),
        in_specs=[in_hbm] * 3,
        out_specs=[tall(toks), ends_spec, strip(modes), strip(modes + PAIR)],
        out_shape=[
            jax.ShapeDtypeStruct((all_tiles * toks, LANES), F32),
            jax.ShapeDtypeStruct((all_tiles, 2, modes * SUB, LANES), F32),
            jax.ShapeDtypeStruct((modes, width), F32),
            jax.ShapeDtypeStruct((modes + PAIR, width), BF16),
        ],
        scratch_shapes=[
            pltpu.VMEM((steps, 2, toks, tile), BF16),
            pltpu.VMEM((steps, 2, PAIR, tile), BF16),
            pltpu.VMEM((2, toks + SUB, LANES), F32),
            pltpu.VMEM((modes, tile), F32),
            pltpu.VMEM((modes, tile), F32),
            pltpu.VMEM((rim + 1, 3, width), F32),
            pltpu.VMEM((modes, width), F32),
            pltpu.SemaphoreType.DMA((3, steps)),
            pltpu.SemaphoreType.DMA((2,)),
        ],
        compiler_params=params,
        name="states",
    )(x_kept, taps_kept, rates_kept)

    def shifted(first, *lead):
        return pl.BlockSpec(lead + (tile,), lambda i, *_: (0,) * len(lead) + (first + i,))

    def local(which, gate, first, count, held, name):
        return pl.pallas_call(
            functools.partial(local_kernel, first),
            grid_spec=pltpu.PrefetchScalarGridSpec(
                num_scalar_prefetch=1,
                grid=(count,),
                in_specs=[
                    in_hbm,
                    shifted(first, rim + 1, 3),
                    pl.BlockSpec((tiles * toks, LANES), lambda i, *_: (first + i, 0)),
                    pl.BlockSpec(
                        (tiles, 2, modes * SUB, LANES), lambda i, *_: (first + i, 0, 0, 0)
                    ),
                    shifted(first, modes),
                    shifted(first, modes),
                    shifted(first, 1),
                ]
                + [pl.BlockSpec(memory_space=pl.ANY)] * len(held),
                out_specs=[pl.BlockSpec((tiles * half, LANES), lambda i, *_: (first + i, 0))] * 2,
                scratch_shapes=[
                    pltpu.VMEM((count, toks, tile), BF16),
                    pltpu.VMEM((half + SUB, LANES), F32),
                    pltpu.VMEM((modes * SUB, LANES), F32),
                    pltpu.VMEM((modes, tile), F32),
                    pltpu.VMEM((modes, tile), F32),
                    pltpu.VMEM((modes, tile), F32),
                    pltpu.SemaphoreType.DMA((count,)),
                ],
            ),
            out_shape=[jax.ShapeDtypeStruct((all_tiles * half, LANES), F32)] * 2,
            input_output_aliases={8: 0, 9: 1} if held else {},
            compiler_params=params,
            name=name,
        )(which, x_kept, short_filter, gate, ends, weights, rates, skip, *held)

    few = steps // 2
    locals_sent = ()
    ids = index.astype(jnp.int32).reshape(1)
    in_vmem = pl.BlockSpec(memory_space=pltpu.VMEM)
    prefix = jnp.zeros((modes, width), F32)
    past = jnp.zeros((SUB, width), F32)
    own = summary
    stride = 1
    counts = scan_counts(ctx_count)
    for level, count in enumerate(counts):
        last = level == len(counts) - 1
        arrived = exchange(summary, ctx_count, index, stride, count)
        if level >= 2:
            gate, arrived[0] = lax.optimization_barrier((gate, arrived[0]))
            first = 0 if level == 2 else few
            locals_sent = local(1 - side, gate, first, few, locals_sent, f"local_sent_{level}")
            locals_sent, arrived = lax.optimization_barrier((locals_sent, arrived))
        shapes = [
            jax.ShapeDtypeStruct((modes, width), F32),
            jax.ShapeDtypeStruct((SUB, width), F32),
        ]
        if not last:
            shapes += [
                jax.ShapeDtypeStruct((modes, width), F32),
                jax.ShapeDtypeStruct((modes + PAIR, width), BF16),
            ]

        def body(ids, *refs, stride=stride, count=count, last=last):
            join_kernel(ids, stride, count, toks, last, *refs)

        results = pl.pallas_call(
            body,
            in_specs=[pl.BlockSpec(memory_space=pltpu.SMEM)] + [in_vmem] * (5 + count),
            out_specs=[in_vmem] * len(shapes),
            out_shape=shapes,
            compiler_params=params,
            name=f"join_{level}",
        )(ids, short_filter, rates, state, prefix, past, summary, *arrived)
        prefix, past = results[:2]
        if not last:
            state, summary = results[2:]
        stride *= count

    def finish(which, column, columns, locals_, prefix, name):
        return pl.pallas_call(
            finish_kernel,
            grid_spec=pltpu.PrefetchScalarGridSpec(
                num_scalar_prefetch=1,
                grid=(steps,),
                in_specs=[
                    tall(half),
                    tall(half),
                    strip(modes),
                    strip(SUB),
                    strip(modes + PAIR),
                    strip(rim + 1, 3),
                    strip(modes),
                    strip(modes),
                    strip(1),
                ],
                out_specs=pl.BlockSpec((half, tile), lambda i, ids: (0, ids[1] * steps + i)),
                scratch_shapes=[
                    pltpu.VMEM((modes * SUB, LANES), F32),
                    pltpu.VMEM((half, LANES), F32),
                ],
            ),
            out_shape=jax.ShapeDtypeStruct((half, columns), BF16),
            compiler_params=params,
            name=name,
        )(
            jnp.concatenate([which, column]),
            *locals_,
            prefix,
            past,
            own,
            short_filter,
            weights,
            rates,
            skip,
        )

    sent = pl.pallas_call(
        finish_kernel,
        in_specs=[pl.BlockSpec(memory_space=pltpu.SMEM)] + [in_vmem] * 9,
        out_specs=in_vmem,
        out_shape=jax.ShapeDtypeStruct((half, width), BF16),
        scratch_shapes=[pltpu.VMEM((modes * SUB, LANES), F32), pltpu.VMEM((half, LANES), F32)],
        compiler_params=params,
        name="finish_sent",
    )(1 - side, *locals_sent, prefix, past, own, short_filter, weights, rates, skip)
    far = lax.ppermute(sent, "chan", [(0, 1), (1, 0)])
    prefix, gate, sent = lax.optimization_barrier((prefix, gate, sent))
    locals_own = local(side, gate, 0, steps, (), "local_own")
    held = finish(side, side, 2 * width, locals_own, prefix, "finish_own")
    return pl.pallas_call(
        place_kernel,
        grid_spec=pltpu.PrefetchScalarGridSpec(
            num_scalar_prefetch=1,
            grid=(1,),
            in_specs=[pl.BlockSpec(memory_space=pl.ANY)] * 2,
            out_specs=pl.BlockSpec(memory_space=pl.ANY),
            scratch_shapes=[pltpu.SemaphoreType.DMA(())],
        ),
        out_shape=jax.ShapeDtypeStruct((half, 2 * width), BF16),
        input_output_aliases={2: 0},
        compiler_params=params,
        name="place",
    )(1 - side, far, held)


def solution(mesh):
    return jax.shard_map(
        shards,
        mesh=mesh,
        in_specs=(
            P("ctx", None, "chan"),
            P(None, None, "chan"),
            P("chan", None),
            P("chan", None),
            P("chan"),
        ),
        out_specs=P(("ctx", "chan"), None),
        check_vma=False,
    )
```

```python
import functools

import jax
import jax.numpy as jnp
from jax import lax
from jax.experimental import pallas as pl
from jax.experimental.pallas import tpu as pltpu
from jax.sharding import PartitionSpec as P

LANES = 128
SUB = 8
UNROLL = 8
STEP = 32
PAIR = 16
F32 = jnp.float32
BF16 = jnp.bfloat16
VMEM_LIMIT = 16 * 1024 * 1024


def spread(ref, m, cols):
    return jnp.broadcast_to(ref[m : m + 1, cols], (SUB, LANES))


def tree_sum(terms):
    terms = list(terms)
    while len(terms) > 1:
        terms = [
            terms[i] + terms[i + 1] if i + 1 < len(terms) else terms[i]
            for i in range(0, len(terms), 2)
        ]
    return terms[0]


def short_conv(line, taps):
    total = taps[0] * line[-1]
    for k in range(1, len(taps)):
        total = total + taps[k] * line[-1 - k]
    return total


def tap_rows(taps_ref, s, cols):
    return [
        jnp.broadcast_to(taps_ref[j, s : s + 1, cols], (SUB, LANES))
        for j in range(taps_ref.shape[0])
    ]


def modes_at(ref, i, modes):
    return jnp.concatenate(
        [ref[pl.ds(i + SUB * m, SUB, stride=SUB), :] for m in range(0, modes, SUB)], axis=0
    )


def put_modes_at(ref, i, value):
    for m in range(0, value.shape[0], SUB):
        ref[pl.ds(i + SUB * m, SUB, stride=SUB), :] = value[m : m + SUB]


def state_kernel(
    x_hbm, taps_hbm, rate_hbm,
    gate_ref, ends_ref, state_ref, sum_ref,
    raw, raw_query, wide, keep_ref, run_ref, taps_all, rate_all, sems, small_sems,
):
    step_id = pl.program_id(0)
    _, _, toks, width = raw.shape
    half = toks // 2
    rim = taps_all.shape[0] - 1
    modes = rate_all.shape[0]
    run = half // SUB

    def fetches(i):
        cols = pl.ds(pl.multiple_of(i * width, LANES), width)
        return (
            pltpu.make_async_copy(x_hbm.at[pl.ds(1, 2), :, cols], raw.at[i], sems.at[0, i]),
            pltpu.make_async_copy(
                x_hbm.at[0, pl.ds(0, PAIR), cols], raw_query.at[i, 0], sems.at[1, i]
            ),
            pltpu.make_async_copy(
                x_hbm.at[0, pl.ds(toks - PAIR, PAIR), cols], raw_query.at[i, 1], sems.at[2, i]
            ),
        )

    small = (
        pltpu.make_async_copy(taps_hbm, taps_all, small_sems.at[0]),
        pltpu.make_async_copy(rate_hbm, rate_all, small_sems.at[1]),
    )

    @pl.when(step_id == 0)
    def _():
        for copy in small:
            copy.start()
        for i in range(raw.shape[0]):
            for copy in fetches(i):
                copy.start()
        for copy in small:
            copy.wait()

    strip = pl.ds(pl.multiple_of(step_id * width, LANES), width)
    taps_ref = taps_all.at[:, :, strip]
    rates = rate_all[:, strip]
    keep_ref[...] = jnp.exp(-rates)
    run_ref[...] = jnp.exp(-rates * run)
    for copy in fetches(step_id):
        copy.wait()
    index = lax.broadcasted_iota(jnp.int32, (SUB, LANES), 0)
    for t, c in enumerate(range(0, width, LANES)):
        cols = slice(c, c + LANES)
        for s in range(2):
            wide[s, :SUB, :] = jnp.zeros((SUB, LANES), F32)
            for r in range(0, toks, STEP):
                wide[s, SUB + r : SUB + r + STEP, :] = raw[
                    step_id, s, r : r + STEP, cols
                ].astype(F32)
        key_taps = tap_rows(taps_ref, 1, cols)
        value_taps = tap_rows(taps_ref, 2, cols)
        keep = [spread(keep_ref, m, cols) for m in range(modes)]
        total = None
        for part in range(2):
            base = part * half
            states = None
            load = lambda s, at: wide[s, pl.ds(SUB + base + at, SUB, stride=run), :]
            lines = [[load(s, at) for at in range(-rim, 0)] for s in range(2)]
            for j in range(run):
                lines = [line[-rim:] + [load(s, j)] for s, line in enumerate(lines)]
                gate = short_conv(lines[0], key_taps) * short_conv(lines[1], value_taps)
                if part == 0 and j < rim:
                    gate = jnp.where(index == 0, 0.0, gate)
                gate_ref[pl.ds(t * toks + base + j, SUB, stride=run), :] = gate
                if states is None:
                    states = [gate] * modes
                else:
                    states = [k * state + gate for k, state in zip(keep, states)]
            for m, end in enumerate(states):
                ends_ref[t, part, m * SUB : (m + 1) * SUB, :] = end
            run_keep = run_ref[:, cols]
            for i in range(SUB):
                end = modes_at(ends_ref.at[t, part], i, modes)
                total = end if total is None else run_keep * total + end
        state_ref[:, cols] = total
        sum_ref[:modes, cols] = total.astype(BF16)
        query = raw_query[step_id, :, :, cols].astype(F32)
        sum_ref[modes:, cols] = jnp.concatenate(
            [
                wide[0, SUB : SUB + rim, :],
                wide[1, SUB : SUB + rim, :],
                query[1, PAIR - rim :],
                wide[0, SUB + toks - rim : SUB + toks, :],
                wide[1, SUB + toks - rim : SUB + toks, :],
                query[0, :rim],
                jnp.zeros((PAIR - 6 * rim, LANES), F32),
            ],
            axis=0,
        ).astype(BF16)


def first_gates(past, first, taps):
    rows = []
    for s in range(2):
        before, here = past[s], first[s]
        line = [before[0:1], before[1:2], here[0:1], here[1:2]]
        rows.append(
            [
                taps[s][0] * line[at] + taps[s][1] * line[at - 1] + taps[s][2] * line[at - 2]
                for at in (2, 3)
            ]
        )
    return [key * value for key, value in zip(*rows)]


def join_kernel(ids, stride, count, toks, last, *refs):
    taps_ref, rate_ref, state_ref, prefix_ref, past_ref, own_ref = refs[:6]
    near = (own_ref,) + refs[6 : 5 + count]
    shared = count == 4 and stride % 2 == 0
    outs = refs[5 + count :]
    prefix_out, past_out = outs[:2]
    modes, width = rate_ref.shape
    index = ids[0]
    place = lax.rem(lax.div(index, stride), count)
    behind = lax.rem(index, stride)
    origins = [lax.rem(place - k + count, count) for k in range(count)]
    as_float = lambda n: n.astype(F32)

    def tile(t, _):
        cols = pl.ds(pl.multiple_of(t * LANES, LANES), LANES)
        rates = rate_ref[:, cols]
        span = rates * float(toks)
        taps = [[taps_ref[j, s : s + 1, cols] for j in range(3)] for s in (1, 2)]
        full = [ref[:, cols].astype(F32) for ref in near]
        if shared:
            odd = lax.rem(index, 2) == 1
            full[1], full[3] = jnp.where(odd, full[3], full[1]), jnp.where(odd, full[1], full[3])
        extra = [value[modes:] for value in full]
        firsts = [(e[0:2], e[2:4]) for e in extra]
        states = [state_ref[:, cols]] + [value[:modes] for value in full[1:]]
        keep = jnp.exp(-rates)
        second_keep = jnp.exp(-rates * float(toks - 2))
        first_keep = second_keep * keep
        block_keep = first_keep * keep
        rest = jnp.exp(-span * float(stride - 1)) if stride > 1 else 1.0
        run_keep = rest * block_keep
        powers = [1.0, run_keep]
        while len(powers) < count:
            powers.append(powers[-1] * run_keep)
        before = jnp.exp(-span * as_float(jnp.maximum(behind - 1, 0)))
        joins = []
        for k in range(count):
            linked = origins[k] >= 1
            past = extra[(k + 1) % count][4:10]
            past = jnp.where(linked, past, 0.0)
            one, two = first_gates((past[2:4], past[4:6]), firsts[k], taps)
            join = first_keep * one + second_keep * two
            if not last:
                join = jnp.where(linked, join, 0.0)
            joins.append(join)
            states[k] = states[k] + rest * join
        passed = jnp.where(behind >= 1, before * block_keep, 1.0)
        prefix = prefix_ref[:, cols] + jnp.where(behind >= 1, before * joins[0], 0.0)
        for k in range(1, count):
            prefix = prefix + jnp.where(place >= k, passed * powers[k - 1] * states[k], 0.0)
        prefix_out[:, cols] = prefix
        past = jnp.where((place >= 1) & (behind == 0), extra[1][4:10], past_ref[0:6, cols])
        past_out[:, cols] = jnp.concatenate([past, jnp.zeros((SUB - 6, LANES), F32)], axis=0)
        if not last:
            state_out, sum_out = outs[2:]
            total = None
            for k in range(count):
                factor = jnp.ones_like(run_keep)
                for gap in range(1, count):
                    factor = jnp.where(origins[k] == count - 1 - gap, powers[gap], factor)
                term = factor * states[k]
                total = term if total is None else total + term
            state_out[:, cols] = total
            first = extra[0]
            end = extra[0]
            for k in range(1, count):
                first = jnp.where(origins[k] == 0, extra[k], first)
                end = jnp.where(origins[k] == count - 1, extra[k], end)
            sum_out[:modes, cols] = total.astype(BF16)
            sum_out[modes:, cols] = jnp.concatenate([first[0:4], end[4:]], axis=0).astype(BF16)
        return 0

    lax.fori_loop(0, width // LANES, tile, 0, unroll=UNROLL)


def local_kernel(
    first_strip, part_id, x_hbm, taps_ref, gate_ref, ends_ref, res_ref, rate_ref, skip_ref, *refs
):
    query_ref, local_ref, raw, wide, begins, keep_ref, gain_ref, run_ref, sems = refs[-9:]
    step_id = pl.program_id(0)
    part = part_id[0]
    _, toks, width = raw.shape
    half = toks // 2
    rim = taps_ref.shape[0] - 1
    modes = rate_ref.shape[0]
    run = half // SUB

    def fetch(i):
        return pltpu.make_async_copy(
            x_hbm.at[0, :, pl.ds(pl.multiple_of((first_strip + i) * width, LANES), width)],
            raw.at[i],
            sems.at[i],
        )

    @pl.when(step_id == 0)
    def _():
        for i in range(raw.shape[0]):
            fetch(i).start()

    rates = rate_ref[...]
    keep_ref[...] = jnp.exp(-rates)
    run_ref[...] = jnp.exp(-rates * run)
    gain_ref[...] = res_ref[...] * jnp.sqrt(2.0 * rates)
    for t, c in enumerate(range(0, width, LANES)):
        cols = slice(c, c + LANES)
        run_keep = run_ref[:, cols]
        state = jnp.zeros((modes, LANES), F32)
        for i in range(SUB):
            state = run_keep * state + modes_at(ends_ref.at[t, 0], i, modes)
        state = jnp.where(part == 0, 0.0, state)
        for i in range(SUB):
            put_modes_at(begins, i, state)
            if i + 1 < SUB:
                state = run_keep * state + modes_at(ends_ref.at[t, part], i, modes)
        keep = [spread(keep_ref, m, cols) for m in range(modes)]
        gains = [spread(gain_ref, m, cols) for m in range(modes)]
        skip = spread(skip_ref, 0, cols)
        states = [begins[m * SUB : (m + 1) * SUB, :] for m in range(modes)]
        for j in range(run):
            now = gate_ref[pl.ds(t * toks + part * half + j, SUB, stride=run), :]
            states = [k * state + now for k, state in zip(keep, states)]
            local_ref[pl.ds(t * half + j, SUB, stride=run), :] = tree_sum(
                [skip * now] + [gain * state for gain, state in zip(gains, states)]
            )

    fetch(step_id).wait()
    start = pl.multiple_of(part * half, half)
    for t, c in enumerate(range(0, width, LANES)):
        cols = slice(c, c + LANES)
        for r in range(0, half, STEP):
            wide[SUB + r : SUB + r + STEP, :] = raw[
                step_id, pl.ds(pl.multiple_of(start + r, STEP), STEP), cols
            ].astype(F32)
        before = raw[step_id, half - 16 : half, cols].astype(F32)[16 - rim :]
        wide[SUB - rim : SUB, :] = before
        taps = tap_rows(taps_ref, 0, cols)
        load = lambda at: wide[pl.ds(SUB + at, SUB, stride=run), :]
        line = [load(at) for at in range(-rim, 0)]
        for j in range(run):
            line = line[-rim:] + [load(j)]
            query_ref[pl.ds(t * half + j, SUB, stride=run), :] = short_conv(line, taps)


def finish_kernel(
    ids, query_ref, local_ref, prefix_ref, past_ref, sum_ref, taps_ref, res_ref, rate_ref, skip_ref,
    out_ref, begins, carry,
):
    part = ids[0]
    modes, width = prefix_ref.shape
    half = out_ref.shape[0]
    run = half // SUB
    row = lax.broadcasted_iota(jnp.int32, (STEP, LANES), 0)

    def tile(t, _):
        cols = pl.ds(pl.multiple_of(t * LANES, LANES), LANES)
        rates = rate_ref[:, cols]
        gains = res_ref[:, cols] * jnp.sqrt(2.0 * rates)
        keep_all = jnp.exp(-rates)
        run_keep = jnp.exp(-rates * run)
        past = past_ref[:, cols]
        here = sum_ref[modes:, cols].astype(F32)
        taps = [[taps_ref[j, s : s + 1, cols] for j in range(3)] for s in range(3)]
        one, two = first_gates((past[2:4], past[4:6]), (here[0:2], here[2:4]), taps[1:])
        line = [past[0:1], past[1:2], here[10:11], here[11:12]]
        queries = [
            taps[0][0] * line[at] + taps[0][1] * line[at - 1] + taps[0][2] * line[at - 2]
            for at in (2, 3)
        ]
        grow = jnp.exp(rates)
        state = gains * (prefix_ref[:, cols] + grow * (one + grow * two))
        state = state * jnp.where(part == 0, keep_all, jnp.exp(-rates * (half + 1)))
        for i in range(SUB):
            put_modes_at(begins, i, state)
            state = run_keep * state
        keep = [jnp.broadcast_to(keep_all[m : m + 1], (SUB, LANES)) for m in range(modes)]
        states = [begins[m * SUB : (m + 1) * SUB, :] for m in range(modes)]
        for j in range(run):
            carry[pl.ds(j, SUB, stride=run), :] = tree_sum(states)
            states = [k * state for k, state in zip(keep, states)]
        skip = skip_ref[:, cols]
        over = jnp.sum(gains * grow, axis=0, keepdims=True)
        for r in range(0, half, STEP):
            rows = pl.ds(pl.multiple_of(t * half + r, STEP), STEP)
            value = query_ref[rows, :] * (local_ref[rows, :] + carry[r : r + STEP, :])
            if r == 0:
                begin = carry[0:SUB, :]
                head = queries[0] * (begin[0:1] - over * two + skip * one)
                second = queries[1] * (begin[1:2] + skip * two)
                value = jnp.where((row == 0) & (part == 0), head, value)
                value = jnp.where((row == 1) & (part == 0), second, value)
            out_ref[r : r + STEP, cols] = value.astype(BF16)
        return 0

    lax.fori_loop(0, width // LANES, tile, 0, unroll=UNROLL)


def place_kernel(ids, far_ref, held_ref, out_ref, sem):
    del held_ref
    width = far_ref.shape[1]
    copy = pltpu.make_async_copy(
        far_ref,
        out_ref.at[:, pl.ds(pl.multiple_of(ids[0] * width, LANES), width)],
        sem,
    )
    copy.start()
    copy.wait()


def exchange(summary, blocks, index, stride, count):
    def route(hop):
        pairs = []
        for i in range(blocks):
            j = i // stride % count
            pairs.append((i, i + ((j + hop(i)) % count - j) * stride))
        return pairs

    def send(value, hop):
        return lax.ppermute(value, "ctx", route(hop))

    if count != 4 or stride % 2:
        return [send(summary, lambda i, k=k: k) for k in range(1, count)]
    beside = send(summary, lambda i: 3 if i % 2 else 1)
    across = send(summary, lambda i: 2)
    other = lax.ppermute(beside, "ctx", [(i, i ^ 1) for i in range(blocks)])
    return [beside, across, other]


def scan_counts(blocks):
    counts = [2] if blocks % 2 == 0 else []
    left = blocks // 2 if counts else blocks
    while left % 4 == 0:
        counts.append(4)
        left //= 4
    if left > 1:
        counts.append(left)
    return counts


def shards(streams, short_filter, residue, decay_rate, skip_gain):
    ctx_count = lax.axis_size("ctx")
    index = lax.axis_index("ctx")
    side = lax.axis_index("chan").astype(jnp.int32).reshape(1)
    toks, _, width = streams.shape
    half = toks // 2
    modes = residue.shape[1]
    rim = short_filter.shape[0] - 1
    tile = 256 if width % 256 == 0 else LANES
    steps = width // tile
    tiles = tile // LANES
    all_tiles = width // LANES
    wide_tile = 512 if width % 512 == 0 else tile
    wide_steps = width // wide_tile
    wide_tiles = wide_tile // LANES

    x = jnp.transpose(streams, (1, 0, 2))
    rates = decay_rate.T
    weights = residue.T
    skip = skip_gain[None, :]
    x_kept, taps_kept, rates_kept = (
        pltpu.with_memory_space_constraint(a, pltpu.HBM) for a in (x, short_filter, rates)
    )
    params = pltpu.CompilerParams(vmem_limit_bytes=VMEM_LIMIT)
    in_hbm = pl.BlockSpec(memory_space=pltpu.HBM)
    strip = lambda *lead: pl.BlockSpec(lead + (tile,), lambda i, *_: (0,) * len(lead) + (i,))
    tall = lambda rows: pl.BlockSpec((tiles * rows, LANES), lambda i, *_: (i, 0))
    ends_spec = pl.BlockSpec((tiles, 2, modes * SUB, LANES), lambda i, *_: (i, 0, 0, 0))
    gate, ends, state, summary = pl.pallas_call(
        state_kernel,
        grid=(wide_steps,),
        in_specs=[in_hbm] * 3,
        out_specs=[
            pl.BlockSpec((wide_tiles * toks, LANES), lambda i: (i, 0)),
            pl.BlockSpec((wide_tiles, 2, modes * SUB, LANES), lambda i: (i, 0, 0, 0)),
            pl.BlockSpec((modes, wide_tile), lambda i: (0, i)),
            pl.BlockSpec((modes + PAIR, wide_tile), lambda i: (0, i)),
        ],
        out_shape=[
            jax.ShapeDtypeStruct((all_tiles * toks, LANES), F32),
            jax.ShapeDtypeStruct((all_tiles, 2, modes * SUB, LANES), F32),
            jax.ShapeDtypeStruct((modes, width), F32),
            jax.ShapeDtypeStruct((modes + PAIR, width), BF16),
        ],
        scratch_shapes=[
            pltpu.VMEM((wide_steps, 2, toks, wide_tile), BF16),
            pltpu.VMEM((wide_steps, 2, PAIR, wide_tile), BF16),
            pltpu.VMEM((2, toks + SUB, LANES), F32),
            pltpu.VMEM((modes, wide_tile), F32),
            pltpu.VMEM((modes, wide_tile), F32),
            pltpu.VMEM((rim + 1, 3, width), F32),
            pltpu.VMEM((modes, width), F32),
            pltpu.SemaphoreType.DMA((3, wide_steps)),
            pltpu.SemaphoreType.DMA((2,)),
        ],
        compiler_params=params,
        name="states",
    )(x_kept, taps_kept, rates_kept)

    def shifted(first, *lead):
        return pl.BlockSpec(lead + (tile,), lambda i, *_: (0,) * len(lead) + (first + i,))

    def local(which, gate, first, count, held, name):
        return pl.pallas_call(
            functools.partial(local_kernel, first),
            grid_spec=pltpu.PrefetchScalarGridSpec(
                num_scalar_prefetch=1,
                grid=(count,),
                in_specs=[
                    in_hbm,
                    shifted(first, rim + 1, 3),
                    pl.BlockSpec((tiles * toks, LANES), lambda i, *_: (first + i, 0)),
                    pl.BlockSpec(
                        (tiles, 2, modes * SUB, LANES), lambda i, *_: (first + i, 0, 0, 0)
                    ),
                    shifted(first, modes),
                    shifted(first, modes),
                    shifted(first, 1),
                ]
                + [pl.BlockSpec(memory_space=pl.ANY)] * len(held),
                out_specs=[pl.BlockSpec((tiles * half, LANES), lambda i, *_: (first + i, 0))] * 2,
                scratch_shapes=[
                    pltpu.VMEM((count, toks, tile), BF16),
                    pltpu.VMEM((half + SUB, LANES), F32),
                    pltpu.VMEM((modes * SUB, LANES), F32),
                    pltpu.VMEM((modes, tile), F32),
                    pltpu.VMEM((modes, tile), F32),
                    pltpu.VMEM((modes, tile), F32),
                    pltpu.SemaphoreType.DMA((count,)),
                ],
            ),
            out_shape=[jax.ShapeDtypeStruct((all_tiles * half, LANES), F32)] * 2,
            input_output_aliases={8: 0, 9: 1} if held else {},
            compiler_params=params,
            name=name,
        )(which, x_kept, short_filter, gate, ends, weights, rates, skip, *held)

    few = steps // 2
    locals_sent = ()
    ids = index.astype(jnp.int32).reshape(1)
    in_vmem = pl.BlockSpec(memory_space=pltpu.VMEM)
    prefix = jnp.zeros((modes, width), F32)
    past = jnp.zeros((SUB, width), F32)
    own = summary
    stride = 1
    counts = scan_counts(ctx_count)
    for level, count in enumerate(counts):
        last = level == len(counts) - 1
        arrived = exchange(summary, ctx_count, index, stride, count)
        if level >= 2:
            gate, arrived[0] = lax.optimization_barrier((gate, arrived[0]))
            first = 0 if level == 2 else few
            locals_sent = local(1 - side, gate, first, few, locals_sent, f"local_sent_{level}")
            locals_sent, arrived = lax.optimization_barrier((locals_sent, arrived))
        shapes = [
            jax.ShapeDtypeStruct((modes, width), F32),
            jax.ShapeDtypeStruct((SUB, width), F32),
        ]
        if not last:
            shapes += [
                jax.ShapeDtypeStruct((modes, width), F32),
                jax.ShapeDtypeStruct((modes + PAIR, width), BF16),
            ]

        def body(ids, *refs, stride=stride, count=count, last=last):
            join_kernel(ids, stride, count, toks, last, *refs)

        results = pl.pallas_call(
            body,
            in_specs=[pl.BlockSpec(memory_space=pltpu.SMEM)] + [in_vmem] * (5 + count),
            out_specs=[in_vmem] * len(shapes),
            out_shape=shapes,
            compiler_params=params,
            name=f"join_{level}",
        )(ids, short_filter, rates, state, prefix, past, summary, *arrived)
        prefix, past = results[:2]
        if not last:
            state, summary = results[2:]
        stride *= count

    def finish(which, column, columns, locals_, prefix, name):
        return pl.pallas_call(
            finish_kernel,
            grid_spec=pltpu.PrefetchScalarGridSpec(
                num_scalar_prefetch=1,
                grid=(steps,),
                in_specs=[
                    tall(half),
                    tall(half),
                    strip(modes),
                    strip(SUB),
                    strip(modes + PAIR),
                    strip(rim + 1, 3),
                    strip(modes),
                    strip(modes),
                    strip(1),
                ],
                out_specs=pl.BlockSpec((half, tile), lambda i, ids: (0, ids[1] * steps + i)),
                scratch_shapes=[
                    pltpu.VMEM((modes * SUB, LANES), F32),
                    pltpu.VMEM((half, LANES), F32),
                ],
            ),
            out_shape=jax.ShapeDtypeStruct((half, columns), BF16),
            compiler_params=params,
            name=name,
        )(
            jnp.concatenate([which, column]),
            *locals_,
            prefix,
            past,
            own,
            short_filter,
            weights,
            rates,
            skip,
        )

    sent = pl.pallas_call(
        finish_kernel,
        in_specs=[pl.BlockSpec(memory_space=pltpu.SMEM)] + [in_vmem] * 9,
        out_specs=in_vmem,
        out_shape=jax.ShapeDtypeStruct((half, width), BF16),
        scratch_shapes=[pltpu.VMEM((modes * SUB, LANES), F32), pltpu.VMEM((half, LANES), F32)],
        compiler_params=params,
        name="finish_sent",
    )(1 - side, *locals_sent, prefix, past, own, short_filter, weights, rates, skip)
    far = lax.ppermute(sent, "chan", [(0, 1), (1, 0)])
    prefix, gate, sent = lax.optimization_barrier((prefix, gate, sent))
    locals_own = local(side, gate, 0, steps, (), "local_own")
    held = finish(side, side, 2 * width, locals_own, prefix, "finish_own")
    return pl.pallas_call(
        place_kernel,
        grid_spec=pltpu.PrefetchScalarGridSpec(
            num_scalar_prefetch=1,
            grid=(1,),
            in_specs=[pl.BlockSpec(memory_space=pl.ANY)] * 2,
            out_specs=pl.BlockSpec(memory_space=pl.ANY),
            scratch_shapes=[pltpu.SemaphoreType.DMA(())],
        ),
        out_shape=jax.ShapeDtypeStruct((half, 2 * width), BF16),
        input_output_aliases={2: 0},
        compiler_params=params,
        name="place",
    )(1 - side, far, held)


def solution(mesh):
    return jax.shard_map(
        shards,
        mesh=mesh,
        in_specs=(
            P("ctx", None, "chan"),
            P(None, None, "chan"),
            P("chan", None),
            P("chan", None),
            P("chan"),
        ),
        out_specs=P(("ctx", "chan"), None),
        check_vma=False,
    )
```

```python
import functools

import jax
import jax.numpy as jnp
from jax import lax
from jax.experimental import pallas as pl
from jax.experimental.pallas import tpu as pltpu
from jax.sharding import PartitionSpec as P

LANES = 128
SUB = 8
UNROLL = 8
STEP = 32
PAIR = 16
F32 = jnp.float32
BF16 = jnp.bfloat16
VMEM_LIMIT = 16 * 1024 * 1024


def spread(ref, m, cols):
    return jnp.broadcast_to(ref[m : m + 1, cols], (SUB, LANES))


def tree_sum(terms):
    terms = list(terms)
    while len(terms) > 1:
        terms = [
            terms[i] + terms[i + 1] if i + 1 < len(terms) else terms[i]
            for i in range(0, len(terms), 2)
        ]
    return terms[0]


def short_conv(line, taps):
    total = taps[0] * line[-1]
    for k in range(1, len(taps)):
        total = total + taps[k] * line[-1 - k]
    return total


def tap_rows(taps_ref, s, cols):
    return [
        jnp.broadcast_to(taps_ref[j, s : s + 1, cols], (SUB, LANES))
        for j in range(taps_ref.shape[0])
    ]


def modes_at(ref, i, modes):
    return jnp.concatenate(
        [ref[pl.ds(i + SUB * m, SUB, stride=SUB), :] for m in range(0, modes, SUB)], axis=0
    )


def put_modes_at(ref, i, value):
    for m in range(0, value.shape[0], SUB):
        ref[pl.ds(i + SUB * m, SUB, stride=SUB), :] = value[m : m + SUB]


def state_kernel(
    x_hbm, taps_hbm, rate_hbm,
    gate_ref, ends_ref, state_ref, sum_ref,
    raw, raw_query, wide, keep_ref, run_ref, taps_all, rate_all, sems, small_sems,
):
    step_id = pl.program_id(0)
    _, _, toks, width = raw.shape
    half = toks // 2
    rim = taps_all.shape[0] - 1
    modes = rate_all.shape[0]
    run = half // SUB

    def fetches(i):
        cols = pl.ds(pl.multiple_of(i * width, LANES), width)
        return (
            pltpu.make_async_copy(x_hbm.at[pl.ds(1, 2), :, cols], raw.at[i], sems.at[0, i]),
            pltpu.make_async_copy(
                x_hbm.at[0, pl.ds(0, PAIR), cols], raw_query.at[i, 0], sems.at[1, i]
            ),
            pltpu.make_async_copy(
                x_hbm.at[0, pl.ds(toks - PAIR, PAIR), cols], raw_query.at[i, 1], sems.at[2, i]
            ),
        )

    small = (
        pltpu.make_async_copy(taps_hbm, taps_all, small_sems.at[0]),
        pltpu.make_async_copy(rate_hbm, rate_all, small_sems.at[1]),
    )

    @pl.when(step_id == 0)
    def _():
        for copy in small:
            copy.start()
        for i in range(raw.shape[0]):
            for copy in fetches(i):
                copy.start()
        for copy in small:
            copy.wait()

    strip = pl.ds(pl.multiple_of(step_id * width, LANES), width)
    taps_ref = taps_all.at[:, :, strip]
    rates = rate_all[:, strip]
    keep_ref[...] = jnp.exp(-rates)
    run_ref[...] = jnp.exp(-rates * run)
    for copy in fetches(step_id):
        copy.wait()
    index = lax.broadcasted_iota(jnp.int32, (SUB, LANES), 0)
    for t, c in enumerate(range(0, width, LANES)):
        cols = slice(c, c + LANES)
        for s in range(2):
            wide[s, :SUB, :] = jnp.zeros((SUB, LANES), F32)
            for r in range(0, toks, STEP):
                wide[s, SUB + r : SUB + r + STEP, :] = raw[
                    step_id, s, r : r + STEP, cols
                ].astype(F32)
        key_taps = tap_rows(taps_ref, 1, cols)
        value_taps = tap_rows(taps_ref, 2, cols)
        keep = [spread(keep_ref, m, cols) for m in range(modes)]
        total = None
        for part in range(2):
            base = part * half
            states = None
            load = lambda s, at: wide[s, pl.ds(SUB + base + at, SUB, stride=run), :]
            lines = [[load(s, at) for at in range(-rim, 0)] for s in range(2)]
            for j in range(run):
                lines = [line[-rim:] + [load(s, j)] for s, line in enumerate(lines)]
                gate = short_conv(lines[0], key_taps) * short_conv(lines[1], value_taps)
                if part == 0 and j < rim:
                    gate = jnp.where(index == 0, 0.0, gate)
                gate_ref[pl.ds(t * toks + base + j, SUB, stride=run), :] = gate
                if states is None:
                    states = [gate] * modes
                else:
                    states = [k * state + gate for k, state in zip(keep, states)]
            for m, end in enumerate(states):
                ends_ref[t, part, m * SUB : (m + 1) * SUB, :] = end
            run_keep = run_ref[:, cols]
            for i in range(SUB):
                end = modes_at(ends_ref.at[t, part], i, modes)
                total = end if total is None else run_keep * total + end
        state_ref[:, cols] = total
        sum_ref[:modes, cols] = total.astype(BF16)
        query = raw_query[step_id, :, :, cols].astype(F32)
        sum_ref[modes:, cols] = jnp.concatenate(
            [
                wide[0, SUB : SUB + rim, :],
                wide[1, SUB : SUB + rim, :],
                query[1, PAIR - rim :],
                wide[0, SUB + toks - rim : SUB + toks, :],
                wide[1, SUB + toks - rim : SUB + toks, :],
                query[0, :rim],
                jnp.zeros((PAIR - 6 * rim, LANES), F32),
            ],
            axis=0,
        ).astype(BF16)


def first_gates(past, first, taps):
    rows = []
    for s in range(2):
        before, here = past[s], first[s]
        line = [before[0:1], before[1:2], here[0:1], here[1:2]]
        rows.append(
            [
                taps[s][0] * line[at] + taps[s][1] * line[at - 1] + taps[s][2] * line[at - 2]
                for at in (2, 3)
            ]
        )
    return [key * value for key, value in zip(*rows)]


def join_kernel(ids, stride, count, toks, last, *refs):
    taps_ref, rate_ref, state_ref, prefix_ref, past_ref, own_ref = refs[:6]
    near = (own_ref,) + refs[6 : 5 + count]
    shared = count == 4 and stride % 2 == 0
    outs = refs[5 + count :]
    prefix_out, past_out = outs[:2]
    modes, width = rate_ref.shape
    index = ids[0]
    place = lax.rem(lax.div(index, stride), count)
    behind = lax.rem(index, stride)
    origins = [lax.rem(place - k + count, count) for k in range(count)]
    as_float = lambda n: n.astype(F32)

    def tile(t, _):
        cols = pl.ds(pl.multiple_of(t * LANES, LANES), LANES)
        rates = rate_ref[:, cols]
        span = rates * float(toks)
        taps = [[taps_ref[j, s : s + 1, cols] for j in range(3)] for s in (1, 2)]
        full = [ref[:, cols].astype(F32) for ref in near]
        if shared:
            odd = lax.rem(index, 2) == 1
            full[1], full[3] = jnp.where(odd, full[3], full[1]), jnp.where(odd, full[1], full[3])
        extra = [value[modes:] for value in full]
        firsts = [(e[0:2], e[2:4]) for e in extra]
        states = [state_ref[:, cols]] + [value[:modes] for value in full[1:]]
        keep = jnp.exp(-rates)
        second_keep = jnp.exp(-rates * float(toks - 2))
        first_keep = second_keep * keep
        block_keep = first_keep * keep
        rest = jnp.exp(-span * float(stride - 1)) if stride > 1 else 1.0
        run_keep = rest * block_keep
        powers = [1.0, run_keep]
        while len(powers) < count:
            powers.append(powers[-1] * run_keep)
        before = jnp.exp(-span * as_float(jnp.maximum(behind - 1, 0)))
        joins = []
        for k in range(count):
            linked = origins[k] >= 1
            past = extra[(k + 1) % count][4:10]
            past = jnp.where(linked, past, 0.0)
            one, two = first_gates((past[2:4], past[4:6]), firsts[k], taps)
            join = first_keep * one + second_keep * two
            if not last:
                join = jnp.where(linked, join, 0.0)
            joins.append(join)
            states[k] = states[k] + rest * join
        passed = jnp.where(behind >= 1, before * block_keep, 1.0)
        prefix = prefix_ref[:, cols] + jnp.where(behind >= 1, before * joins[0], 0.0)
        for k in range(1, count):
            prefix = prefix + jnp.where(place >= k, passed * powers[k - 1] * states[k], 0.0)
        prefix_out[:, cols] = prefix
        past = jnp.where((place >= 1) & (behind == 0), extra[1][4:10], past_ref[0:6, cols])
        past_out[:, cols] = jnp.concatenate([past, jnp.zeros((SUB - 6, LANES), F32)], axis=0)
        if not last:
            state_out, sum_out = outs[2:]
            total = None
            for k in range(count):
                factor = jnp.ones_like(run_keep)
                for gap in range(1, count):
                    factor = jnp.where(origins[k] == count - 1 - gap, powers[gap], factor)
                term = factor * states[k]
                total = term if total is None else total + term
            state_out[:, cols] = total
            first = extra[0]
            end = extra[0]
            for k in range(1, count):
                first = jnp.where(origins[k] == 0, extra[k], first)
                end = jnp.where(origins[k] == count - 1, extra[k], end)
            sum_out[:modes, cols] = total.astype(BF16)
            sum_out[modes:, cols] = jnp.concatenate([first[0:4], end[4:]], axis=0).astype(BF16)
        return 0

    lax.fori_loop(0, width // LANES, tile, 0, unroll=UNROLL)


def local_kernel(
    first, part_id, x_hbm, taps_ref, gate_ref, ends_ref, res_ref, rate_ref, skip_ref, *refs
):
    query_ref, local_ref, raw, wide, begins, sem = refs[-6:]
    part = part_id[0]
    toks, width = raw.shape
    half = toks // 2
    rim = taps_ref.shape[0] - 1
    modes = rate_ref.shape[0]
    run = half // SUB
    start = pl.multiple_of(part * half, half)
    fetch = pltpu.make_async_copy(x_hbm.at[0, :, first : first + width], raw, sem)
    fetch.start()
    for t in range(width // LANES):
        at = first // LANES + t
        cols = slice(at * LANES, (at + 1) * LANES)
        rates = rate_ref[:, cols]
        keep_all = jnp.exp(-rates)
        run_keep = jnp.exp(-rates * run)
        gains = res_ref[:, cols] * jnp.sqrt(2.0 * rates)
        state = jnp.zeros((modes, LANES), F32)
        for i in range(SUB):
            state = run_keep * state + modes_at(ends_ref.at[at, 0], i, modes)
        state = jnp.where(part == 0, 0.0, state)
        for i in range(SUB):
            put_modes_at(begins.at[t], i, state)
            if i + 1 < SUB:
                state = run_keep * state + modes_at(ends_ref.at[at, part], i, modes)
        keep = [jnp.broadcast_to(keep_all[m : m + 1], (SUB, LANES)) for m in range(modes)]
        gain = [jnp.broadcast_to(gains[m : m + 1], (SUB, LANES)) for m in range(modes)]
        skip = spread(skip_ref, 0, cols)
        states = [begins[t, m * SUB : (m + 1) * SUB, :] for m in range(modes)]
        for j in range(run):
            now = gate_ref[pl.ds(at * toks + part * half + j, SUB, stride=run), :]
            states = [k * state + now for k, state in zip(keep, states)]
            local_ref[pl.ds(at * half + j, SUB, stride=run), :] = tree_sum(
                [skip * now] + [g * state for g, state in zip(gain, states)]
            )
    fetch.wait()
    for t in range(width // LANES):
        at = first // LANES + t
        near = slice(t * LANES, (t + 1) * LANES)
        for r in range(0, half, STEP):
            wide[t, SUB + r : SUB + r + STEP, :] = raw[
                pl.ds(pl.multiple_of(start + r, STEP), STEP), near
            ].astype(F32)
        wide[t, SUB - rim : SUB, :] = raw[half - PAIR : half, near].astype(F32)[PAIR - rim :]
        taps = tap_rows(taps_ref, 0, slice(at * LANES, (at + 1) * LANES))
        load = lambda j: wide[t, pl.ds(SUB + j, SUB, stride=run), :]
        line = [load(j) for j in range(-rim, 0)]
        for j in range(run):
            line = line[-rim:] + [load(j)]
            query_ref[pl.ds(at * half + j, SUB, stride=run), :] = short_conv(line, taps)


def finish_kernel(
    ids, query_ref, local_ref, prefix_ref, past_ref, sum_ref, taps_ref, res_ref, rate_ref, skip_ref,
    out_ref, begins, carry,
):
    part = ids[0]
    modes, width = prefix_ref.shape
    half = out_ref.shape[0]
    run = half // SUB
    row = lax.broadcasted_iota(jnp.int32, (STEP, LANES), 0)

    def tile(t, _):
        cols = pl.ds(pl.multiple_of(t * LANES, LANES), LANES)
        rates = rate_ref[:, cols]
        gains = res_ref[:, cols] * jnp.sqrt(2.0 * rates)
        keep_all = jnp.exp(-rates)
        run_keep = jnp.exp(-rates * run)
        past = past_ref[:, cols]
        here = sum_ref[modes:, cols].astype(F32)
        taps = [[taps_ref[j, s : s + 1, cols] for j in range(3)] for s in range(3)]
        one, two = first_gates((past[2:4], past[4:6]), (here[0:2], here[2:4]), taps[1:])
        line = [past[0:1], past[1:2], here[10:11], here[11:12]]
        queries = [
            taps[0][0] * line[at] + taps[0][1] * line[at - 1] + taps[0][2] * line[at - 2]
            for at in (2, 3)
        ]
        grow = jnp.exp(rates)
        state = gains * (prefix_ref[:, cols] + grow * (one + grow * two))
        state = state * jnp.where(part == 0, keep_all, jnp.exp(-rates * (half + 1)))
        for i in range(SUB):
            put_modes_at(begins, i, state)
            state = run_keep * state
        keep = [jnp.broadcast_to(keep_all[m : m + 1], (SUB, LANES)) for m in range(modes)]
        states = [begins[m * SUB : (m + 1) * SUB, :] for m in range(modes)]
        for j in range(run):
            carry[pl.ds(j, SUB, stride=run), :] = tree_sum(states)
            states = [k * state for k, state in zip(keep, states)]
        skip = skip_ref[:, cols]
        over = jnp.sum(gains * grow, axis=0, keepdims=True)
        for r in range(0, half, STEP):
            rows = pl.ds(pl.multiple_of(t * half + r, STEP), STEP)
            value = query_ref[rows, :] * (local_ref[rows, :] + carry[r : r + STEP, :])
            if r == 0:
                begin = carry[0:SUB, :]
                head = queries[0] * (begin[0:1] - over * two + skip * one)
                second = queries[1] * (begin[1:2] + skip * two)
                value = jnp.where((row == 0) & (part == 0), head, value)
                value = jnp.where((row == 1) & (part == 0), second, value)
            out_ref[r : r + STEP, cols] = value.astype(BF16)
        return 0

    lax.fori_loop(0, width // LANES, tile, 0, unroll=UNROLL)


def place_kernel(ids, far_ref, held_ref, out_ref, sem):
    del held_ref
    width = far_ref.shape[1]
    copy = pltpu.make_async_copy(
        far_ref,
        out_ref.at[:, pl.ds(pl.multiple_of(ids[0] * width, LANES), width)],
        sem,
    )
    copy.start()
    copy.wait()


def exchange(summary, blocks, index, stride, count):
    def route(hop):
        pairs = []
        for i in range(blocks):
            j = i // stride % count
            pairs.append((i, i + ((j + hop(i)) % count - j) * stride))
        return pairs

    def send(value, hop):
        return lax.ppermute(value, "ctx", route(hop))

    if count != 4 or stride % 2:
        return [send(summary, lambda i, k=k: k) for k in range(1, count)]
    beside = send(summary, lambda i: 3 if i % 2 else 1)
    across = send(summary, lambda i: 2)
    other = lax.ppermute(beside, "ctx", [(i, i ^ 1) for i in range(blocks)])
    return [beside, across, other]


def scan_counts(blocks):
    counts = [2] if blocks % 2 == 0 else []
    left = blocks // 2 if counts else blocks
    while left % 4 == 0:
        counts.append(4)
        left //= 4
    if left > 1:
        counts.append(left)
    return counts


def shards(streams, short_filter, residue, decay_rate, skip_gain):
    ctx_count = lax.axis_size("ctx")
    index = lax.axis_index("ctx")
    side = lax.axis_index("chan").astype(jnp.int32).reshape(1)
    toks, _, width = streams.shape
    half = toks // 2
    modes = residue.shape[1]
    rim = short_filter.shape[0] - 1
    tile = 256 if width % 256 == 0 else LANES
    steps = width // tile
    tiles = tile // LANES
    all_tiles = width // LANES
    wide_tile = 512 if width % 512 == 0 else tile
    wide_steps = width // wide_tile
    wide_tiles = wide_tile // LANES

    x = jnp.transpose(streams, (1, 0, 2))
    rates = decay_rate.T
    weights = residue.T
    skip = skip_gain[None, :]
    x_kept, taps_kept, rates_kept = (
        pltpu.with_memory_space_constraint(a, pltpu.HBM) for a in (x, short_filter, rates)
    )
    params = pltpu.CompilerParams(vmem_limit_bytes=VMEM_LIMIT)
    in_hbm = pl.BlockSpec(memory_space=pltpu.HBM)
    strip = lambda *lead: pl.BlockSpec(lead + (tile,), lambda i, *_: (0,) * len(lead) + (i,))
    tall = lambda rows: pl.BlockSpec((tiles * rows, LANES), lambda i, *_: (i, 0))
    ends_spec = pl.BlockSpec((tiles, 2, modes * SUB, LANES), lambda i, *_: (i, 0, 0, 0))
    gate, ends, state, summary = pl.pallas_call(
        state_kernel,
        grid=(wide_steps,),
        in_specs=[in_hbm] * 3,
        out_specs=[
            pl.BlockSpec((wide_tiles * toks, LANES), lambda i: (i, 0)),
            pl.BlockSpec((wide_tiles, 2, modes * SUB, LANES), lambda i: (i, 0, 0, 0)),
            pl.BlockSpec((modes, wide_tile), lambda i: (0, i)),
            pl.BlockSpec((modes + PAIR, wide_tile), lambda i: (0, i)),
        ],
        out_shape=[
            jax.ShapeDtypeStruct((all_tiles * toks, LANES), F32),
            jax.ShapeDtypeStruct((all_tiles, 2, modes * SUB, LANES), F32),
            jax.ShapeDtypeStruct((modes, width), F32),
            jax.ShapeDtypeStruct((modes + PAIR, width), BF16),
        ],
        scratch_shapes=[
            pltpu.VMEM((wide_steps, 2, toks, wide_tile), BF16),
            pltpu.VMEM((wide_steps, 2, PAIR, wide_tile), BF16),
            pltpu.VMEM((2, toks + SUB, LANES), F32),
            pltpu.VMEM((modes, wide_tile), F32),
            pltpu.VMEM((modes, wide_tile), F32),
            pltpu.VMEM((rim + 1, 3, width), F32),
            pltpu.VMEM((modes, width), F32),
            pltpu.SemaphoreType.DMA((3, wide_steps)),
            pltpu.SemaphoreType.DMA((2,)),
        ],
        compiler_params=params,
        name="states",
    )(x_kept, taps_kept, rates_kept)

    def shifted(first, *lead):
        return pl.BlockSpec(lead + (tile,), lambda i, *_: (0,) * len(lead) + (first + i,))

    in_vmem = pl.BlockSpec(memory_space=pltpu.VMEM)

    def local(which, gate, first, count, held, name):
        return pl.pallas_call(
            functools.partial(local_kernel, first * tile),
            in_specs=[pl.BlockSpec(memory_space=pltpu.SMEM), in_hbm]
            + [in_vmem] * (6 + len(held)),
            out_specs=[in_vmem] * 2,
            out_shape=[jax.ShapeDtypeStruct((all_tiles * half, LANES), F32)] * 2,
            scratch_shapes=[
                pltpu.VMEM((toks, count * tile), BF16),
                pltpu.VMEM((count * tiles, half + SUB, LANES), F32),
                pltpu.VMEM((count * tiles, modes * SUB, LANES), F32),
                pltpu.SemaphoreType.DMA(()),
            ],
            input_output_aliases={8: 0, 9: 1} if held else {},
            compiler_params=params,
            name=name,
        )(which, x_kept, short_filter, gate, ends, weights, rates, skip, *held)

    few = steps // 2
    locals_sent = ()
    ids = index.astype(jnp.int32).reshape(1)
    prefix = jnp.zeros((modes, width), F32)
    past = jnp.zeros((SUB, width), F32)
    own = summary
    stride = 1
    counts = scan_counts(ctx_count)
    for level, count in enumerate(counts):
        last = level == len(counts) - 1
        arrived = exchange(summary, ctx_count, index, stride, count)
        if level >= 2:
            gate, arrived[0] = lax.optimization_barrier((gate, arrived[0]))
            first = 0 if level == 2 else few
            locals_sent = local(1 - side, gate, first, few, locals_sent, f"local_sent_{level}")
            locals_sent, arrived = lax.optimization_barrier((locals_sent, arrived))
        shapes = [
            jax.ShapeDtypeStruct((modes, width), F32),
            jax.ShapeDtypeStruct((SUB, width), F32),
        ]
        if not last:
            shapes += [
                jax.ShapeDtypeStruct((modes, width), F32),
                jax.ShapeDtypeStruct((modes + PAIR, width), BF16),
            ]

        def body(ids, *refs, stride=stride, count=count, last=last):
            join_kernel(ids, stride, count, toks, last, *refs)

        results = pl.pallas_call(
            body,
            in_specs=[pl.BlockSpec(memory_space=pltpu.SMEM)] + [in_vmem] * (5 + count),
            out_specs=[in_vmem] * len(shapes),
            out_shape=shapes,
            compiler_params=params,
            name=f"join_{level}",
        )(ids, short_filter, rates, state, prefix, past, summary, *arrived)
        prefix, past = results[:2]
        if not last:
            state, summary = results[2:]
        stride *= count

    def finish(which, column, columns, locals_, prefix, name):
        return pl.pallas_call(
            finish_kernel,
            grid_spec=pltpu.PrefetchScalarGridSpec(
                num_scalar_prefetch=1,
                grid=(steps,),
                in_specs=[
                    tall(half),
                    tall(half),
                    strip(modes),
                    strip(SUB),
                    strip(modes + PAIR),
                    strip(rim + 1, 3),
                    strip(modes),
                    strip(modes),
                    strip(1),
                ],
                out_specs=pl.BlockSpec((half, tile), lambda i, ids: (0, ids[1] * steps + i)),
                scratch_shapes=[
                    pltpu.VMEM((modes * SUB, LANES), F32),
                    pltpu.VMEM((half, LANES), F32),
                ],
            ),
            out_shape=jax.ShapeDtypeStruct((half, columns), BF16),
            compiler_params=params,
            name=name,
        )(
            jnp.concatenate([which, column]),
            *locals_,
            prefix,
            past,
            own,
            short_filter,
            weights,
            rates,
            skip,
        )

    sent = pl.pallas_call(
        finish_kernel,
        in_specs=[pl.BlockSpec(memory_space=pltpu.SMEM)] + [in_vmem] * 9,
        out_specs=in_vmem,
        out_shape=jax.ShapeDtypeStruct((half, width), BF16),
        scratch_shapes=[pltpu.VMEM((modes * SUB, LANES), F32), pltpu.VMEM((half, LANES), F32)],
        compiler_params=params,
        name="finish_sent",
    )(1 - side, *locals_sent, prefix, past, own, short_filter, weights, rates, skip)
    far = lax.ppermute(sent, "chan", [(0, 1), (1, 0)])
    prefix, gate, sent = lax.optimization_barrier((prefix, gate, sent))
    locals_own = local(side, gate, 0, steps, (), "local_own")
    held = finish(side, side, 2 * width, locals_own, prefix, "finish_own")
    return pl.pallas_call(
        place_kernel,
        grid_spec=pltpu.PrefetchScalarGridSpec(
            num_scalar_prefetch=1,
            grid=(1,),
            in_specs=[pl.BlockSpec(memory_space=pl.ANY)] * 2,
            out_specs=pl.BlockSpec(memory_space=pl.ANY),
            scratch_shapes=[pltpu.SemaphoreType.DMA(())],
        ),
        out_shape=jax.ShapeDtypeStruct((half, 2 * width), BF16),
        input_output_aliases={2: 0},
        compiler_params=params,
        name="place",
    )(1 - side, far, held)


def solution(mesh):
    return jax.shard_map(
        shards,
        mesh=mesh,
        in_specs=(
            P("ctx", None, "chan"),
            P(None, None, "chan"),
            P("chan", None),
            P("chan", None),
            P("chan"),
        ),
        out_specs=P(("ctx", "chan"), None),
        check_vma=False,
    )
```

```python
import functools

import jax
import jax.numpy as jnp
from jax import lax
from jax.experimental import pallas as pl
from jax.experimental.pallas import tpu as pltpu
from jax.sharding import PartitionSpec as P

LANES = 128
SUB = 8
UNROLL = 8
STEP = 32
PAIR = 16
F32 = jnp.float32
BF16 = jnp.bfloat16
VMEM_LIMIT = 16 * 1024 * 1024


def spread(ref, m, cols):
    return jnp.broadcast_to(ref[m : m + 1, cols], (SUB, LANES))


def tree_sum(terms):
    terms = list(terms)
    while len(terms) > 1:
        terms = [
            terms[i] + terms[i + 1] if i + 1 < len(terms) else terms[i]
            for i in range(0, len(terms), 2)
        ]
    return terms[0]


def short_conv(line, taps):
    total = taps[0] * line[-1]
    for k in range(1, len(taps)):
        total = total + taps[k] * line[-1 - k]
    return total


def tap_rows(taps_ref, s, cols):
    return [
        jnp.broadcast_to(taps_ref[j, s : s + 1, cols], (SUB, LANES))
        for j in range(taps_ref.shape[0])
    ]


def modes_at(ref, i, modes):
    return jnp.concatenate(
        [ref[pl.ds(i + SUB * m, SUB, stride=SUB), :] for m in range(0, modes, SUB)], axis=0
    )


def put_modes_at(ref, i, value):
    for m in range(0, value.shape[0], SUB):
        ref[pl.ds(i + SUB * m, SUB, stride=SUB), :] = value[m : m + SUB]


def state_kernel(
    x_hbm, taps_hbm, rate_hbm,
    gate_ref, ends_ref, state_ref, sum_ref,
    raw, raw_query, wide, keep_ref, run_ref, taps_all, rate_all, sems, small_sems,
):
    step_id = pl.program_id(0)
    _, _, toks, width = raw.shape
    half = toks // 2
    rim = taps_all.shape[0] - 1
    modes = rate_all.shape[0]
    run = half // SUB

    def fetches(i):
        cols = pl.ds(pl.multiple_of(i * width, LANES), width)
        return (
            pltpu.make_async_copy(x_hbm.at[pl.ds(1, 2), :, cols], raw.at[i], sems.at[0, i]),
            pltpu.make_async_copy(
                x_hbm.at[0, pl.ds(0, PAIR), cols], raw_query.at[i, 0], sems.at[1, i]
            ),
            pltpu.make_async_copy(
                x_hbm.at[0, pl.ds(toks - PAIR, PAIR), cols], raw_query.at[i, 1], sems.at[2, i]
            ),
        )

    small = (
        pltpu.make_async_copy(taps_hbm, taps_all, small_sems.at[0]),
        pltpu.make_async_copy(rate_hbm, rate_all, small_sems.at[1]),
    )

    @pl.when(step_id == 0)
    def _():
        for copy in small:
            copy.start()
        for i in range(raw.shape[0]):
            for copy in fetches(i):
                copy.start()
        for copy in small:
            copy.wait()

    strip = pl.ds(pl.multiple_of(step_id * width, LANES), width)
    taps_ref = taps_all.at[:, :, strip]
    rates = rate_all[:, strip]
    keep_ref[...] = jnp.exp(-rates)
    run_ref[...] = jnp.exp(-rates * run)
    for copy in fetches(step_id):
        copy.wait()
    index = lax.broadcasted_iota(jnp.int32, (SUB, LANES), 0)
    for t, c in enumerate(range(0, width, LANES)):
        cols = slice(c, c + LANES)
        for s in range(2):
            wide[s, :SUB, :] = jnp.zeros((SUB, LANES), F32)
            for r in range(0, toks, STEP):
                wide[s, SUB + r : SUB + r + STEP, :] = raw[
                    step_id, s, r : r + STEP, cols
                ].astype(F32)
        key_taps = tap_rows(taps_ref, 1, cols)
        value_taps = tap_rows(taps_ref, 2, cols)
        keep = [spread(keep_ref, m, cols) for m in range(modes)]
        total = None
        for part in range(2):
            base = part * half
            states = None
            load = lambda s, at: wide[s, pl.ds(SUB + base + at, SUB, stride=run), :]
            lines = [[load(s, at) for at in range(-rim, 0)] for s in range(2)]
            for j in range(run):
                lines = [line[-rim:] + [load(s, j)] for s, line in enumerate(lines)]
                gate = short_conv(lines[0], key_taps) * short_conv(lines[1], value_taps)
                if part == 0 and j < rim:
                    gate = jnp.where(index == 0, 0.0, gate)
                gate_ref[pl.ds(t * toks + base + j, SUB, stride=run), :] = gate
                if states is None:
                    states = [gate] * modes
                else:
                    states = [k * state + gate for k, state in zip(keep, states)]
            for m, end in enumerate(states):
                ends_ref[t, part, m * SUB : (m + 1) * SUB, :] = end
            run_keep = run_ref[:, cols]
            for i in range(SUB):
                end = modes_at(ends_ref.at[t, part], i, modes)
                total = end if total is None else run_keep * total + end
        state_ref[:, cols] = total
        sum_ref[:modes, cols] = total.astype(BF16)
        query = raw_query[step_id, :, :, cols].astype(F32)
        sum_ref[modes:, cols] = jnp.concatenate(
            [
                wide[0, SUB : SUB + rim, :],
                wide[1, SUB : SUB + rim, :],
                query[1, PAIR - rim :],
                wide[0, SUB + toks - rim : SUB + toks, :],
                wide[1, SUB + toks - rim : SUB + toks, :],
                query[0, :rim],
                jnp.zeros((PAIR - 6 * rim, LANES), F32),
            ],
            axis=0,
        ).astype(BF16)


def first_gates(past, first, taps):
    rows = []
    for s in range(2):
        before, here = past[s], first[s]
        line = [before[0:1], before[1:2], here[0:1], here[1:2]]
        rows.append(
            [
                taps[s][0] * line[at] + taps[s][1] * line[at - 1] + taps[s][2] * line[at - 2]
                for at in (2, 3)
            ]
        )
    return [key * value for key, value in zip(*rows)]


def join_kernel(ids, stride, count, toks, last, *refs):
    taps_ref, rate_ref, state_ref, prefix_ref, past_ref, own_ref = refs[:6]
    near = (own_ref,) + refs[6 : 5 + count]
    shared = count == 4 and stride % 2 == 0
    outs = refs[5 + count :]
    prefix_out, past_out = outs[:2]
    modes, width = rate_ref.shape
    index = ids[0]
    place = lax.rem(lax.div(index, stride), count)
    behind = lax.rem(index, stride)
    origins = [lax.rem(place - k + count, count) for k in range(count)]
    as_float = lambda n: n.astype(F32)

    def tile(t, _):
        cols = pl.ds(pl.multiple_of(t * LANES, LANES), LANES)
        rates = rate_ref[:, cols]
        span = rates * float(toks)
        taps = [[taps_ref[j, s : s + 1, cols] for j in range(3)] for s in (1, 2)]
        full = [ref[:, cols].astype(F32) for ref in near]
        if shared:
            odd = lax.rem(index, 2) == 1
            full[1], full[3] = jnp.where(odd, full[3], full[1]), jnp.where(odd, full[1], full[3])
        extra = [value[modes:] for value in full]
        firsts = [(e[0:2], e[2:4]) for e in extra]
        states = [state_ref[:, cols]] + [value[:modes] for value in full[1:]]
        keep = jnp.exp(-rates)
        second_keep = jnp.exp(-rates * float(toks - 2))
        first_keep = second_keep * keep
        block_keep = first_keep * keep
        rest = jnp.exp(-span * float(stride - 1)) if stride > 1 else 1.0
        run_keep = rest * block_keep
        powers = [1.0, run_keep]
        while len(powers) < count:
            powers.append(powers[-1] * run_keep)
        before = jnp.exp(-span * as_float(jnp.maximum(behind - 1, 0)))
        joins = []
        for k in range(count):
            linked = origins[k] >= 1
            past = extra[(k + 1) % count][4:10]
            past = jnp.where(linked, past, 0.0)
            one, two = first_gates((past[2:4], past[4:6]), firsts[k], taps)
            join = first_keep * one + second_keep * two
            if not last:
                join = jnp.where(linked, join, 0.0)
            joins.append(join)
            states[k] = states[k] + rest * join
        passed = jnp.where(behind >= 1, before * block_keep, 1.0)
        prefix = prefix_ref[:, cols] + jnp.where(behind >= 1, before * joins[0], 0.0)
        for k in range(1, count):
            prefix = prefix + jnp.where(place >= k, passed * powers[k - 1] * states[k], 0.0)
        prefix_out[:, cols] = prefix
        past = jnp.where((place >= 1) & (behind == 0), extra[1][4:10], past_ref[0:6, cols])
        past_out[:, cols] = jnp.concatenate([past, jnp.zeros((SUB - 6, LANES), F32)], axis=0)
        if not last:
            state_out, sum_out = outs[2:]
            total = None
            for k in range(count):
                factor = jnp.ones_like(run_keep)
                for gap in range(1, count):
                    factor = jnp.where(origins[k] == count - 1 - gap, powers[gap], factor)
                term = factor * states[k]
                total = term if total is None else total + term
            state_out[:, cols] = total
            first = extra[0]
            end = extra[0]
            for k in range(1, count):
                first = jnp.where(origins[k] == 0, extra[k], first)
                end = jnp.where(origins[k] == count - 1, extra[k], end)
            sum_out[:modes, cols] = total.astype(BF16)
            sum_out[modes:, cols] = jnp.concatenate([first[0:4], end[4:]], axis=0).astype(BF16)
        return 0

    lax.fori_loop(0, width // LANES, tile, 0, unroll=UNROLL)


def local_kernel(
    first, part_id, x_hbm, taps_ref, gate_ref, ends_ref, res_ref, rate_ref, skip_ref, *refs
):
    query_ref, local_ref, raw, wide, begins, sem = refs[-6:]
    part = part_id[0]
    toks, width = raw.shape
    half = toks // 2
    rim = taps_ref.shape[0] - 1
    modes = rate_ref.shape[0]
    run = half // SUB
    start = pl.multiple_of(part * half, half)
    fetch = pltpu.make_async_copy(x_hbm.at[0, :, first : first + width], raw, sem)
    fetch.start()
    for t in range(width // LANES):
        at = first // LANES + t
        cols = slice(at * LANES, (at + 1) * LANES)
        rates = rate_ref[:, cols]
        keep_all = jnp.exp(-rates)
        run_keep = jnp.exp(-rates * run)
        gains = res_ref[:, cols] * jnp.sqrt(2.0 * rates)
        state = jnp.zeros((modes, LANES), F32)
        for i in range(SUB):
            state = run_keep * state + modes_at(ends_ref.at[at, 0], i, modes)
        state = jnp.where(part == 0, 0.0, state)
        for i in range(SUB):
            put_modes_at(begins.at[t], i, state)
            if i + 1 < SUB:
                state = run_keep * state + modes_at(ends_ref.at[at, part], i, modes)
        keep = [jnp.broadcast_to(keep_all[m : m + 1], (SUB, LANES)) for m in range(modes)]
        gain = [jnp.broadcast_to(gains[m : m + 1], (SUB, LANES)) for m in range(modes)]
        skip = spread(skip_ref, 0, cols)
        states = [begins[t, m * SUB : (m + 1) * SUB, :] for m in range(modes)]
        for j in range(run):
            now = gate_ref[pl.ds(at * toks + part * half + j, SUB, stride=run), :]
            states = [k * state + now for k, state in zip(keep, states)]
            local_ref[pl.ds(at * half + j, SUB, stride=run), :] = tree_sum(
                [skip * now] + [g * state for g, state in zip(gain, states)]
            )
    fetch.wait()
    for t in range(width // LANES):
        at = first // LANES + t
        near = slice(t * LANES, (t + 1) * LANES)
        for r in range(0, half, STEP):
            wide[t, SUB + r : SUB + r + STEP, :] = raw[
                pl.ds(pl.multiple_of(start + r, STEP), STEP), near
            ].astype(F32)
        wide[t, SUB - rim : SUB, :] = raw[half - PAIR : half, near].astype(F32)[PAIR - rim :]
        taps = tap_rows(taps_ref, 0, slice(at * LANES, (at + 1) * LANES))
        load = lambda j: wide[t, pl.ds(SUB + j, SUB, stride=run), :]
        line = [load(j) for j in range(-rim, 0)]
        for j in range(run):
            line = line[-rim:] + [load(j)]
            query_ref[pl.ds(at * half + j, SUB, stride=run), :] = short_conv(line, taps)


def finish_kernel(
    ids, query_ref, local_ref, prefix_ref, past_ref, sum_ref, taps_ref, res_ref, rate_ref, skip_ref,
    out_ref, begins, carry,
):
    part = ids[0]
    modes, width = prefix_ref.shape
    half = out_ref.shape[0]
    run = half // SUB
    row = lax.broadcasted_iota(jnp.int32, (STEP, LANES), 0)

    def tile(t, _):
        cols = pl.ds(pl.multiple_of(t * LANES, LANES), LANES)
        rates = rate_ref[:, cols]
        gains = res_ref[:, cols] * jnp.sqrt(2.0 * rates)
        keep_all = jnp.exp(-rates)
        run_keep = jnp.exp(-rates * run)
        past = past_ref[:, cols]
        here = sum_ref[modes:, cols].astype(F32)
        taps = [[taps_ref[j, s : s + 1, cols] for j in range(3)] for s in range(3)]
        one, two = first_gates((past[2:4], past[4:6]), (here[0:2], here[2:4]), taps[1:])
        line = [past[0:1], past[1:2], here[10:11], here[11:12]]
        queries = [
            taps[0][0] * line[at] + taps[0][1] * line[at - 1] + taps[0][2] * line[at - 2]
            for at in (2, 3)
        ]
        grow = jnp.exp(rates)
        state = gains * (prefix_ref[:, cols] + grow * (one + grow * two))
        state = state * jnp.where(part == 0, keep_all, jnp.exp(-rates * (half + 1)))
        for i in range(SUB):
            put_modes_at(begins, i, state)
            state = run_keep * state
        keep = [jnp.broadcast_to(keep_all[m : m + 1], (SUB, LANES)) for m in range(modes)]
        states = [begins[m * SUB : (m + 1) * SUB, :] for m in range(modes)]
        for j in range(run):
            carry[pl.ds(j, SUB, stride=run), :] = tree_sum(states)
            states = [k * state for k, state in zip(keep, states)]
        skip = skip_ref[:, cols]
        over = jnp.sum(gains * grow, axis=0, keepdims=True)
        for r in range(0, half, STEP):
            rows = pl.ds(pl.multiple_of(t * half + r, STEP), STEP)
            value = query_ref[rows, :] * (local_ref[rows, :] + carry[r : r + STEP, :])
            if r == 0:
                begin = carry[0:SUB, :]
                head = queries[0] * (begin[0:1] - over * two + skip * one)
                second = queries[1] * (begin[1:2] + skip * two)
                value = jnp.where((row == 0) & (part == 0), head, value)
                value = jnp.where((row == 1) & (part == 0), second, value)
            out_ref[r : r + STEP, cols] = value.astype(BF16)
        return 0

    lax.fori_loop(0, width // LANES, tile, 0, unroll=UNROLL)


def place_kernel(ids, far_ref, held_ref, out_ref, sem):
    del held_ref
    width = far_ref.shape[1]
    copy = pltpu.make_async_copy(
        far_ref,
        out_ref.at[:, pl.ds(pl.multiple_of(ids[0] * width, LANES), width)],
        sem,
    )
    copy.start()
    copy.wait()


def exchange(summary, blocks, index, stride, count):
    def route(hop):
        pairs = []
        for i in range(blocks):
            j = i // stride % count
            pairs.append((i, i + ((j + hop(i)) % count - j) * stride))
        return pairs

    def send(value, hop):
        return lax.ppermute(value, "ctx", route(hop))

    if count != 4 or stride % 2:
        return [send(summary, lambda i, k=k: k) for k in range(1, count)]
    beside = send(summary, lambda i: 3 if i % 2 else 1)
    across = send(summary, lambda i: 2)
    other = lax.ppermute(beside, "ctx", [(i, i ^ 1) for i in range(blocks)])
    return [beside, across, other]


def scan_counts(blocks):
    counts = [2] if blocks % 2 == 0 else []
    left = blocks // 2 if counts else blocks
    while left % 4 == 0:
        counts.append(4)
        left //= 4
    if left > 1:
        counts.append(left)
    return counts


def shards(streams, short_filter, residue, decay_rate, skip_gain):
    ctx_count = lax.axis_size("ctx")
    index = lax.axis_index("ctx")
    side = lax.axis_index("chan").astype(jnp.int32).reshape(1)
    toks, _, width = streams.shape
    half = toks // 2
    modes = residue.shape[1]
    rim = short_filter.shape[0] - 1
    tile = 256 if width % 256 == 0 else LANES
    steps = width // tile
    tiles = tile // LANES
    all_tiles = width // LANES
    wide_tile = 512 if width % 512 == 0 else tile
    wide_steps = width // wide_tile
    wide_tiles = wide_tile // LANES

    x = jnp.transpose(streams, (1, 0, 2))
    rates = decay_rate.T
    weights = residue.T
    skip = skip_gain[None, :]
    x_kept, taps_kept, rates_kept = (
        pltpu.with_memory_space_constraint(a, pltpu.HBM) for a in (x, short_filter, rates)
    )
    params = pltpu.CompilerParams(vmem_limit_bytes=VMEM_LIMIT)
    in_hbm = pl.BlockSpec(memory_space=pltpu.HBM)
    strip = lambda *lead: pl.BlockSpec(lead + (tile,), lambda i, *_: (0,) * len(lead) + (i,))
    tall = lambda rows: pl.BlockSpec((tiles * rows, LANES), lambda i, *_: (i, 0))
    ends_spec = pl.BlockSpec((tiles, 2, modes * SUB, LANES), lambda i, *_: (i, 0, 0, 0))
    gate, ends, state, summary = pl.pallas_call(
        state_kernel,
        grid=(wide_steps,),
        in_specs=[in_hbm] * 3,
        out_specs=[
            pl.BlockSpec((wide_tiles * toks, LANES), lambda i: (i, 0)),
            pl.BlockSpec((wide_tiles, 2, modes * SUB, LANES), lambda i: (i, 0, 0, 0)),
            pl.BlockSpec((modes, wide_tile), lambda i: (0, i)),
            pl.BlockSpec((modes + PAIR, wide_tile), lambda i: (0, i)),
        ],
        out_shape=[
            jax.ShapeDtypeStruct((all_tiles * toks, LANES), F32),
            jax.ShapeDtypeStruct((all_tiles, 2, modes * SUB, LANES), F32),
            jax.ShapeDtypeStruct((modes, width), F32),
            jax.ShapeDtypeStruct((modes + PAIR, width), BF16),
        ],
        scratch_shapes=[
            pltpu.VMEM((wide_steps, 2, toks, wide_tile), BF16),
            pltpu.VMEM((wide_steps, 2, PAIR, wide_tile), BF16),
            pltpu.VMEM((2, toks + SUB, LANES), F32),
            pltpu.VMEM((modes, wide_tile), F32),
            pltpu.VMEM((modes, wide_tile), F32),
            pltpu.VMEM((rim + 1, 3, width), F32),
            pltpu.VMEM((modes, width), F32),
            pltpu.SemaphoreType.DMA((3, wide_steps)),
            pltpu.SemaphoreType.DMA((2,)),
        ],
        compiler_params=params,
        name="states",
    )(x_kept, taps_kept, rates_kept)

    def shifted(first, *lead):
        return pl.BlockSpec(lead + (tile,), lambda i, *_: (0,) * len(lead) + (first + i,))

    in_vmem = pl.BlockSpec(memory_space=pltpu.VMEM)

    def local(which, gate, first, count, held, name):
        return pl.pallas_call(
            functools.partial(local_kernel, first * tile),
            in_specs=[pl.BlockSpec(memory_space=pltpu.SMEM), in_hbm]
            + [in_vmem] * (6 + len(held)),
            out_specs=[in_vmem] * 2,
            out_shape=[jax.ShapeDtypeStruct((all_tiles * half, LANES), F32)] * 2,
            scratch_shapes=[
                pltpu.VMEM((toks, count * tile), BF16),
                pltpu.VMEM((count * tiles, half + SUB, LANES), F32),
                pltpu.VMEM((count * tiles, modes * SUB, LANES), F32),
                pltpu.SemaphoreType.DMA(()),
            ],
            input_output_aliases={8: 0, 9: 1} if held else {},
            compiler_params=params,
            name=name,
        )(which, x_kept, short_filter, gate, ends, weights, rates, skip, *held)

    few = steps // 2
    locals_sent = ()
    ids = index.astype(jnp.int32).reshape(1)
    prefix = jnp.zeros((modes, width), F32)
    past = jnp.zeros((SUB, width), F32)
    own = summary
    stride = 1
    counts = scan_counts(ctx_count)
    for level, count in enumerate(counts):
        last = level == len(counts) - 1
        arrived = exchange(summary, ctx_count, index, stride, count)
        if 1 <= level <= 2:
            gate, arrived[0] = lax.optimization_barrier((gate, arrived[0]))
            first = 0 if level == 1 else few
            locals_sent = local(1 - side, gate, first, few, locals_sent, f"local_sent_{level}")
            locals_sent, arrived = lax.optimization_barrier((locals_sent, arrived))
        shapes = [
            jax.ShapeDtypeStruct((modes, width), F32),
            jax.ShapeDtypeStruct((SUB, width), F32),
        ]
        if not last:
            shapes += [
                jax.ShapeDtypeStruct((modes, width), F32),
                jax.ShapeDtypeStruct((modes + PAIR, width), BF16),
            ]

        def body(ids, *refs, stride=stride, count=count, last=last):
            join_kernel(ids, stride, count, toks, last, *refs)

        results = pl.pallas_call(
            body,
            in_specs=[pl.BlockSpec(memory_space=pltpu.SMEM)] + [in_vmem] * (5 + count),
            out_specs=[in_vmem] * len(shapes),
            out_shape=shapes,
            compiler_params=params,
            name=f"join_{level}",
        )(ids, short_filter, rates, state, prefix, past, summary, *arrived)
        prefix, past = results[:2]
        if not last:
            state, summary = results[2:]
        stride *= count

    def finish(which, column, columns, locals_, prefix, name):
        return pl.pallas_call(
            finish_kernel,
            grid_spec=pltpu.PrefetchScalarGridSpec(
                num_scalar_prefetch=1,
                grid=(steps,),
                in_specs=[
                    tall(half),
                    tall(half),
                    strip(modes),
                    strip(SUB),
                    strip(modes + PAIR),
                    strip(rim + 1, 3),
                    strip(modes),
                    strip(modes),
                    strip(1),
                ],
                out_specs=pl.BlockSpec((half, tile), lambda i, ids: (0, ids[1] * steps + i)),
                scratch_shapes=[
                    pltpu.VMEM((modes * SUB, LANES), F32),
                    pltpu.VMEM((half, LANES), F32),
                ],
            ),
            out_shape=jax.ShapeDtypeStruct((half, columns), BF16),
            compiler_params=params,
            name=name,
        )(
            jnp.concatenate([which, column]),
            *locals_,
            prefix,
            past,
            own,
            short_filter,
            weights,
            rates,
            skip,
        )

    sent = pl.pallas_call(
        finish_kernel,
        in_specs=[pl.BlockSpec(memory_space=pltpu.SMEM)] + [in_vmem] * 9,
        out_specs=in_vmem,
        out_shape=jax.ShapeDtypeStruct((half, width), BF16),
        scratch_shapes=[pltpu.VMEM((modes * SUB, LANES), F32), pltpu.VMEM((half, LANES), F32)],
        compiler_params=params,
        name="finish_sent",
    )(1 - side, *locals_sent, prefix, past, own, short_filter, weights, rates, skip)
    far = lax.ppermute(sent, "chan", [(0, 1), (1, 0)])
    prefix, gate, sent = lax.optimization_barrier((prefix, gate, sent))
    locals_own = local(side, gate, 0, steps, (), "local_own")
    held = finish(side, side, 2 * width, locals_own, prefix, "finish_own")
    return pl.pallas_call(
        place_kernel,
        grid_spec=pltpu.PrefetchScalarGridSpec(
            num_scalar_prefetch=1,
            grid=(1,),
            in_specs=[pl.BlockSpec(memory_space=pl.ANY)] * 2,
            out_specs=pl.BlockSpec(memory_space=pl.ANY),
            scratch_shapes=[pltpu.SemaphoreType.DMA(())],
        ),
        out_shape=jax.ShapeDtypeStruct((half, 2 * width), BF16),
        input_output_aliases={2: 0},
        compiler_params=params,
        name="place",
    )(1 - side, far, held)


def solution(mesh):
    return jax.shard_map(
        shards,
        mesh=mesh,
        in_specs=(
            P("ctx", None, "chan"),
            P(None, None, "chan"),
            P("chan", None),
            P("chan", None),
            P("chan"),
        ),
        out_specs=P(("ctx", "chan"), None),
        check_vma=False,
    )
```

```python
import functools

import jax
import jax.numpy as jnp
from jax import lax
from jax.experimental import pallas as pl
from jax.experimental.pallas import tpu as pltpu
from jax.sharding import PartitionSpec as P

LANES = 128
SUB = 8
UNROLL = 8
STEP = 32
PAIR = 16
F32 = jnp.float32
BF16 = jnp.bfloat16
VMEM_LIMIT = 16 * 1024 * 1024


def spread(ref, m, cols):
    return jnp.broadcast_to(ref[m : m + 1, cols], (SUB, LANES))


def tree_sum(terms):
    terms = list(terms)
    while len(terms) > 1:
        terms = [
            terms[i] + terms[i + 1] if i + 1 < len(terms) else terms[i]
            for i in range(0, len(terms), 2)
        ]
    return terms[0]


def short_conv(line, taps):
    total = taps[0] * line[-1]
    for k in range(1, len(taps)):
        total = total + taps[k] * line[-1 - k]
    return total


def tap_rows(taps_ref, s, cols):
    return [
        jnp.broadcast_to(taps_ref[j, s : s + 1, cols], (SUB, LANES))
        for j in range(taps_ref.shape[0])
    ]


def modes_at(ref, i, modes):
    return jnp.concatenate(
        [ref[pl.ds(i + SUB * m, SUB, stride=SUB), :] for m in range(0, modes, SUB)], axis=0
    )


def put_modes_at(ref, i, value):
    for m in range(0, value.shape[0], SUB):
        ref[pl.ds(i + SUB * m, SUB, stride=SUB), :] = value[m : m + SUB]


def state_kernel(
    x_hbm, taps_hbm, rate_hbm,
    gate_ref, ends_ref, state_ref, sum_ref,
    raw, raw_query, wide, keep_ref, run_ref, taps_all, rate_all, sems, small_sems,
):
    step_id = pl.program_id(0)
    _, _, toks, width = raw.shape
    half = toks // 2
    rim = taps_all.shape[0] - 1
    modes = rate_all.shape[0]
    run = half // SUB

    def fetches(i):
        cols = pl.ds(pl.multiple_of(i * width, LANES), width)
        return (
            pltpu.make_async_copy(x_hbm.at[pl.ds(1, 2), :, cols], raw.at[i], sems.at[0, i]),
            pltpu.make_async_copy(
                x_hbm.at[0, pl.ds(0, PAIR), cols], raw_query.at[i, 0], sems.at[1, i]
            ),
            pltpu.make_async_copy(
                x_hbm.at[0, pl.ds(toks - PAIR, PAIR), cols], raw_query.at[i, 1], sems.at[2, i]
            ),
        )

    small = (
        pltpu.make_async_copy(taps_hbm, taps_all, small_sems.at[0]),
        pltpu.make_async_copy(rate_hbm, rate_all, small_sems.at[1]),
    )

    @pl.when(step_id == 0)
    def _():
        for copy in small:
            copy.start()
        for i in range(raw.shape[0]):
            for copy in fetches(i):
                copy.start()
        for copy in small:
            copy.wait()

    strip = pl.ds(pl.multiple_of(step_id * width, LANES), width)
    taps_ref = taps_all.at[:, :, strip]
    rates = rate_all[:, strip]
    keep_ref[...] = jnp.exp(-rates)
    run_ref[...] = jnp.exp(-rates * run)
    for copy in fetches(step_id):
        copy.wait()
    index = lax.broadcasted_iota(jnp.int32, (SUB, LANES), 0)
    for t, c in enumerate(range(0, width, LANES)):
        cols = slice(c, c + LANES)
        for s in range(2):
            wide[s, :SUB, :] = jnp.zeros((SUB, LANES), F32)
            for r in range(0, toks, STEP):
                wide[s, SUB + r : SUB + r + STEP, :] = raw[
                    step_id, s, r : r + STEP, cols
                ].astype(F32)
        key_taps = tap_rows(taps_ref, 1, cols)
        value_taps = tap_rows(taps_ref, 2, cols)
        keep = [spread(keep_ref, m, cols) for m in range(modes)]
        total = None
        for part in range(2):
            base = part * half
            states = None
            load = lambda s, at: wide[s, pl.ds(SUB + base + at, SUB, stride=run), :]
            lines = [[load(s, at) for at in range(-rim, 0)] for s in range(2)]
            for j in range(run):
                lines = [line[-rim:] + [load(s, j)] for s, line in enumerate(lines)]
                gate = short_conv(lines[0], key_taps) * short_conv(lines[1], value_taps)
                if part == 0 and j < rim:
                    gate = jnp.where(index == 0, 0.0, gate)
                gate_ref[pl.ds(t * toks + base + j, SUB, stride=run), :] = gate
                if states is None:
                    states = [gate] * modes
                else:
                    states = [k * state + gate for k, state in zip(keep, states)]
            for m, end in enumerate(states):
                ends_ref[t, part, m * SUB : (m + 1) * SUB, :] = end
            run_keep = run_ref[:, cols]
            for i in range(SUB):
                end = modes_at(ends_ref.at[t, part], i, modes)
                total = end if total is None else run_keep * total + end
        state_ref[:, cols] = total
        sum_ref[:modes, cols] = total.astype(BF16)
        query = raw_query[step_id, :, :, cols].astype(F32)
        sum_ref[modes:, cols] = jnp.concatenate(
            [
                wide[0, SUB : SUB + rim, :],
                wide[1, SUB : SUB + rim, :],
                query[1, PAIR - rim :],
                wide[0, SUB + toks - rim : SUB + toks, :],
                wide[1, SUB + toks - rim : SUB + toks, :],
                query[0, :rim],
                jnp.zeros((PAIR - 6 * rim, LANES), F32),
            ],
            axis=0,
        ).astype(BF16)


def first_gates(past, first, taps):
    rows = []
    for s in range(2):
        before, here = past[s], first[s]
        line = [before[0:1], before[1:2], here[0:1], here[1:2]]
        rows.append(
            [
                taps[s][0] * line[at] + taps[s][1] * line[at - 1] + taps[s][2] * line[at - 2]
                for at in (2, 3)
            ]
        )
    return [key * value for key, value in zip(*rows)]


def join_kernel(ids, stride, count, toks, last, *refs):
    taps_ref, rate_ref, state_ref, prefix_ref, past_ref, own_ref = refs[:6]
    near = (own_ref,) + refs[6 : 5 + count]
    shared = count == 4 and stride % 2 == 0
    outs = refs[5 + count :]
    prefix_out, past_out = outs[:2]
    modes, width = rate_ref.shape
    index = ids[0]
    place = lax.rem(lax.div(index, stride), count)
    behind = lax.rem(index, stride)
    origins = [lax.rem(place - k + count, count) for k in range(count)]
    as_float = lambda n: n.astype(F32)

    def tile(t, _):
        cols = pl.ds(pl.multiple_of(t * LANES, LANES), LANES)
        rates = rate_ref[:, cols]
        span = rates * float(toks)
        taps = [[taps_ref[j, s : s + 1, cols] for j in range(3)] for s in (1, 2)]
        full = [ref[:, cols].astype(F32) for ref in near]
        if shared:
            odd = lax.rem(index, 2) == 1
            full[1], full[3] = jnp.where(odd, full[3], full[1]), jnp.where(odd, full[1], full[3])
        extra = [value[modes:] for value in full]
        firsts = [(e[0:2], e[2:4]) for e in extra]
        states = [state_ref[:, cols]] + [value[:modes] for value in full[1:]]
        keep = jnp.exp(-rates)
        second_keep = jnp.exp(-rates * float(toks - 2))
        first_keep = second_keep * keep
        block_keep = first_keep * keep
        rest = jnp.exp(-span * float(stride - 1)) if stride > 1 else 1.0
        run_keep = rest * block_keep
        powers = [1.0, run_keep]
        while len(powers) < count:
            powers.append(powers[-1] * run_keep)
        before = jnp.exp(-span * as_float(jnp.maximum(behind - 1, 0)))
        joins = []
        for k in range(count):
            linked = origins[k] >= 1
            past = extra[(k + 1) % count][4:10]
            past = jnp.where(linked, past, 0.0)
            one, two = first_gates((past[2:4], past[4:6]), firsts[k], taps)
            join = first_keep * one + second_keep * two
            if not last:
                join = jnp.where(linked, join, 0.0)
            joins.append(join)
            states[k] = states[k] + rest * join
        passed = jnp.where(behind >= 1, before * block_keep, 1.0)
        prefix = prefix_ref[:, cols] + jnp.where(behind >= 1, before * joins[0], 0.0)
        for k in range(1, count):
            prefix = prefix + jnp.where(place >= k, passed * powers[k - 1] * states[k], 0.0)
        prefix_out[:, cols] = prefix
        past = jnp.where((place >= 1) & (behind == 0), extra[1][4:10], past_ref[0:6, cols])
        past_out[:, cols] = jnp.concatenate([past, jnp.zeros((SUB - 6, LANES), F32)], axis=0)
        if not last:
            state_out, sum_out = outs[2:]
            total = None
            for k in range(count):
                factor = jnp.ones_like(run_keep)
                for gap in range(1, count):
                    factor = jnp.where(origins[k] == count - 1 - gap, powers[gap], factor)
                term = factor * states[k]
                total = term if total is None else total + term
            state_out[:, cols] = total
            first = extra[0]
            end = extra[0]
            for k in range(1, count):
                first = jnp.where(origins[k] == 0, extra[k], first)
                end = jnp.where(origins[k] == count - 1, extra[k], end)
            sum_out[:modes, cols] = total.astype(BF16)
            sum_out[modes:, cols] = jnp.concatenate([first[0:4], end[4:]], axis=0).astype(BF16)
        return 0

    lax.fori_loop(0, width // LANES, tile, 0, unroll=UNROLL)


def local_kernel(
    first, part_id, x_hbm, taps_ref, gate_ref, ends_ref, res_ref, rate_ref, skip_ref, *refs
):
    query_ref, local_ref, raw, wide, begins, sem = refs[-6:]
    part = part_id[0]
    toks, width = raw.shape
    half = toks // 2
    rim = taps_ref.shape[0] - 1
    modes = rate_ref.shape[0]
    run = half // SUB
    start = pl.multiple_of(part * half, half)
    fetch = pltpu.make_async_copy(x_hbm.at[0, :, first : first + width], raw, sem)
    fetch.start()
    for t in range(width // LANES):
        at = first // LANES + t
        cols = slice(at * LANES, (at + 1) * LANES)
        rates = rate_ref[:, cols]
        keep_all = jnp.exp(-rates)
        run_keep = jnp.exp(-rates * run)
        gains = res_ref[:, cols] * jnp.sqrt(2.0 * rates)
        state = jnp.zeros((modes, LANES), F32)
        for i in range(SUB):
            state = run_keep * state + modes_at(ends_ref.at[at, 0], i, modes)
        state = jnp.where(part == 0, 0.0, state)
        for i in range(SUB):
            put_modes_at(begins.at[t], i, state)
            if i + 1 < SUB:
                state = run_keep * state + modes_at(ends_ref.at[at, part], i, modes)
        keep = [jnp.broadcast_to(keep_all[m : m + 1], (SUB, LANES)) for m in range(modes)]
        gain = [jnp.broadcast_to(gains[m : m + 1], (SUB, LANES)) for m in range(modes)]
        skip = spread(skip_ref, 0, cols)
        states = [begins[t, m * SUB : (m + 1) * SUB, :] for m in range(modes)]
        for j in range(run):
            now = gate_ref[pl.ds(at * toks + part * half + j, SUB, stride=run), :]
            states = [k * state + now for k, state in zip(keep, states)]
            local_ref[pl.ds(at * half + j, SUB, stride=run), :] = tree_sum(
                [skip * now] + [g * state for g, state in zip(gain, states)]
            )
    fetch.wait()
    for t in range(width // LANES):
        at = first // LANES + t
        near = slice(t * LANES, (t + 1) * LANES)
        for r in range(0, half, STEP):
            wide[t, SUB + r : SUB + r + STEP, :] = raw[
                pl.ds(pl.multiple_of(start + r, STEP), STEP), near
            ].astype(F32)
        wide[t, SUB - rim : SUB, :] = raw[half - PAIR : half, near].astype(F32)[PAIR - rim :]
        taps = tap_rows(taps_ref, 0, slice(at * LANES, (at + 1) * LANES))
        load = lambda j: wide[t, pl.ds(SUB + j, SUB, stride=run), :]
        line = [load(j) for j in range(-rim, 0)]
        for j in range(run):
            line = line[-rim:] + [load(j)]
            query_ref[pl.ds(at * half + j, SUB, stride=run), :] = short_conv(line, taps)


def finish_kernel(
    ids, query_ref, local_ref, prefix_ref, past_ref, sum_ref, taps_ref, res_ref, rate_ref, skip_ref,
    out_ref, all_begins, all_carry,
):
    part = ids[0]
    modes, width = prefix_ref.shape
    half = out_ref.shape[0]
    run = half // SUB
    row = lax.broadcasted_iota(jnp.int32, (STEP, LANES), 0)

    for t in range(width // LANES):
        begins, carry = all_begins.at[t], all_carry.at[t]
        cols = slice(t * LANES, (t + 1) * LANES)
        rates = rate_ref[:, cols]
        gains = res_ref[:, cols] * jnp.sqrt(2.0 * rates)
        keep_all = jnp.exp(-rates)
        run_keep = jnp.exp(-rates * run)
        past = past_ref[:, cols]
        here = sum_ref[modes:, cols].astype(F32)
        taps = [[taps_ref[j, s : s + 1, cols] for j in range(3)] for s in range(3)]
        one, two = first_gates((past[2:4], past[4:6]), (here[0:2], here[2:4]), taps[1:])
        line = [past[0:1], past[1:2], here[10:11], here[11:12]]
        queries = [
            taps[0][0] * line[at] + taps[0][1] * line[at - 1] + taps[0][2] * line[at - 2]
            for at in (2, 3)
        ]
        grow = jnp.exp(rates)
        state = gains * (prefix_ref[:, cols] + grow * (one + grow * two))
        state = state * jnp.where(part == 0, keep_all, jnp.exp(-rates * (half + 1)))
        for i in range(SUB):
            put_modes_at(begins, i, state)
            state = run_keep * state
        keep = [jnp.broadcast_to(keep_all[m : m + 1], (SUB, LANES)) for m in range(modes)]
        states = [begins[m * SUB : (m + 1) * SUB, :] for m in range(modes)]
        for j in range(run):
            carry[pl.ds(j, SUB, stride=run), :] = tree_sum(states)
            states = [k * state for k, state in zip(keep, states)]
        skip = skip_ref[:, cols]
        over = jnp.sum(gains * grow, axis=0, keepdims=True)
        for r in range(0, half, STEP):
            rows = slice(t * half + r, t * half + r + STEP)
            value = query_ref[rows, :] * (local_ref[rows, :] + carry[r : r + STEP, :])
            if r == 0:
                begin = carry[0:SUB, :]
                head = queries[0] * (begin[0:1] - over * two + skip * one)
                second = queries[1] * (begin[1:2] + skip * two)
                value = jnp.where((row == 0) & (part == 0), head, value)
                value = jnp.where((row == 1) & (part == 0), second, value)
            out_ref[r : r + STEP, cols] = value.astype(BF16)


def place_kernel(ids, far_ref, held_ref, out_ref, sem):
    del held_ref
    width = far_ref.shape[1]
    copy = pltpu.make_async_copy(
        far_ref,
        out_ref.at[:, pl.ds(pl.multiple_of(ids[0] * width, LANES), width)],
        sem,
    )
    copy.start()
    copy.wait()


def exchange(summary, blocks, index, stride, count):
    def route(hop):
        pairs = []
        for i in range(blocks):
            j = i // stride % count
            pairs.append((i, i + ((j + hop(i)) % count - j) * stride))
        return pairs

    def send(value, hop):
        return lax.ppermute(value, "ctx", route(hop))

    if count != 4 or stride % 2:
        return [send(summary, lambda i, k=k: k) for k in range(1, count)]
    beside = send(summary, lambda i: 3 if i % 2 else 1)
    across = send(summary, lambda i: 2)
    other = lax.ppermute(beside, "ctx", [(i, i ^ 1) for i in range(blocks)])
    return [beside, across, other]


def scan_counts(blocks):
    counts = [2] if blocks % 2 == 0 else []
    left = blocks // 2 if counts else blocks
    while left % 4 == 0:
        counts.append(4)
        left //= 4
    if left > 1:
        counts.append(left)
    return counts


def shards(streams, short_filter, residue, decay_rate, skip_gain):
    ctx_count = lax.axis_size("ctx")
    index = lax.axis_index("ctx")
    side = lax.axis_index("chan").astype(jnp.int32).reshape(1)
    toks, _, width = streams.shape
    half = toks // 2
    modes = residue.shape[1]
    rim = short_filter.shape[0] - 1
    tile = 256 if width % 256 == 0 else LANES
    steps = width // tile
    tiles = tile // LANES
    all_tiles = width // LANES
    wide_tile = 512 if width % 512 == 0 else tile
    wide_steps = width // wide_tile
    wide_tiles = wide_tile // LANES

    x = jnp.transpose(streams, (1, 0, 2))
    rates = decay_rate.T
    weights = residue.T
    skip = skip_gain[None, :]
    x_kept, taps_kept, rates_kept = (
        pltpu.with_memory_space_constraint(a, pltpu.HBM) for a in (x, short_filter, rates)
    )
    params = pltpu.CompilerParams(vmem_limit_bytes=VMEM_LIMIT)
    in_hbm = pl.BlockSpec(memory_space=pltpu.HBM)
    strip = lambda *lead: pl.BlockSpec(lead + (tile,), lambda i, *_: (0,) * len(lead) + (i,))
    tall = lambda rows: pl.BlockSpec((tiles * rows, LANES), lambda i, *_: (i, 0))
    ends_spec = pl.BlockSpec((tiles, 2, modes * SUB, LANES), lambda i, *_: (i, 0, 0, 0))
    gate, ends, state, summary = pl.pallas_call(
        state_kernel,
        grid=(wide_steps,),
        in_specs=[in_hbm] * 3,
        out_specs=[
            pl.BlockSpec((wide_tiles * toks, LANES), lambda i: (i, 0)),
            pl.BlockSpec((wide_tiles, 2, modes * SUB, LANES), lambda i: (i, 0, 0, 0)),
            pl.BlockSpec((modes, wide_tile), lambda i: (0, i)),
            pl.BlockSpec((modes + PAIR, wide_tile), lambda i: (0, i)),
        ],
        out_shape=[
            jax.ShapeDtypeStruct((all_tiles * toks, LANES), F32),
            jax.ShapeDtypeStruct((all_tiles, 2, modes * SUB, LANES), F32),
            jax.ShapeDtypeStruct((modes, width), F32),
            jax.ShapeDtypeStruct((modes + PAIR, width), BF16),
        ],
        scratch_shapes=[
            pltpu.VMEM((wide_steps, 2, toks, wide_tile), BF16),
            pltpu.VMEM((wide_steps, 2, PAIR, wide_tile), BF16),
            pltpu.VMEM((2, toks + SUB, LANES), F32),
            pltpu.VMEM((modes, wide_tile), F32),
            pltpu.VMEM((modes, wide_tile), F32),
            pltpu.VMEM((rim + 1, 3, width), F32),
            pltpu.VMEM((modes, width), F32),
            pltpu.SemaphoreType.DMA((3, wide_steps)),
            pltpu.SemaphoreType.DMA((2,)),
        ],
        compiler_params=params,
        name="states",
    )(x_kept, taps_kept, rates_kept)

    def shifted(first, *lead):
        return pl.BlockSpec(lead + (tile,), lambda i, *_: (0,) * len(lead) + (first + i,))

    in_vmem = pl.BlockSpec(memory_space=pltpu.VMEM)

    def local(which, gate, first, count, held, name):
        return pl.pallas_call(
            functools.partial(local_kernel, first * tile),
            in_specs=[pl.BlockSpec(memory_space=pltpu.SMEM), in_hbm]
            + [in_vmem] * (6 + len(held)),
            out_specs=[in_vmem] * 2,
            out_shape=[jax.ShapeDtypeStruct((all_tiles * half, LANES), F32)] * 2,
            scratch_shapes=[
                pltpu.VMEM((toks, count * tile), BF16),
                pltpu.VMEM((count * tiles, half + SUB, LANES), F32),
                pltpu.VMEM((count * tiles, modes * SUB, LANES), F32),
                pltpu.SemaphoreType.DMA(()),
            ],
            input_output_aliases={8: 0, 9: 1} if held else {},
            compiler_params=params,
            name=name,
        )(which, x_kept, short_filter, gate, ends, weights, rates, skip, *held)

    few = steps // 2
    locals_sent = ()
    ids = index.astype(jnp.int32).reshape(1)
    prefix = jnp.zeros((modes, width), F32)
    past = jnp.zeros((SUB, width), F32)
    own = summary
    stride = 1
    counts = scan_counts(ctx_count)
    for level, count in enumerate(counts):
        last = level == len(counts) - 1
        arrived = exchange(summary, ctx_count, index, stride, count)
        if level >= 2:
            gate, arrived[0] = lax.optimization_barrier((gate, arrived[0]))
            first = 0 if level == 2 else few
            locals_sent = local(1 - side, gate, first, few, locals_sent, f"local_sent_{level}")
            locals_sent, arrived = lax.optimization_barrier((locals_sent, arrived))
        shapes = [
            jax.ShapeDtypeStruct((modes, width), F32),
            jax.ShapeDtypeStruct((SUB, width), F32),
        ]
        if not last:
            shapes += [
                jax.ShapeDtypeStruct((modes, width), F32),
                jax.ShapeDtypeStruct((modes + PAIR, width), BF16),
            ]

        def body(ids, *refs, stride=stride, count=count, last=last):
            join_kernel(ids, stride, count, toks, last, *refs)

        results = pl.pallas_call(
            body,
            in_specs=[pl.BlockSpec(memory_space=pltpu.SMEM)] + [in_vmem] * (5 + count),
            out_specs=[in_vmem] * len(shapes),
            out_shape=shapes,
            compiler_params=params,
            name=f"join_{level}",
        )(ids, short_filter, rates, state, prefix, past, summary, *arrived)
        prefix, past = results[:2]
        if not last:
            state, summary = results[2:]
        stride *= count

    def finish(which, column, columns, locals_, prefix, name):
        return pl.pallas_call(
            finish_kernel,
            grid_spec=pltpu.PrefetchScalarGridSpec(
                num_scalar_prefetch=1,
                grid=(steps,),
                in_specs=[
                    tall(half),
                    tall(half),
                    strip(modes),
                    strip(SUB),
                    strip(modes + PAIR),
                    strip(rim + 1, 3),
                    strip(modes),
                    strip(modes),
                    strip(1),
                ],
                out_specs=pl.BlockSpec((half, tile), lambda i, ids: (0, ids[1] * steps + i)),
                scratch_shapes=[
                    pltpu.VMEM((tiles, modes * SUB, LANES), F32),
                    pltpu.VMEM((tiles, half, LANES), F32),
                ],
            ),
            out_shape=jax.ShapeDtypeStruct((half, columns), BF16),
            compiler_params=params,
            name=name,
        )(
            jnp.concatenate([which, column]),
            *locals_,
            prefix,
            past,
            own,
            short_filter,
            weights,
            rates,
            skip,
        )

    sent = pl.pallas_call(
        finish_kernel,
        in_specs=[pl.BlockSpec(memory_space=pltpu.SMEM)] + [in_vmem] * 9,
        out_specs=in_vmem,
        out_shape=jax.ShapeDtypeStruct((half, width), BF16),
        scratch_shapes=[
            pltpu.VMEM((all_tiles, modes * SUB, LANES), F32),
            pltpu.VMEM((all_tiles, half, LANES), F32),
        ],
        compiler_params=params,
        name="finish_sent",
    )(1 - side, *locals_sent, prefix, past, own, short_filter, weights, rates, skip)
    far = lax.ppermute(sent, "chan", [(0, 1), (1, 0)])
    prefix, gate, sent = lax.optimization_barrier((prefix, gate, sent))
    locals_own = local(side, gate, 0, steps, (), "local_own")
    held = finish(side, side, 2 * width, locals_own, prefix, "finish_own")
    return pl.pallas_call(
        place_kernel,
        grid_spec=pltpu.PrefetchScalarGridSpec(
            num_scalar_prefetch=1,
            grid=(1,),
            in_specs=[pl.BlockSpec(memory_space=pl.ANY)] * 2,
            out_specs=pl.BlockSpec(memory_space=pl.ANY),
            scratch_shapes=[pltpu.SemaphoreType.DMA(())],
        ),
        out_shape=jax.ShapeDtypeStruct((half, 2 * width), BF16),
        input_output_aliases={2: 0},
        compiler_params=params,
        name="place",
    )(1 - side, far, held)


def solution(mesh):
    return jax.shard_map(
        shards,
        mesh=mesh,
        in_specs=(
            P("ctx", None, "chan"),
            P(None, None, "chan"),
            P("chan", None),
            P("chan", None),
            P("chan"),
        ),
        out_specs=P(("ctx", "chan"), None),
        check_vma=False,
    )
```
